32 devices in a mesh: gx: 4 (over y, x), gy: 8 (over z, core).
Axes of the slice: x: 2, y: 2, z: 4, core: 2. Of those that a mesh axis runs over, the one named last changes fastest.
Arguments:
- layer_in: bfloat16 [2, 2048, 1024], P(None, ('gx', 'gy')), may hold values from -6 to 6
- first_layer_value: bfloat16 [2, 2048, 1024], P(None, ('gx', 'gy')), may hold values from -6 to 6
- v1_acc: float32 [2, 2048, 1024], P(None, ('gx', 'gy')), may hold values from -6 to 6
- cotangent: bfloat16 [2, 2048, 1024], P(None, ('gx', 'gy')), may hold values from -6 to 6
- seq_starts: int32 [2, 11], replicated, may hold values from 0 to 1920, as said below
- norm1_gain: bfloat16 [1024], P(('gx', 'gy')), may hold values from 0.5 to 1.5
- w_query: bfloat16 [1024, 1024], P(('gx', 'gy')), may hold values from -0.1875 to 0.1875
- w_key: bfloat16 [1024, 1024], P(('gx', 'gy')), may hold values from -0.1875 to 0.1875
- w_value: bfloat16 [1024, 1024], P(('gx', 'gy')), may hold values from -0.1875 to 0.1875
- w_out: bfloat16 [1024, 1024], P(('gx', 'gy')), may hold values from -1.5 to 1.5
- norm2_gain: bfloat16 [1024], P(('gx', 'gy')), may hold values from 0.5 to 1.5
- w_gate: bfloat16 [1024, 2816], P(('gx', 'gy')), may hold values from -0.1875 to 0.1875
- w_up: bfloat16 [1024, 2816], P(('gx', 'gy')), may hold values from -0.1875 to 0.1875
- w_down: bfloat16 [2816, 1024], P(('gx', 'gy')), may hold values from -0.109375 to 0.109375
Outputs:
- layer_out: bfloat16 [2, 2048, 1024], P(None, ('gx', 'gy'))
- input_grad: float32 [2, 2048, 1024], P(None, ('gx', 'gy'))
- v1_acc_out: float32 [2, 2048, 1024], P(None, ('gx', 'gy'))
- norm1_gain_grad: float32 [1024], P(('gx', 'gy'))
- w_query_grad: float32 [1024, 1024], P(('gx', 'gy'))
- w_key_grad: float32 [1024, 1024], P(('gx', 'gy'))
- w_value_grad: float32 [1024, 1024], P(('gx', 'gy'))
- output_weight_gradient: float32 [1024, 1024], P(('gx', 'gy'))
- norm2_gain_grad: float32 [1024], P(('gx', 'gy'))
- w_gate_grad: float32 [1024, 2816], P(('gx', 'gy'))
- w_up_grad: float32 [1024, 2816], P(('gx', 'gy'))
- w_down_grad: float32 [2816, 1024], P(('gx', 'gy'))
The draws below stay inside these ranges and needn't reach their ends.
Inputs may be any that keep to these rules, and one draw needn't show every extreme that they name: `seq_starts`: sorted ascending within each micro-batch; each sequence runs to the next start or to the end of the micro-batch. Every block of 512 rows holds whole sequences: one of 512, two of 256, or four of 128, in 1, 1 and 2 of the blocks of each micro-batch.
All inputs are finite; a program needn't handle non-finite values.
Results may differ from the reference program's by a relative error of at most 0.03.
Values may be sent and summed in bfloat16 or wider, within the bound.
No kernel may reach another device: no remote copies, remote signals or barrier semaphores. Data moves between devices by JAX's collectives and lax.ppermute only.
A program may use at most 320 MiB of HBM per device.

```python
import functools
import math
import jax
import jax.numpy as jnp
from jax import lax

D = 1024
H = 16
HD = 64
FF = 2816
MICRO = 2
TOK_DEV = 64
TOKENS = 2048
SEQS = 11
N_GX = 4
N_GY = 8


def draw_seq_starts(key, part):
    unit_len = N_GY * TOK_DEV // 4
    row_len = N_GY * TOK_DEV
    quarter = N_GX // 4
    kinds = jnp.concatenate([jnp.zeros((quarter,), jnp.int32), jnp.ones((quarter,), jnp.int32), jnp.full((N_GX - 2 * quarter,), 2, jnp.int32)])
    valid_table = jnp.array([[1, 0, 0, 0], [1, 0, 1, 0], [1, 1, 1, 1]], jnp.int32)

    def one_batch(subkey):
        order = jnp.concatenate([jax.random.permutation(subkey, kinds[:-1]), jnp.full((1,), 2, jnp.int32)])
        valid = valid_table[order].reshape(-1)
        offsets = (jnp.arange(N_GX, dtype=jnp.int32)[:, None] * row_len + jnp.arange(4, dtype=jnp.int32)[None, :] * unit_len).reshape(-1)
        ranking = (1 - valid) * (4 * N_GX) + jnp.arange(4 * N_GX, dtype=jnp.int32)
        picked = jnp.argsort(ranking)[:SEQS]
        return offsets[picked]
    subkeys = jax.random.split(jax.random.fold_in(key, 7), MICRO)
    return jax.vmap(one_batch)(subkeys).astype(jnp.int32)


def spiked(values, own_key, source, target, parts, factor):
    def block_of(dim):
        return (jnp.arange(values.shape[dim]) // (values.shape[dim] // parts)).reshape((-1,) + (1,) * (values.ndim - 1 - dim))

    near = jax.random.permutation(own_key, parts)[block_of(target)]
    other_side = (block_of(target) + parts // 2) % parts
    return jnp.where((block_of(source) == near) | (block_of(source) == other_side), factor * values, values)


def block_scale(key, dims, cuts, low, top_value):
    def one(position, shards_of):
        steps = jax.random.uniform(jax.random.fold_in(jax.random.fold_in(key, 6), position), (shards_of,), jnp.float32, low / len(cuts), top_value / len(cuts))
        return jnp.repeat(jnp.exp(steps), dims[position] // shards_of).reshape((-1,) + (1,) * (len(dims) - position - 1))

    level = one(*cuts[0])
    for cut in cuts[1:]:
        level = level * one(*cut)
    return level


def normal_values(rng, dims, scale, reach, cuts=(), kind=jnp.bfloat16):
    entries = scale * jax.random.normal(rng, dims, jnp.float32)
    if cuts:
        entries = entries * block_scale(rng, dims, cuts, -0.22, 0.18)
    return jnp.clip(entries, -reach, reach).astype(kind)


def heavy_noise(stream_key, dims, deviation, bound, shards, heavy, kind=jnp.bfloat16):
    values = deviation * jax.random.normal(stream_key, dims, jnp.float32)
    if shards:
        values = values * block_scale(stream_key, dims, shards, -0.22, 0.18)
    return jnp.clip(spiked(values, jax.random.fold_in(stream_key, 3), *heavy), -bound, bound).astype(kind)


def setup_inputs(seed: int = 0) -> dict:
    key_of = jax.random.split(jax.random.key(seed), 15)
    layer_in = heavy_noise(key_of[0], (MICRO, TOKENS, D), 1.0, 6.0, ((1, 32),), (1, 2, 32, 2.75))
    first_layer_value = normal_values(key_of[1], (MICRO, TOKENS, D), 1.0, 6.0, ((1, 32),))
    v1_acc = normal_values(key_of[2], (MICRO, TOKENS, D), 1.0, 6.0, ((1, 32),), jnp.float32)
    cotangent = normal_values(key_of[3], (MICRO, TOKENS, D), 1.0, 6.0, ((1, 32),))
    seq_starts = draw_seq_starts(jax.random.fold_in(key_of[14], 71), 0)
    norm1_gain = jnp.clip(1.0 + 0.1 * jax.random.normal(key_of[5], (D,), jnp.float32), 0.5, 1.5).astype(jnp.bfloat16)
    w_query = normal_values(key_of[6], (D, D), D ** -0.5, 0.1875, ((0, 32),))
    w_key = normal_values(key_of[7], (D, D), D ** -0.5, 0.1875, ((0, 32),))
    w_value = normal_values(key_of[8], (D, D), D ** -0.5, 0.1875, ((0, 32),))
    w_out = normal_values(key_of[9], (D, D), (D // 64) ** -0.5, 1.5, ((0, 32),))
    norm2_gain = jnp.clip(1.0 + 0.1 * jax.random.normal(key_of[10], (D,), jnp.float32), 0.5, 1.5).astype(jnp.bfloat16)
    w_gate = normal_values(key_of[11], (D, FF), D ** -0.5, 0.1875, ((0, 32),))
    w_up = normal_values(key_of[12], (D, FF), D ** -0.5, 0.1875, ((0, 32),))
    w_down = normal_values(key_of[13], (FF, D), FF ** -0.5, 0.109375, ((0, 32),))
    return {"layer_in": layer_in, "first_layer_value": first_layer_value, "v1_acc": v1_acc, "cotangent": cotangent, "seq_starts": seq_starts, "norm1_gain": norm1_gain, "w_query": w_query, "w_key": w_key, "w_value": w_value, "w_out": w_out, "norm2_gain": norm2_gain, "w_gate": w_gate, "w_up": w_up, "w_down": w_down}


@jax.custom_vjp
def low(v):
    return lax.optimization_barrier(v.astype(jnp.bfloat16)).astype(jnp.float32)

@jax.custom_vjp
def low_back(v):
    return v

def low_keep(v):
    return (low(v), None)

def low_pass(kept, grad):
    return (grad,)

def back_keep(v):
    return (v, None)

def back_low(kept, grad):
    return (low(grad),)
low.defvjp(low_keep, low_pass)
low_back.defvjp(back_keep, back_low)
EPS = 1e-05
NEG = -1e+30
SCORE_SCALE = 0.125
HIGH = lax.Precision.HIGHEST

def matmul_hi(left, right):
    return jnp.dot(left, right, precision=HIGH, preferred_element_type=jnp.float32)

def rms_scale(hidden_in, gain):
    return hidden_in * lax.rsqrt(lax.optimization_barrier(jnp.mean(hidden_in * hidden_in, axis=-1, keepdims=True)) + EPS) * gain

def rotary(values, positions):
    half_dim = values.shape[-1] // 2
    frequency = 10000.0 ** (-(jnp.arange(half_dim, dtype=jnp.float32) * 2.0 / values.shape[-1]))
    angles = positions.astype(jnp.float32)[:, None] * frequency[None, :]
    cosine = jnp.cos(angles)[:, None, :]
    sine_part = jnp.sin(angles)[:, None, :]
    first_half = values[..., :half_dim]
    second_half = values[..., half_dim:]
    return jnp.concatenate([first_half * cosine - second_half * sine_part, second_half * cosine + first_half * sine_part], axis=-1)

def seq_start_of(positions, starts):
    return lax.optimization_barrier(jnp.max(jnp.where(starts[None, :] <= positions[:, None], starts[None, :], 0), axis=1))

def attend_row(row_args):
    queries, keys_row, values_row, positions, seq_begin = row_args
    row_len = queries.shape[0]
    block_rows = math.gcd(row_len, 512)
    num_blocks = row_len // block_rows

    def one_block(block_args):
        query_block, query_pos, query_begin = block_args
        scores = low_back(jnp.einsum('thd,nhd->htn', query_block, keys_row, precision=HIGH) * SCORE_SCALE)
        visible = (query_begin[:, None] == seq_begin[None, :]) & (positions[None, :] <= query_pos[:, None])
        scores = jnp.where(visible[None], scores, NEG)
        row_max = lax.optimization_barrier(jnp.max(scores, axis=-1, keepdims=True))
        expo_vals = jnp.where(visible[None], jnp.exp(scores - row_max), 0.0)
        softmax_w = expo_vals / lax.optimization_barrier(jnp.sum(expo_vals, axis=-1, keepdims=True))
        return jnp.einsum('htn,nhd->thd', low(softmax_w), values_row, precision=HIGH)
    blocks_out = lax.map(jax.checkpoint(one_block), (queries.reshape(num_blocks, block_rows, H, HD), positions.reshape(num_blocks, block_rows), seq_begin.reshape(num_blocks, block_rows)))
    return blocks_out.reshape(row_len, H, HD)

def layer(x_in, v_in, gain_one, query_w, key_w, value_w, out_w, gain_two, gate_w, up_w, down_w, starts):
    positions = jnp.arange(TOKENS, dtype=jnp.int32)
    seq_begin = seq_start_of(positions, starts)
    relative = positions - seq_begin
    normed_one = low(rms_scale(x_in, gain_one))
    queries = low(rotary(low_back(matmul_hi(normed_one, query_w)).reshape(TOKENS, H, HD), relative))
    keys_all = low(rotary(low_back(matmul_hi(normed_one, key_w)).reshape(TOKENS, H, HD), relative))
    values_own = low_back(matmul_hi(normed_one, value_w))
    blended = low(0.5 * values_own + 0.5 * v_in).reshape(TOKENS, H, HD)
    row_len = TOKENS // N_GX
    attended = lax.map(attend_row, (queries.reshape(N_GX, row_len, H, HD), keys_all.reshape(N_GX, row_len, H, HD), blended.reshape(N_GX, row_len, H, HD), positions.reshape(N_GX, row_len), seq_begin.reshape(N_GX, row_len)))
    attended = low(low_back(attended.reshape(TOKENS, D)))
    after_attn = x_in + low_back(matmul_hi(attended, out_w))
    normed_two = low(rms_scale(after_attn, gain_two))
    gate_pre = low_back(matmul_hi(normed_two, gate_w))
    up_pre = low_back(matmul_hi(normed_two, up_w))
    hidden = low(jax.nn.silu(gate_pre) * up_pre)
    return after_attn + low_back(matmul_hi(hidden, down_w))

def reference(layer_in, first_layer_value, v1_acc, cotangent, seq_starts, norm1_gain, w_query, w_key, w_value, w_out, norm2_gain, w_gate, w_up, w_down):
    weights = [w.astype(jnp.float32) for w in (norm1_gain, w_query, w_key, w_value, w_out, norm2_gain, w_gate, w_up, w_down)]
    outputs = []
    input_grads = []
    accums = []
    grad_sums = [jnp.zeros_like(w) for w in weights]
    for micro_step in range(MICRO):
        forward = functools.partial(layer, starts=seq_starts[micro_step])
        result, pull = jax.vjp(forward, layer_in[micro_step].astype(jnp.float32), first_layer_value[micro_step].astype(jnp.float32), *weights)
        grads = pull(cotangent[micro_step].astype(jnp.float32))
        outputs.append(result.astype(jnp.bfloat16))
        input_grads.append(grads[0])
        accums.append(v1_acc[micro_step] + grads[1])
        grad_sums = [total_g + grad_g for total_g, grad_g in zip(grad_sums, grads[2:])]
    return (jnp.stack(outputs), jnp.stack(input_grads), jnp.stack(accums), grad_sums[0], grad_sums[1], grad_sums[2], grad_sums[3], grad_sums[4], grad_sums[5], grad_sums[6], grad_sums[7], grad_sums[8])
```

```python
import functools

import jax
import jax.numpy as jnp
from jax import lax
from jax.sharding import PartitionSpec as P

H = 16
EPS = 1e-05
NEG = -1e30
SCALE = 0.125
ALL = ("gx", "gy")
F32 = jnp.float32
BF16 = jnp.bfloat16


class Plan:
    def __init__(self, n_gx, n_gy):
        self.n_gx, self.n_gy = n_gx, n_gy
        self.T, self.R = n_gy // 2, n_gx
        self.square = self.T == self.R
        every = [(t, r, c) for t in range(self.T) for r in range(self.R) for c in range(2)]
        at = self.device
        self.t_swap = {k: [(at(t, r, c), at(t ^ k, r, c)) for t, r, c in every] for k in range(1, self.T)}
        self.r_swap = {k: [(at(t, r, c), at(t, r ^ k, c)) for t, r, c in every] for k in range(1, self.R)}
        self.c_swap = [(at(t, r, c), at(t, r, 1 - c)) for t, r, c in every]
        self.inward = []
        for flip in range(2):
            self.inward.append([(self.home(self.chunk(t, r), r, c ^ flip), at(t, r, c)) for t, r, c in every])

    def device(self, t, r, c):
        return t * self.n_gy + r * 2 + c if self.square else r * self.n_gy + t * 2 + c

    def home(self, z, g, c):
        return g * self.n_gy + z * 2 + c

    def chunk(self, t, r):
        return t ^ r if self.square else t


def pick(array, index):
    return lax.dynamic_index_in_dim(array, index, 0, keepdims=False)


def send(array, pairs):
    if all(a == b for a, b in pairs):
        return array
    return lax.ppermute(array, ALL, pairs)


def dot(a, b):
    return lax.dot_general(a, b, (((1,), (0,)), ((), ())), preferred_element_type=F32)


def dot_rows(a, b):
    return lax.dot_general(a, b, (((0,), (0,)), ((), ())), preferred_element_type=F32)


def dot_cols(a, b):
    return lax.dot_general(a, b, (((1,), (1,)), ((), ())), preferred_element_type=F32)


def rotate(values, cosine, sine):
    half = values.shape[-1] // 2
    a, b = values[..., :half], values[..., half:]
    return jnp.concatenate([a * cosine - b * sine, b * cosine + a * sine], axis=-1)


def local(plan, layer_in, first_layer_value, v1_acc, cotangent, seq_starts, norm1_gain, w_query, w_key, w_value,
          w_out, norm2_gain, w_gate, w_up, w_down):
    T, R = plan.T, plan.R
    micro, L, D = layer_in.shape
    FF = w_gate.shape[1]
    HT, FT, heads = D // T, FF // T, H // T
    HD = D // H
    N = T * 2 * L
    gx, gy = lax.axis_index("gx"), lax.axis_index("gy")
    c = gy % 2
    t, r = (gx, gy // 2) if plan.square else (gy // 2, gx)
    swap_t = lambda array, k: send(array, plan.t_swap[k]) if k else array
    swap_r = lambda array, k: send(array, plan.r_swap[k]) if k else array

    def inward(array):
        parts = [send(pick(array, c ^ flip), plan.inward[flip]) for flip in range(2)]
        return jnp.concatenate(parts, axis=0)

    def outward(array):
        parts = [send(array[flip * L:(flip + 1) * L], [(b, a) for a, b in plan.inward[flip]]) for flip in range(2)]
        swapped = jnp.where(c == 0, parts[0], parts[1]), jnp.where(c == 0, parts[1], parts[0])
        return jnp.stack(swapped)

    def gather_t(array):
        return [swap_t(array, k) for k in range(T)]

    def reduce_t(partial):
        own = partial[:2 * L]
        for k in range(1, T):
            own = own + swap_t(partial[k * 2 * L:(k + 1) * 2 * L].astype(BF16), k).astype(F32)
        return own

    def gather_cols(shards):
        rows = shards[0].shape[0]
        if not plan.square:
            return [lax.dynamic_slice_in_dim(lax.all_gather(s, ALL, axis=0, tiled=True), t * (s.shape[1] // T), s.shape[1] // T, 1)
                    for s in shards]
        pieces = jnp.concatenate([s.reshape(rows, T, -1) for s in shards], axis=2).transpose(1, 0, 2)
        width = pieces.shape[2]
        block = jnp.stack([swap_t(pick(pieces, t ^ k), k) for k in range(T)])
        blocks = jnp.stack([swap_r(block, j) for j in range(R)])
        both = (blocks, send(blocks, plan.c_swap))
        full = jnp.zeros((T, R, 2, rows, width), BF16)
        for i in range(2):
            for j in range(R):
                for k in range(T):
                    full = lax.dynamic_update_slice(full, both[i][j, k][None, None, None], (t ^ k, r ^ j, c ^ i, 0, 0))
        full = full.reshape(T * R * 2 * rows, width)
        out, at = [], 0
        for s in shards:
            w = s.shape[1] // T
            out.append(full[:, at:at + w])
            at += w
        return out

    def gather_rows(shard):
        rows = shard.shape[0]
        if not plan.square:
            full = lax.all_gather(shard, ALL, axis=0, tiled=True)
            return lax.dynamic_slice_in_dim(full, t * (full.shape[0] // T), full.shape[0] // T, 0)
        blocks = jnp.stack([swap_r(shard, j) for j in range(R)])
        both = (blocks, send(blocks, plan.c_swap))
        full = jnp.zeros((R, 2) + shard.shape, shard.dtype)
        for i in range(2):
            for j in range(R):
                full = lax.dynamic_update_slice(full, both[i][j][None, None], (r ^ j, c ^ i) + (0,) * shard.ndim)
        return full.reshape((R * 2 * rows,) + shard.shape[1:])

    def reduce_r(grad):
        axis = grad.ndim - 4
        take = lambda a, i, ax: lax.dynamic_index_in_dim(a, i, ax, keepdims=False)
        kept = take(grad, c, axis + 1).astype(F32)
        kept = kept + send(take(grad, 1 - c, axis + 1), plan.c_swap).astype(F32)
        low = kept.astype(grad.dtype)
        total = take(kept, r, axis)
        for j in range(1, R):
            total = total + swap_r(take(low, r ^ j, axis), j).astype(F32)
        return total

    def scatter_cols(grad, widths):
        if not plan.square:
            out, at = [], 0
            for w in widths:
                full = lax.dynamic_update_slice(jnp.zeros((D, w * T), F32), grad[:, at:at + w].astype(F32), (0, t * w))
                out.append(lax.psum_scatter(full, ALL, scatter_dimension=0, tiled=True))
                at += w
            return out
        rows = D // (T * R * 2)
        total = reduce_r(grad.astype(BF16).reshape(T, R, 2, rows, -1))
        low = total.astype(BF16)
        parts = [swap_t(pick(low, t ^ k), k).astype(F32) if k else pick(total, t) for k in range(T)]
        parts = jnp.stack(parts)
        order = [pick(parts, s ^ t) for s in range(T)]
        out, at = [], 0
        for w in widths:
            out.append(jnp.concatenate([p[:, at:at + w] for p in order], axis=1))
            at += w
        return out

    def scatter_rows(grad):
        if not plan.square:
            full = lax.dynamic_update_slice(jnp.zeros((grad.shape[0] * T, D), F32), grad, (t * grad.shape[0], 0))
            return lax.psum_scatter(full, ALL, scatter_dimension=0, tiled=True)
        return reduce_r(grad.astype(BF16).reshape(R, 2, -1, D))

    def scatter_gains(grads):
        if not plan.square:
            return lax.psum_scatter(grads, ALL, scatter_dimension=1, tiled=True)
        rows = D // (T * R * 2)
        total = reduce_r(grads.reshape(2, T, R, 2, rows, 1).transpose(1, 2, 3, 0, 4, 5).reshape(T, R, 2, 2 * rows, 1))
        own = pick(total, t)
        for k in range(1, T):
            own = own + swap_t(pick(total, t ^ k), k)
        return own.reshape(2, rows)

    def gather_gains(gains):
        if not plan.square:
            return lax.all_gather(gains, ALL, axis=0, tiled=True).T
        rows = gains.shape[0]
        part = gather_rows(gains)
        full = jnp.zeros((T,) + part.shape, part.dtype)
        for k in range(T):
            full = lax.dynamic_update_slice(full, swap_t(part, k)[None], (t ^ k, 0, 0))
        return full.reshape(D, 2).T

    x_own = inward(layer_in)
    query_w, key_w, value_w = gather_cols([w_query, w_key, w_value])
    gains = gather_gains(jnp.stack([norm1_gain, norm2_gain], axis=1)).astype(F32)
    gain_one, gain_two = gains[0], gains[1]
    x_all = jnp.concatenate(gather_t(x_own), axis=0)
    v_own = inward(first_layer_value)
    v_cols = v_own.reshape(2 * L, T, HT).transpose(1, 0, 2)
    v_all = jnp.concatenate([swap_t(pick(v_cols, t ^ k), k) for k in range(T)], axis=0)
    out_rows = gather_rows(w_out)
    gate_w, up_w = gather_cols([w_gate, w_up])
    down_w = gather_rows(w_down)
    out_parts = gather_t(out_rows)
    c_own = inward(cotangent)
    c_all = jnp.concatenate(gather_t(c_own), axis=0)

    starts = pick(seq_starts, c)
    blocks = plan.chunk(t ^ jnp.arange(T, dtype=jnp.int32), r) if plan.square else (t ^ jnp.arange(T, dtype=jnp.int32))
    position = (blocks[:, None] * 2 + (c ^ jnp.arange(2, dtype=jnp.int32))[None, :])[:, :, None] * L
    position = (position + jnp.arange(L, dtype=jnp.int32)).reshape(N) + r * N
    begin = jnp.max(jnp.where(starts[None, :] <= position[:, None], starts[None, :], 0), axis=1)
    rel = (position - begin).astype(F32)
    visible = (begin[:, None] == begin[None, :]) & (position[None, :] <= position[:, None])
    frequency = 10000.0 ** (-(jnp.arange(HD // 2, dtype=F32) * 2.0 / HD))
    angles = rel[:, None] * frequency[None, :]
    cosine, sine = jnp.cos(angles)[:, None, :], jnp.sin(angles)[:, None, :]

    x = x_all.astype(F32)
    rstd_one = lax.rsqrt(jnp.mean(x * x, axis=-1, keepdims=True) + EPS)
    normed_one = (x * rstd_one * gain_one).astype(BF16)
    query = rotate(dot(normed_one, query_w).reshape(N, heads, HD), cosine, sine).astype(BF16)
    key = rotate(dot(normed_one, key_w).reshape(N, heads, HD), cosine, sine).astype(BF16)
    value = (0.5 * dot(normed_one, value_w) + 0.5 * v_all.astype(F32)).astype(BF16).reshape(N, heads, HD)
    scores = jnp.einsum("ihd,jhd->hij", query, key, preferred_element_type=F32) * SCALE
    scores = jnp.where(visible[None], scores, NEG)
    top = jnp.max(scores, axis=-1, keepdims=True)
    probs = jnp.exp(scores - top)
    denom = jnp.sum(probs, axis=-1, keepdims=True)
    probs = probs / denom
    probs_low = probs.astype(BF16)
    attn = jnp.einsum("hij,jhd->ihd", probs_low, value, preferred_element_type=F32)
    attn_low = attn.reshape(N, HT).astype(BF16)
    after = x
    for k in range(T):
        part = swap_t(attn_low, k).reshape(T, 2 * L, HT)
        part = jnp.concatenate([part[b ^ k] for b in range(T)], axis=0)
        after = after + dot(part, out_parts[k])
    rstd_two = lax.rsqrt(jnp.mean(after * after, axis=-1, keepdims=True) + EPS)
    hat_two = after * rstd_two
    normed_two = (hat_two * gain_two).astype(BF16)
    gate = dot(normed_two, gate_w)
    up = dot(normed_two, up_w)
    sig = jax.nn.sigmoid(gate)
    act = gate * sig
    hidden = (act * up).astype(BF16)
    result = reduce_t(dot(hidden, down_w)) + after[:2 * L]
    layer_out = outward(result.astype(BF16))

    grad_down = dot_rows(hidden, c_all)
    grad_hidden = dot_cols(c_all, down_w)
    grad_gate = (grad_hidden * up * (sig * (1.0 + gate * (1.0 - sig)))).astype(BF16)
    grad_up = (grad_hidden * act).astype(BF16)
    grad_gu = dot_rows(normed_two, jnp.concatenate([grad_gate, grad_up], axis=1))
    grad_two_part = dot_cols(grad_gate, gate_w) + dot_cols(grad_up, up_w)
    gain_two_grad = jnp.sum(grad_two_part * hat_two, axis=0)
    grad_two = reduce_t(grad_two_part) * gain_two
    hat_own = hat_two[:2 * L]
    grad_after = c_own.astype(F32) + rstd_two[:2 * L] * (
        grad_two - hat_own * jnp.mean(grad_two * hat_own, axis=-1, keepdims=True))
    grad_branch = jnp.concatenate(gather_t(grad_after.astype(BF16)), axis=0)
    grad_out = dot_rows(attn_low, grad_branch)
    grad_attn = dot_cols(grad_branch, out_rows).astype(BF16).reshape(N, heads, HD)
    delta = jnp.sum(grad_attn.astype(F32) * attn, axis=-1).T
    grad_probs = jnp.einsum("ihd,jhd->hij", grad_attn, value, preferred_element_type=F32)
    grad_scores = (probs * (grad_probs - delta[..., None])).astype(BF16)
    grad_query = jnp.einsum("hij,jhd->ihd", grad_scores, key, preferred_element_type=F32) * SCALE
    grad_key = jnp.einsum("hij,ihd->jhd", grad_scores, query, preferred_element_type=F32) * SCALE
    grad_blend = jnp.einsum("hij,ihd->jhd", probs_low, grad_attn, preferred_element_type=F32).reshape(N, HT)
    grad_query = rotate(grad_query, cosine, -sine).reshape(N, HT).astype(BF16)
    grad_key = rotate(grad_key, cosine, -sine).reshape(N, HT).astype(BF16)
    grad_value = (0.5 * grad_blend).astype(BF16)
    grad_qkv = dot_rows(normed_one, jnp.concatenate([grad_query, grad_key, grad_value], axis=1))
    grad_one_part = dot_cols(grad_query, query_w) + dot_cols(grad_key, key_w) + dot_cols(grad_value, value_w)
    hat_one = x * rstd_one
    gain_one_grad = jnp.sum(grad_one_part * hat_one, axis=0)
    grad_one = reduce_t(grad_one_part) * gain_one
    hat_own = hat_one[:2 * L]
    input_grad = grad_after + rstd_one[:2 * L] * (
        grad_one - hat_own * jnp.mean(grad_one * hat_own, axis=-1, keepdims=True))
    input_grad = outward(input_grad.astype(BF16)).astype(F32)
    v_parts = jnp.stack([swap_t(grad_value[k * 2 * L:(k + 1) * 2 * L], k) for k in range(T)])
    v_rows = jnp.concatenate([pick(v_parts, s ^ t) for s in range(T)], axis=1)
    v1_out = v1_acc + outward(v_rows).astype(F32)

    gate_g, up_g = scatter_cols(grad_gu, [FT, FT])
    down_g = scatter_rows(grad_down)
    out_g = scatter_rows(grad_out)
    query_g, key_g, value_g = scatter_cols(grad_qkv, [HT, HT, HT])
    gain_g = scatter_gains(jnp.stack([gain_one_grad, gain_two_grad]))
    return (layer_out, input_grad, v1_out, gain_g[0], query_g, key_g, value_g, out_g, gain_g[1], gate_g, up_g, down_g)


def solution(mesh):
    plan = Plan(mesh.shape["gx"], mesh.shape["gy"])
    tokens, rows, vector = P(None, ALL, None), P(ALL, None), P(ALL)
    return jax.shard_map(
        functools.partial(local, plan),
        mesh=mesh,
        in_specs=(tokens, tokens, tokens, tokens, P(), vector, rows, rows, rows, rows, vector, rows, rows, rows),
        out_specs=(tokens, tokens, tokens, vector, rows, rows, rows, rows, vector, rows, rows, rows),
        check_vma=False,
    )
```

```python
import functools

import jax
import jax.numpy as jnp
from jax import lax
from jax.sharding import PartitionSpec as P

H = 16
EPS = 1e-05
NEG = -1e30
SCALE = 0.125
ALL = ("gx", "gy")
F32 = jnp.float32
BF16 = jnp.bfloat16


class Plan:
    def __init__(self, n_gx, n_gy):
        self.G, self.T = n_gx, n_gy // 2
        every = [(g, h, t) for g in range(self.G) for h in range(2) for t in range(self.T)]
        at = lambda g, h, t: g * n_gy + h * self.T + t
        self.g_swap = {k: [(at(g, h, t), at(g ^ k, h, t)) for g, h, t in every] for k in range(1, self.G)}
        self.t_swap = {k: [(at(g, h, t), at(g, h, t ^ k)) for g, h, t in every] for k in range(1, self.T)}
        self.h_swap = [(at(g, h, t), at(g, 1 - h, t)) for g, h, t in every]
        self.bits = []
        bit = self.T // 2
        while bit:
            self.bits.append(bit)
            bit //= 2


def pick(array, index, axis=0):
    return lax.dynamic_index_in_dim(array, index, axis, keepdims=False)


def send(array, pairs):
    return lax.ppermute(array, ALL, pairs)


def dot(a, b):
    return lax.dot_general(a, b, (((1,), (0,)), ((), ())), preferred_element_type=F32)


def dot_rows(a, b):
    return lax.dot_general(a, b, (((0,), (0,)), ((), ())), preferred_element_type=F32)


def dot_cols(a, b):
    return lax.dot_general(a, b, (((1,), (1,)), ((), ())), preferred_element_type=F32)


def rotate(values, cosine, sine):
    half = values.shape[-1] // 2
    a, b = values[..., :half], values[..., half:]
    return jnp.concatenate([a * cosine - b * sine, b * cosine + a * sine], axis=-1)


def local(plan, layer_in, first_layer_value, v1_acc, cotangent, seq_starts, norm1_gain, w_query, w_key, w_value,
          w_out, norm2_gain, w_gate, w_up, w_down):
    G, T, bits = plan.G, plan.T, plan.bits
    micro, L, D = layer_in.shape
    FF = w_gate.shape[1]
    HT, FT, heads = D // T, FF // T, H // T
    HD = D // H
    M = 2 * L
    N = T * M
    rows, frows = w_query.shape[0], w_down.shape[0]
    g, gy = lax.axis_index("gx"), lax.axis_index("gy")
    h, t = gy // T, gy % T

    def to_t(array, bit):
        return send(array, plan.t_swap[bit])

    def to_g(array, k):
        return send(array, plan.g_swap[k]) if k else array

    def to_h(array):
        return send(array, plan.h_swap)

    def inward(array):
        return jnp.concatenate([pick(array, h), to_h(pick(array, 1 - h))], axis=0)

    def outward(array):
        own, other = array[:L], to_h(array[L:])
        return jnp.stack([jnp.where(h == 0, own, other), jnp.where(h == 0, other, own)])

    def gather_t(array):
        parts = {0: array}
        for bit in bits:
            order = sorted(parts)
            moved = to_t(jnp.concatenate([parts[j] for j in order], axis=0), bit)
            size = array.shape[0]
            for i, j in enumerate(order):
                parts[j ^ bit] = moved[i * size:(i + 1) * size]
        return [parts[j] for j in range(T)]

    def reduce_t(partial):
        blocks = partial.reshape((T, -1) + partial.shape[1:])
        for bit in reversed(bits):
            order = [j for j in range(blocks.shape[0])]
            shape = blocks.shape
            split = blocks.reshape((-1, 2, 1) + shape[1:]) if False else blocks
            split = blocks.reshape((shape[0] // 2, 2) + shape[1:])
            blocks = split[:, 0] + to_t(split[:, 1].astype(BF16), bit).astype(F32)
        return blocks[0]

    def exchange_t(parts):
        held = {j: [parts[j]] for j in range(T)}
        sources = [0]
        for bit in bits:
            out = [j for j in sorted(held) if j & bit]
            flat = [p for j in out for p in held[j]]
            moved = to_t(jnp.stack(flat), bit)
            n = len(sources)
            new = {}
            for i, j in enumerate(out):
                new[j ^ bit] = held[j ^ bit] + [moved[i * n + s] for s in range(n)]
            sources = sources + [s ^ bit for s in sources]
            held = new
        result = [None] * T
        for s, p in zip(sources, held[0]):
            result[s] = p
        return result

    def natural(parts):
        array = jnp.stack(parts)
        for bit in bits:
            split = array.reshape((-1, 2, bit) + array.shape[1:])
            array = jnp.where((t & bit) != 0, split[:, ::-1], split).reshape(array.shape)
        return array

    def gather_r(block):
        other = to_h(block)
        pair = jnp.where(h == 0, jnp.stack([block, other]), jnp.stack([other, block]))
        full = jnp.zeros((G,) + pair.shape, pair.dtype)
        for k in range(G):
            full = lax.dynamic_update_slice(full, to_g(pair, k)[None], (g ^ k,) + (0,) * pair.ndim)
        return full.reshape((G * 2 * block.shape[0],) + block.shape[1:])

    def gather_cols(slices):
        block = natural(exchange_t([pick(slices, t ^ j) for j in range(T)]))
        return gather_r(block.reshape(T * block.shape[1], -1))

    def reduce_r(grad):
        n, w = grad.shape[0] // (2 * G), grad.shape[1]
        grad = grad.astype(BF16).reshape(G, 2 * n, w)
        total = pick(grad, g).astype(F32)
        for k in range(1, G):
            total = total + to_g(pick(grad, g ^ k), k).astype(F32)
        total = total.reshape(2, n, w)
        return pick(total, h) + to_h(pick(total, 1 - h).astype(BF16)).astype(F32)

    def scatter_cols(grad):
        total = reduce_r(grad).reshape(T, rows, -1)
        low = total.astype(BF16)
        return natural(exchange_t([pick(low, t ^ j) for j in range(T)])).astype(F32)

    pad = jnp.zeros((rows, 126), BF16)
    gains_in = jnp.concatenate([norm1_gain[:, None], norm2_gain[:, None], pad], axis=1)

    def col_slices(w):
        return w.reshape(rows, T, HT).transpose(1, 0, 2)

    def hidden_slices(w):
        return w.reshape(rows, 2 * G, T, frows).transpose(2, 0, 1, 3).reshape(T, rows, FT)

    qkv_slices = jnp.concatenate([col_slices(w_query), col_slices(w_key), col_slices(w_value),
                                  jnp.broadcast_to(gains_in[None], (T, rows, 128))], axis=2)
    x_own = inward(layer_in)
    qkv_w = gather_cols(qkv_slices)
    x_all = jnp.concatenate(gather_t(x_own), axis=0)
    v_own = inward(first_layer_value).reshape(M, T, HT).transpose(1, 0, 2)
    v_all = jnp.concatenate(exchange_t([pick(v_own, t ^ j) for j in range(T)]), axis=0)
    gu_w = gather_cols(jnp.concatenate([hidden_slices(w_gate), hidden_slices(w_up)], axis=2))
    down_w = gather_r(w_down)
    c_own = inward(cotangent)
    c_all = jnp.concatenate(gather_t(c_own), axis=0)
    out_w = natural(gather_t(gather_r(w_out))).reshape(T, 2 * G, rows, D).transpose(1, 0, 2, 3).reshape(D, D)
    out_w = out_w.reshape(T, HT, D)

    gains = qkv_w[:, 3 * HT:3 * HT + 2].astype(F32).T
    gain_one, gain_two = gains[0], gains[1]
    query_w, key_w, value_w = qkv_w[:, :HT], qkv_w[:, HT:2 * HT], qkv_w[:, 2 * HT:3 * HT]
    gate_w, up_w = gu_w[:, :FT], gu_w[:, FT:]

    starts = pick(seq_starts, h)
    member = t ^ jnp.arange(T, dtype=jnp.int32)
    half = h ^ jnp.arange(2, dtype=jnp.int32)
    position = ((half[None, :] * T + member[:, None]) * L)[:, :, None] + jnp.arange(L, dtype=jnp.int32)
    position = position.reshape(N) + g * N
    begin = jnp.max(jnp.where(starts[None, :] <= position[:, None], starts[None, :], 0), axis=1)
    rel = (position - begin).astype(F32)
    visible = (begin[:, None] == begin[None, :]) & (position[None, :] <= position[:, None])
    frequency = 10000.0 ** (-(jnp.arange(HD // 2, dtype=F32) * 2.0 / HD))
    angles = rel[:, None] * frequency[None, :]
    cosine, sine = jnp.cos(angles)[:, None, :], jnp.sin(angles)[:, None, :]

    x = x_all.astype(F32)
    rstd_one = lax.rsqrt(jnp.mean(x * x, axis=-1, keepdims=True) + EPS)
    normed_one = (x * rstd_one * gain_one).astype(BF16)
    query = rotate(dot(normed_one, query_w).reshape(N, heads, HD), cosine, sine).astype(BF16)
    key = rotate(dot(normed_one, key_w).reshape(N, heads, HD), cosine, sine).astype(BF16)
    value = (0.5 * dot(normed_one, value_w) + 0.5 * v_all.astype(F32)).astype(BF16).reshape(N, heads, HD)
    scores = jnp.einsum("ihd,jhd->hij", query, key, preferred_element_type=F32) * SCALE
    scores = jnp.where(visible[None], scores, NEG)
    top = jnp.max(scores, axis=-1, keepdims=True)
    probs = jnp.exp(scores - top)
    denom = jnp.sum(probs, axis=-1, keepdims=True)
    probs = probs / denom
    probs_low = probs.astype(BF16)
    attn = jnp.einsum("hij,jhd->ihd", probs_low, value, preferred_element_type=F32)
    attn_low = attn.reshape(N, HT).astype(BF16)
    attn_parts = []
    for j, part in enumerate(gather_t(attn_low)):
        part = part.reshape(T, M, HT)
        attn_parts.append(jnp.concatenate([part[b ^ j] for b in range(T)], axis=0))
    after = x
    for j in range(T):
        after = after + dot(attn_parts[j], pick(out_w, t ^ j))
    rstd_two = lax.rsqrt(jnp.mean(after * after, axis=-1, keepdims=True) + EPS)
    hat_two = after * rstd_two
    normed_two = (hat_two * gain_two).astype(BF16)
    gate = dot(normed_two, gate_w)
    up = dot(normed_two, up_w)
    sig = jax.nn.sigmoid(gate)
    act = gate * sig
    hidden = (act * up).astype(BF16)

    grad_hidden = dot_cols(c_all, down_w)
    grad_gate = (grad_hidden * up * (sig * (1.0 + gate * (1.0 - sig)))).astype(BF16)
    grad_up = (grad_hidden * act).astype(BF16)
    grad_two_part = dot_cols(grad_gate, gate_w) + dot_cols(grad_up, up_w)
    gain_two_grad = jnp.sum(grad_two_part * hat_two, axis=0)
    grad_two = reduce_t(grad_two_part) * gain_two
    hat_own = hat_two[:M]
    grad_after = c_own.astype(F32) + rstd_two[:M] * (
        grad_two - hat_own * jnp.mean(grad_two * hat_own, axis=-1, keepdims=True))
    grad_branch = jnp.concatenate(gather_t(grad_after.astype(BF16)), axis=0)
    result = reduce_t(dot(hidden, down_w)) + after[:M]
    layer_out = outward(result.astype(BF16))
    grad_down = dot_rows(hidden, c_all)
    grad_gu = dot_rows(normed_two, jnp.concatenate([grad_gate, grad_up], axis=1))

    grad_attn = dot_cols(grad_branch, pick(out_w, t)).astype(BF16).reshape(N, heads, HD)
    delta = jnp.sum(grad_attn.astype(F32) * attn, axis=-1).T
    grad_probs = jnp.einsum("ihd,jhd->hij", grad_attn, value, preferred_element_type=F32)
    grad_scores = (probs * (grad_probs - delta[..., None])).astype(BF16)
    grad_query = jnp.einsum("hij,jhd->ihd", grad_scores, key, preferred_element_type=F32) * SCALE
    grad_key = jnp.einsum("hij,ihd->jhd", grad_scores, query, preferred_element_type=F32) * SCALE
    grad_blend = jnp.einsum("hij,ihd->jhd", probs_low, grad_attn, preferred_element_type=F32).reshape(N, HT)
    grad_query = rotate(grad_query, cosine, -sine).reshape(N, HT).astype(BF16)
    grad_key = rotate(grad_key, cosine, -sine).reshape(N, HT).astype(BF16)
    grad_value = (0.5 * grad_blend).astype(BF16)
    grad_one_part = dot_cols(grad_query, query_w) + dot_cols(grad_key, key_w) + dot_cols(grad_value, value_w)
    hat_one = x * rstd_one
    gain_one_grad = jnp.sum(grad_one_part * hat_one, axis=0)
    grad_one = reduce_t(grad_one_part) * gain_one
    hat_own = hat_one[:M]
    input_grad = grad_after + rstd_one[:M] * (
        grad_one - hat_own * jnp.mean(grad_one * hat_own, axis=-1, keepdims=True))
    input_grad = outward(input_grad.astype(BF16)).astype(F32)
    v_parts = natural(exchange_t([grad_value[j * M:(j + 1) * M] for j in range(T)]))
    v1_out = v1_acc + outward(v_parts.transpose(1, 0, 2).reshape(M, D)).astype(F32)

    attn_full = natural([p.T for p in attn_parts]).reshape(2 * G, T, rows, N)
    grad_out = dot(pick(attn_full, t, 1).reshape(2 * G * rows, N), grad_branch)
    grad_gains = jnp.stack([gain_one_grad, gain_two_grad], axis=1)
    grad_gains = jnp.concatenate([grad_gains, jnp.zeros((D, 126), F32)], axis=1)
    grad_qkv = dot_rows(normed_one, jnp.concatenate([grad_query, grad_key, grad_value], axis=1))
    down_g = reduce_r(grad_down)
    gu_g = scatter_cols(grad_gu)
    out_g = reduce_r(grad_out)
    qkv_g = scatter_cols(jnp.concatenate([grad_qkv, grad_gains], axis=1))

    def col_join(parts):
        return parts.transpose(1, 0, 2).reshape(rows, D)

    def hidden_join(parts):
        return parts.reshape(T, rows, 2 * G, frows).transpose(1, 2, 0, 3).reshape(rows, FF)

    gain_g = jnp.sum(qkv_g[:, :, 3 * HT:3 * HT + 2], axis=0)
    return (layer_out, input_grad, v1_out, gain_g[:, 0], col_join(qkv_g[:, :, :HT]), col_join(qkv_g[:, :, HT:2 * HT]),
            col_join(qkv_g[:, :, 2 * HT:3 * HT]), out_g, gain_g[:, 1], hidden_join(gu_g[:, :, :FT]),
            hidden_join(gu_g[:, :, FT:]), down_g)


def solution(mesh):
    plan = Plan(mesh.shape["gx"], mesh.shape["gy"])
    tokens, rows, vector = P(None, ALL, None), P(ALL, None), P(ALL)
    return jax.shard_map(
        functools.partial(local, plan),
        mesh=mesh,
        in_specs=(tokens, tokens, tokens, tokens, P(), vector, rows, rows, rows, rows, vector, rows, rows, rows),
        out_specs=(tokens, tokens, tokens, vector, rows, rows, rows, rows, vector, rows, rows, rows),
        check_vma=False,
    )
```

```python
import functools

import jax
import jax.numpy as jnp
from jax import lax
from jax.experimental import pallas as pl
from jax.experimental.pallas import tpu as pltpu
from jax.sharding import PartitionSpec as P

H = 16
EPS = 1e-05
NEG = -1e30
SCALE = 0.125
ALL = ("gx", "gy")
F32 = jnp.float32
BF16 = jnp.bfloat16


class Plan:
    def __init__(self, n_gx, n_gy):
        self.G, self.T = n_gx, n_gy // 2
        every = [(g, h, t) for g in range(self.G) for h in range(2) for t in range(self.T)]
        at = lambda g, h, t: g * n_gy + h * self.T + t
        self.g_swap = {k: [(at(g, h, t), at(g ^ k, h, t)) for g, h, t in every] for k in range(1, self.G)}
        self.t_swap = {k: [(at(g, h, t), at(g, h, t ^ k)) for g, h, t in every] for k in range(1, self.T)}
        self.h_swap = [(at(g, h, t), at(g, 1 - h, t)) for g, h, t in every]
        self.bits = []
        bit = self.T // 2
        while bit:
            self.bits.append(bit)
            bit //= 2


def pick(array, index, axis=0):
    return lax.dynamic_index_in_dim(array, index, axis, keepdims=False)


def send(array, pairs):
    return lax.ppermute(array, ALL, pairs)


def dot(a, b):
    return lax.dot_general(a, b, (((1,), (0,)), ((), ())), preferred_element_type=F32)


def dot_rows(a, b):
    return lax.dot_general(a, b, (((0,), (0,)), ((), ())), preferred_element_type=F32)


def dot_cols(a, b):
    return lax.dot_general(a, b, (((1,), (1,)), ((), ())), preferred_element_type=F32)


def rotate(values, cosine, sine):
    half = values.shape[-1] // 2
    a, b = values[..., :half], values[..., half:]
    return jnp.concatenate([a * cosine - b * sine, b * cosine + a * sine], axis=-1)


def general(plan, layer_in, first_layer_value, v1_acc, cotangent, seq_starts, norm1_gain, w_query, w_key, w_value,
          w_out, norm2_gain, w_gate, w_up, w_down):
    G, T, bits = plan.G, plan.T, plan.bits
    micro, L, D = layer_in.shape
    FF = w_gate.shape[1]
    HT, FT, heads = D // T, FF // T, H // T
    HD = D // H
    M = 2 * L
    N = T * M
    rows, frows = w_query.shape[0], w_down.shape[0]
    g, gy = lax.axis_index("gx"), lax.axis_index("gy")
    h, t = gy // T, gy % T

    def to_t(array, bit):
        return send(array, plan.t_swap[bit])

    def to_g(array, k):
        return send(array, plan.g_swap[k]) if k else array

    def to_h(array):
        return send(array, plan.h_swap)

    def inward(array):
        return jnp.concatenate([pick(array, h), to_h(pick(array, 1 - h))], axis=0)

    def outward(array):
        own, other = array[:L], to_h(array[L:])
        return jnp.stack([jnp.where(h == 0, own, other), jnp.where(h == 0, other, own)])

    def gather_t(array):
        parts = {0: array}
        for bit in bits:
            order = sorted(parts)
            moved = to_t(jnp.concatenate([parts[j] for j in order], axis=0), bit)
            size = array.shape[0]
            for i, j in enumerate(order):
                parts[j ^ bit] = moved[i * size:(i + 1) * size]
        return [parts[j] for j in range(T)]

    def reduce_t(partial):
        blocks = partial.reshape((T, -1) + partial.shape[1:])
        for bit in reversed(bits):
            shape = blocks.shape
            split = blocks.reshape((shape[0] // 2, 2) + shape[1:])
            blocks = split[:, 0] + to_t(split[:, 1].astype(BF16), bit).astype(F32)
        return blocks[0]

    def exchange_t(parts):
        held = {j: [parts[j]] for j in range(T)}
        sources = [0]
        for bit in bits:
            out = [j for j in sorted(held) if j & bit]
            flat = [p for j in out for p in held[j]]
            moved = to_t(jnp.stack(flat), bit)
            n = len(sources)
            new = {}
            for i, j in enumerate(out):
                new[j ^ bit] = held[j ^ bit] + [moved[i * n + s] for s in range(n)]
            sources = sources + [s ^ bit for s in sources]
            held = new
        result = [None] * T
        for s, p in zip(sources, held[0]):
            result[s] = p
        return result

    def natural(parts):
        array = jnp.stack(parts)
        for bit in bits:
            split = array.reshape((-1, 2, bit) + array.shape[1:])
            array = jnp.where((t & bit) != 0, split[:, ::-1], split).reshape(array.shape)
        return array

    def gather_r(block):
        other = to_h(block)
        pair = jnp.where(h == 0, jnp.stack([block, other]), jnp.stack([other, block]))
        full = jnp.zeros((G,) + pair.shape, pair.dtype)
        for k in range(G):
            full = lax.dynamic_update_slice(full, to_g(pair, k)[None], (g ^ k,) + (0,) * pair.ndim)
        return full.reshape((G * 2 * block.shape[0],) + block.shape[1:])

    def gather_cols(slices):
        block = natural(exchange_t([pick(slices, t ^ j) for j in range(T)]))
        return gather_r(block.reshape(T * block.shape[1], -1))

    def reduce_r(grad):
        n, w = grad.shape[0] // (2 * G), grad.shape[1]
        grad = grad.astype(BF16).reshape(G, 2 * n, w)
        total = pick(grad, g).astype(F32)
        for k in range(1, G):
            total = total + to_g(pick(grad, g ^ k), k).astype(F32)
        total = total.reshape(2, n, w)
        return pick(total, h) + to_h(pick(total, 1 - h).astype(BF16)).astype(F32)

    def scatter_cols(grad):
        total = reduce_r(grad).reshape(T, rows, -1)
        low = total.astype(BF16)
        return natural(exchange_t([pick(low, t ^ j) for j in range(T)])).astype(F32)

    pad = jnp.zeros((rows, 126), BF16)
    gains_in = jnp.concatenate([norm1_gain[:, None], norm2_gain[:, None], pad], axis=1)

    def col_slices(w):
        return w.reshape(rows, T, HT).transpose(1, 0, 2)

    def hidden_slices(w):
        return w.reshape(rows, 2 * G, T, frows).transpose(2, 0, 1, 3).reshape(T, rows, FT)

    qkv_slices = jnp.concatenate([col_slices(w_query), col_slices(w_key), col_slices(w_value),
                                  jnp.broadcast_to(gains_in[None], (T, rows, 128))], axis=2)
    x_own = inward(layer_in)
    qkv_w = gather_cols(qkv_slices)
    x_all = jnp.concatenate(gather_t(x_own), axis=0)
    v_own = inward(first_layer_value).reshape(M, T, HT).transpose(1, 0, 2)
    v_all = jnp.concatenate(exchange_t([pick(v_own, t ^ j) for j in range(T)]), axis=0)
    gu_w = gather_cols(jnp.concatenate([hidden_slices(w_gate), hidden_slices(w_up)], axis=2))
    down_w = gather_r(w_down)
    c_own = inward(cotangent)
    c_all = jnp.concatenate(gather_t(c_own), axis=0)
    out_w = natural(gather_t(gather_r(w_out))).reshape(T, 2 * G, rows, D).transpose(1, 0, 2, 3).reshape(D, D)
    out_w = out_w.reshape(T, HT, D)

    gains = qkv_w[:, 3 * HT:3 * HT + 2].astype(F32).T
    gain_one, gain_two = gains[0], gains[1]
    query_w, key_w, value_w = qkv_w[:, :HT], qkv_w[:, HT:2 * HT], qkv_w[:, 2 * HT:3 * HT]
    gate_w, up_w = gu_w[:, :FT], gu_w[:, FT:]

    starts = pick(seq_starts, h)
    member = t ^ jnp.arange(T, dtype=jnp.int32)
    half = h ^ jnp.arange(2, dtype=jnp.int32)
    position = ((half[None, :] * T + member[:, None]) * L)[:, :, None] + jnp.arange(L, dtype=jnp.int32)
    position = position.reshape(N) + g * N
    begin = jnp.max(jnp.where(starts[None, :] <= position[:, None], starts[None, :], 0), axis=1)
    rel = (position - begin).astype(F32)
    visible = (begin[:, None] == begin[None, :]) & (position[None, :] <= position[:, None])
    frequency = 10000.0 ** (-(jnp.arange(HD // 2, dtype=F32) * 2.0 / HD))
    angles = rel[:, None] * frequency[None, :]
    cosine, sine = jnp.cos(angles)[:, None, :], jnp.sin(angles)[:, None, :]

    x = x_all.astype(F32)
    rstd_one = lax.rsqrt(jnp.mean(x * x, axis=-1, keepdims=True) + EPS)
    normed_one = (x * rstd_one * gain_one).astype(BF16)
    query = rotate(dot(normed_one, query_w).reshape(N, heads, HD), cosine, sine).astype(BF16)
    key = rotate(dot(normed_one, key_w).reshape(N, heads, HD), cosine, sine).astype(BF16)
    value = (0.5 * dot(normed_one, value_w) + 0.5 * v_all.astype(F32)).astype(BF16).reshape(N, heads, HD)
    scores = jnp.einsum("ihd,jhd->hij", query, key, preferred_element_type=F32) * SCALE
    scores = jnp.where(visible[None], scores, NEG)
    top = jnp.max(scores, axis=-1, keepdims=True)
    probs = jnp.exp(scores - top)
    denom = jnp.sum(probs, axis=-1, keepdims=True)
    probs = probs / denom
    probs_low = probs.astype(BF16)
    attn = jnp.einsum("hij,jhd->ihd", probs_low, value, preferred_element_type=F32)
    attn_low = attn.reshape(N, HT).astype(BF16)
    attn_parts = []
    for j, part in enumerate(gather_t(attn_low)):
        part = part.reshape(T, M, HT)
        attn_parts.append(jnp.concatenate([part[b ^ j] for b in range(T)], axis=0))
    after = x
    for j in range(T):
        after = after + dot(attn_parts[j], pick(out_w, t ^ j))
    rstd_two = lax.rsqrt(jnp.mean(after * after, axis=-1, keepdims=True) + EPS)
    hat_two = after * rstd_two
    normed_two = (hat_two * gain_two).astype(BF16)
    gate = dot(normed_two, gate_w)
    up = dot(normed_two, up_w)
    sig = jax.nn.sigmoid(gate)
    act = gate * sig
    hidden = (act * up).astype(BF16)

    grad_hidden = dot_cols(c_all, down_w)
    grad_gate = (grad_hidden * up * (sig * (1.0 + gate * (1.0 - sig)))).astype(BF16)
    grad_up = (grad_hidden * act).astype(BF16)
    grad_two_part = dot_cols(grad_gate, gate_w) + dot_cols(grad_up, up_w)
    gain_two_grad = jnp.sum(grad_two_part * hat_two, axis=0)
    grad_two = reduce_t(grad_two_part) * gain_two
    hat_own = hat_two[:M]
    grad_after = c_own.astype(F32) + rstd_two[:M] * (
        grad_two - hat_own * jnp.mean(grad_two * hat_own, axis=-1, keepdims=True))
    grad_branch = jnp.concatenate(gather_t(grad_after.astype(BF16)), axis=0)
    result = reduce_t(dot(hidden, down_w)) + after[:M]
    layer_out = outward(result.astype(BF16))
    grad_down = dot_rows(hidden, c_all)
    grad_gu = dot_rows(normed_two, jnp.concatenate([grad_gate, grad_up], axis=1))

    grad_attn = dot_cols(grad_branch, pick(out_w, t)).astype(BF16).reshape(N, heads, HD)
    delta = jnp.sum(grad_attn.astype(F32) * attn, axis=-1).T
    grad_probs = jnp.einsum("ihd,jhd->hij", grad_attn, value, preferred_element_type=F32)
    grad_scores = (probs * (grad_probs - delta[..., None])).astype(BF16)
    grad_query = jnp.einsum("hij,jhd->ihd", grad_scores, key, preferred_element_type=F32) * SCALE
    grad_key = jnp.einsum("hij,ihd->jhd", grad_scores, query, preferred_element_type=F32) * SCALE
    grad_blend = jnp.einsum("hij,ihd->jhd", probs_low, grad_attn, preferred_element_type=F32).reshape(N, HT)
    grad_query = rotate(grad_query, cosine, -sine).reshape(N, HT).astype(BF16)
    grad_key = rotate(grad_key, cosine, -sine).reshape(N, HT).astype(BF16)
    grad_value = (0.5 * grad_blend).astype(BF16)
    grad_one_part = dot_cols(grad_query, query_w) + dot_cols(grad_key, key_w) + dot_cols(grad_value, value_w)
    hat_one = x * rstd_one
    gain_one_grad = jnp.sum(grad_one_part * hat_one, axis=0)
    grad_one = reduce_t(grad_one_part) * gain_one
    hat_own = hat_one[:M]
    input_grad = grad_after + rstd_one[:M] * (
        grad_one - hat_own * jnp.mean(grad_one * hat_own, axis=-1, keepdims=True))
    input_grad = outward(input_grad.astype(BF16)).astype(F32)
    v_parts = natural(exchange_t([grad_value[j * M:(j + 1) * M] for j in range(T)]))
    v1_out = v1_acc + outward(v_parts.transpose(1, 0, 2).reshape(M, D)).astype(F32)

    attn_full = natural([p.T for p in attn_parts]).reshape(2 * G, T, rows, N)
    grad_out = dot(pick(attn_full, t, 1).reshape(2 * G * rows, N), grad_branch)
    grad_gains = jnp.stack([gain_one_grad, gain_two_grad], axis=1)
    grad_gains = jnp.concatenate([grad_gains, jnp.zeros((D, 126), F32)], axis=1)
    grad_qkv = dot_rows(normed_one, jnp.concatenate([grad_query, grad_key, grad_value], axis=1))
    down_g = reduce_r(grad_down)
    gu_g = scatter_cols(grad_gu)
    out_g = reduce_r(grad_out)
    qkv_g = scatter_cols(jnp.concatenate([grad_qkv, grad_gains], axis=1))

    def col_join(parts):
        return parts.transpose(1, 0, 2).reshape(rows, D)

    def hidden_join(parts):
        return parts.reshape(T, rows, 2 * G, frows).transpose(1, 2, 0, 3).reshape(rows, FF)

    gain_g = jnp.sum(qkv_g[:, :, 3 * HT:3 * HT + 2], axis=0)
    return (layer_out, input_grad, v1_out, gain_g[:, 0], col_join(qkv_g[:, :, :HT]), col_join(qkv_g[:, :, HT:2 * HT]),
            col_join(qkv_g[:, :, 2 * HT:3 * HT]), out_g, gain_g[:, 1], hidden_join(gu_g[:, :, :FT]),
            hidden_join(gu_g[:, :, FT:]), down_g)


FAST_G, FAST_T, FAST_L, D, HT, FT, FROWS, ROWS = 4, 4, 64, 1024, 256, 704, 88, 32
M, N = 2 * FAST_L, 8 * FAST_L
HALF = N // 2
WQ = 3 * HT + 128
ORDER = (0, 2, 1, 3)
HD = 64
ARRIVED = ((0, 0), (1, 0), (2, 0), (3, 0), (0, 1), (2, 1), (1, 1), (3, 1))
LEAVING = {(0, 0): (0, 0), (1, 0): (0, 1), (2, 0): (1, 0), (3, 0): (1, 1), (0, 1): (2, 0), (2, 1): (2, 1), (1, 1): (3, 0), (3, 1): (3, 1)}
VMEM = pl.BlockSpec(memory_space=pltpu.VMEM)
SMEM = pl.BlockSpec(memory_space=pltpu.SMEM)
ANY = pl.BlockSpec(memory_space=pltpu.HBM)


def shape(dims, dtype=BF16):
    return jax.ShapeDtypeStruct(dims, dtype)


def call(kernel, outs, specs, args, scratch=(), mib=40):
    return pl.pallas_call(
        kernel,
        out_shape=outs,
        in_specs=specs,
        out_specs=jax.tree.map(lambda _: VMEM, outs),
        scratch_shapes=list(scratch),
        compiler_params=pltpu.CompilerParams(vmem_limit_bytes=mib << 20),
        cost_estimate=pl.CostEstimate(flops=1, bytes_accessed=1, transcendentals=0),
    )(*args)


def aligned(index, size):
    return pl.ds(pl.multiple_of(index * size, size), size)


def eye(rows, lanes):
    return (lax.broadcasted_iota(jnp.int32, (rows, lanes), 0) == lax.broadcasted_iota(jnp.int32, (rows, lanes), 1)).astype(BF16)


def tiles_in(block):
    lines = [jnp.concatenate([block[j * 8:j * 8 + 8, i * 128:i * 128 + 128] for j in range(11)], axis=1) for i in range(8)]
    return jnp.concatenate(lines, axis=0)


def tiles_out(block):
    lines = [jnp.concatenate([block[i * 8:i * 8 + 8, j * 128:j * 128 + 128] for i in range(8)], axis=1) for j in range(11)]
    return jnp.concatenate(lines, axis=0)


def line_tiles_in(block):
    tiles = [block[j * 8:j * 8 + 8, i * 128:i * 128 + 128] for j in range(4) for i in range(8)]
    tiles += [jnp.zeros_like(tiles[0])] * 3
    return jnp.concatenate([jnp.concatenate(tiles[n * 7:n * 7 + 7], axis=1) for n in range(5)], axis=0)


def line_tiles_out(block):
    tiles = [block[n * 8:n * 8 + 8, i * 128:i * 128 + 128] for n in range(5) for i in range(7)]
    return jnp.concatenate([jnp.concatenate(tiles[j * 8:j * 8 + 8], axis=1) for j in range(4)], axis=0)


def pack_first(ids, gain_one, gain_two, wq, wk, wv, wo, x, v, c, out, keep, lines, xv_out, c_out, rows, whole, sem):
    h, t = ids[1], ids[2]
    copies = []
    for j in (2, 3, 0, 1):
        to = keep if j < 2 else out
        for i, w in enumerate((wq, wk, wv)):
            copies.append((w.at[:, aligned(t ^ j, HT)], to.at[j % 2, :, i * HT:(i + 1) * HT]))
    copies += [(wo, whole), (x.at[1 - h], xv_out.at[:, :D]), (v.at[1 - h], xv_out.at[:, D:]), (c.at[1 - h], c_out)]
    started = fetch(copies, sem)
    rows[...] = jnp.zeros_like(rows)
    rows[0:1] = gain_one[...].astype(F32)
    rows[1:2] = gain_two[...].astype(F32)
    gains = dot_rows(rows[...].astype(BF16), eye(8, 128)).astype(BF16)
    for j in range(4):
        (keep if j < 2 else out)[j % 2, :, 3 * HT:] = gains
    started[12].wait()
    lines[...] = line_tiles_in(whole[...].astype(F32)).astype(BF16)
    for n, copy in enumerate(started):
        if n != 12:
            copy.wait()


def pack_hidden(ids, wg, wu, wd, keep, out, down, nat, gate, up, whole, sem):
    t = ids[2]
    started = fetch([(wg, gate), (wu, up), (wd, whole)], sem)
    for a, w in enumerate((gate, up)):
        started[a].wait()
        for m in range(4):
            for i in range(8):
                at, to = (i * 4 + m) * FROWS, a * FT + i * FROWS
                nat[m, :, to:to + FROWS] = w[:, at:at + FROWS].astype(F32)
    for j in range(4):
        to = keep if j < 2 else out
        to[j % 2] = nat[t ^ j].astype(BF16)
    started[2].wait()
    down[...] = tiles_in(whole[...].astype(F32)).astype(BF16)


def pack_out(b0, b1, b2, b3, out, raw, sem):
    started = fetch([((b0, b1, b2, b3)[n // 2].at[n % 2, 4 * ROWS:], raw.at[n]) for n in range(8)], sem)
    for n in range(8):
        started[n].wait()
        out[n * ROWS:(n + 1) * ROWS] = line_tiles_out(raw[n].astype(F32)).astype(BF16)


def pack_second(ids, x, v, moved, xv_out, v_keep, own, sem):
    h, t = ids[1], ids[2]
    started = fetch([(x.at[h], xv_out.at[:FAST_L, :D]), (v.at[h], own.at[:FAST_L]),
                     (moved.at[:, :D], xv_out.at[FAST_L:, :D]), (moved.at[:, D:], own.at[FAST_L:])], sem)
    for copy in started:
        copy.wait()
    for j in range(2):
        v_keep[j] = own[:, aligned(t ^ j, HT)]
        xv_out[:, D + j * HT:D + (j + 1) * HT] = own[:, aligned(t ^ (j + 2), HT)]


def pack_third(mine, moved, v_keep, out, v_two):
    out[:M, :D] = mine[:, :D]
    out[M:, :D] = moved[:, :D]
    out[:M, D:] = v_keep[1]
    out[M:, D:] = moved[:, D + HT:]
    v_two[:M] = v_keep[0]
    v_two[M:] = moved[:, D:D + HT]


def fetch(copies, sem):
    started = []
    for i, (source, target) in enumerate(copies):
        copy = pltpu.make_async_copy(source, target, sem.at[i])
        copy.start()
        started.append(copy)
    return started


def swap_halves(u):
    width = u.shape[-1]
    lane = lax.broadcasted_iota(jnp.int32, u.shape, 1)
    up = pltpu.roll(u, width - HD // 2, 1)
    down = pltpu.roll(u, HD // 2, 1)
    return jnp.where(lane % HD < HD // 2, up, down)


def scale_of(x):
    return lax.rsqrt(jnp.mean(x * x, axis=-1, keepdims=True) + EPS)


def attend_kernel(ids, x2, xc, v2, cs, sn, bias, b0, b1, b2, b3, w, normed, qkv, attn, low, lse, gains, sem):
    g, h, t = ids[0], ids[1], ids[2]
    copies = []
    for n, (k, dh) in enumerate(ARRIVED):
        b = (b0, b1, b2, b3)[n // 2]
        for i, s in enumerate(ORDER):
            row = ((g ^ k) * 2 + (h ^ dh)) * 4 + (t ^ s)
            copies.append((b.at[n % 2, i * ROWS:(i + 1) * ROWS], w.at[aligned(row, ROWS)]))
    for copy in fetch(copies, sem):
        copy.wait()
    gains[...] = dot_cols(eye(8, 128), w[:, 3 * HT:])
    gain = gains[0:1, :]
    for b in range(2):
        rows = slice(b * HALF, (b + 1) * HALF)
        source = x2 if b == 0 else xc
        x = source[:, :D].astype(F32)
        r = (x * scale_of(x) * gain).astype(BF16)
        normed[rows] = r
        out = dot(r, w[:, :3 * HT])
        for i in range(2):
            u = out[:, i * HT:(i + 1) * HT]
            qkv[rows, i * HT:(i + 1) * HT] = (u * cs[rows] + swap_halves(u) * sn[rows]).astype(BF16)
        value = v2[...] if b == 0 else xc[:, D:]
        qkv[rows, 2 * HT:] = (0.5 * out[:, 2 * HT:] + 0.5 * value.astype(F32)).astype(BF16)
    for b in range(2):
        rows = slice(b * HALF, (b + 1) * HALF)
        outs, tops = [], []
        for i in range(4):
            lanes = slice(i * HD, (i + 1) * HD)
            q = qkv[rows, lanes]
            k = qkv[:, HT + i * HD:HT + (i + 1) * HD]
            v = qkv[:, 2 * HT + i * HD:2 * HT + (i + 1) * HD]
            s = dot_cols(q, k) * SCALE + bias[rows]
            top = jnp.max(s, axis=-1, keepdims=True)
            p = jnp.exp(s - top)
            total = jnp.sum(p, axis=-1, keepdims=True)
            outs.append(dot(p.astype(BF16), v) / total)
            tops.append(top + jnp.log(total))
        o = jnp.concatenate(outs, axis=1)
        attn[rows] = o
        low[rows] = o.astype(BF16)
        lse[rows] = jnp.concatenate(tops, axis=1)


def after_kernel(ids, x2, xc, o2, oc, gains, co2, coc, full, after, normed, own_w, w, sem):
    g, h, t = ids[0], ids[1], ids[2]
    copies = []
    for i, s in enumerate(ORDER):
        source = co2 if i < 2 else coc
        for n, (k, dh) in enumerate(ARRIVED):
            row = ((g ^ k) * 2 + (h ^ dh)) * 4 + (t ^ s)
            at = (i % 2) * HT + n * ROWS
            copies.append((source.at[at:at + ROWS], w.at[aligned(row, ROWS)]))
    started = fetch(copies, sem)
    for i, s in enumerate(ORDER):
        source = o2 if i < 2 else oc
        for p in range(4):
            q = ORDER.index(ORDER[p] ^ s)
            full[p * M:(p + 1) * M, aligned(t ^ s, HT)] = source[(i % 2) * N + q * M:(i % 2) * N + (q + 1) * M]
    for copy in started:
        copy.wait()
    own_w[...] = w[aligned(t, HT)]
    gain = gains[1:2, :]
    for b in range(2):
        rows = slice(b * HALF, (b + 1) * HALF)
        source = x2 if b == 0 else xc
        a = source[:, :D].astype(F32) + dot(full[rows], w[...])
        after[rows] = a
        normed[rows] = (a * scale_of(a) * gain).astype(BF16)


def feed_kernel(ids, normed, after, c2, cc, u0, u1, u2, u3,
                hidden, dgu, out_keep, out_send, r_keep, r_send, gain_g, c_all, w, wd, wide, raw, sem, sem_d):
    g, h, t = ids[0], ids[1], ids[2]
    copies, copies_d = [], []
    for n, (k, dh) in enumerate(ARRIVED):
        b = (u0, u1, u2, u3)[n // 2]
        for i, s in enumerate(ORDER):
            row = ((g ^ k) * 2 + (h ^ dh)) * 4 + (t ^ s)
            copies.append((b.at[n % 2, i * ROWS:(i + 1) * ROWS], w.at[aligned(row, ROWS)]))
        copies_d.append((b.at[n % 2, 4 * ROWS:], raw.at[n]))
    started, started_d = fetch(copies, sem), fetch(copies_d, sem_d)
    for p in range(4):
        c_all[p * M:(p + 1) * M] = (c2 if p < 2 else cc)[(p % 2) * M:(p % 2 + 1) * M]
    for copy in started_d:
        copy.wait()
    for n, (k, dh) in enumerate(ARRIVED):
        wide[aligned((g ^ k) * 2 + (h ^ dh), FROWS)] = tiles_out(raw[n].astype(F32))
    wd[...] = wide[...].astype(BF16)
    for copy in started:
        copy.wait()
    gain_sum = jnp.zeros((1, D), F32)
    for b in range(2):
        rows = slice(b * HALF, (b + 1) * HALF)
        gu = dot(normed[rows], w[...])
        gate, up = gu[:, :FT], gu[:, FT:]
        sig = 1.0 / (1.0 + jnp.exp(-gate))
        act = gate * sig
        hid = (act * up).astype(BF16)
        hidden[rows] = hid
        dh = dot_cols(c_all[rows], wd[...])
        dgate = (dh * up * (sig * (1.0 + gate * (1.0 - sig)))).astype(BF16)
        dup = (dh * act).astype(BF16)
        dgu[rows, :FT] = dgate
        dgu[rows, FT:] = dup
        dr = dot_cols(dgu[rows], w[...])
        out = dot(hid, wd[...])
        a = after[rows]
        gain_sum = gain_sum + jnp.sum(dr * (a * scale_of(a)), axis=0, keepdims=True)
        if b == 0:
            r_keep[...] = dr
            out_keep[...] = out
        else:
            r_send[...] = dr.astype(BF16)
            out_send[...] = out.astype(BF16)
    gain_g[...] = gain_sum


def feed_weights_kernel(ids, normed, dgu, hidden, c_all, a_keep, a_send, b_keep, b_send, gu, full):
    g, h = ids[0], ids[1]
    full[...] = dot_rows(hidden[...], c_all[...])
    for k in range(4):
        gu[...] = dot_rows(normed[:, aligned(g ^ k, HT)], dgu[...])
        for e in range(2):
            target, at = LEAVING[(k, e)]
            target = (a_keep, a_send, b_keep, b_send)[target]
            target[at, :4 * ROWS] = gu[aligned(h ^ e, 4 * ROWS)].astype(BF16)
            target[at, 4 * ROWS:] = tiles_in(full[aligned((g ^ k) * 2 + (h ^ e), FROWS)]).astype(BF16)


def fold_kernel(keep, moved, kept, send):
    kept[...] = keep[:M] + moved[:M].astype(F32)
    send[...] = (keep[M:] + moved[M:].astype(F32)).astype(BF16)


def fold_both_kernel(keep, dv, moved, kept, send):
    kept[...] = keep[:M] + moved[:M, :D].astype(F32)
    send[:, :D] = (keep[M:] + moved[M:, :D].astype(F32)).astype(BF16)
    send[:, D:D + HT] = dv[M:]
    send[:, D + HT:] = moved[M:, D:]


def branch_kernel(keep, moved, after, gains, c2, grad_after, low):
    a = after[:M]
    scale = scale_of(a)
    hat = a * scale
    dy = (keep[...] + moved[...].astype(F32)) * gains[1:2, :]
    d = c2[:M].astype(F32) + scale * (dy - hat * jnp.mean(dy * hat, axis=-1, keepdims=True))
    grad_after[...] = d
    low[...] = d.astype(BF16)


def attend_back_kernel(ids, da2, dac, wo, qkv, attn, lse, bias, cs, sn, w, x2, xc,
                       dqkv, r_keep, r_send, gain_g, do, dk, dv):
    for b in range(2):
        rows = slice(b * HALF, (b + 1) * HALF)
        do[rows] = dot_cols((da2 if b == 0 else dac)[...], wo[...]).astype(BF16)
    for b in range(2):
        rows = slice(b * HALF, (b + 1) * HALF)
        dqs = []
        for i in range(4):
            lanes = slice(i * HD, (i + 1) * HD)
            q = qkv[rows, lanes]
            k = qkv[:, HT + i * HD:HT + (i + 1) * HD]
            v = qkv[:, 2 * HT + i * HD:2 * HT + (i + 1) * HD]
            d = do[rows, lanes]
            delta = jnp.sum(d.astype(F32) * attn[rows, lanes], axis=-1, keepdims=True)
            p = jnp.exp(dot_cols(q, k) * SCALE + bias[rows] - lse[rows, i:i + 1])
            ds = (p * (dot_cols(d, v) - delta)).astype(BF16)
            dqs.append(dot(ds, k))
            dki, dvi = dot_rows(ds, q), dot_rows(p.astype(BF16), d)
            if b == 0:
                dk[:, lanes], dv[:, lanes] = dki, dvi
            else:
                dk[:, lanes], dv[:, lanes] = dk[:, lanes] + dki, dv[:, lanes] + dvi
        u = jnp.concatenate(dqs, axis=1) * SCALE
        dqkv[rows, :HT] = (u * cs[rows] - swap_halves(u) * sn[rows]).astype(BF16)
    gain_sum = jnp.zeros((1, D), F32)
    for b in range(2):
        rows = slice(b * HALF, (b + 1) * HALF)
        u = dk[rows] * SCALE
        dqkv[rows, HT:2 * HT] = (u * cs[rows] - swap_halves(u) * sn[rows]).astype(BF16)
        dqkv[rows, 2 * HT:] = (0.5 * dv[rows]).astype(BF16)
        dr = dot_cols(dqkv[rows], w[:, :3 * HT])
        x = (x2 if b == 0 else xc)[:, :D].astype(F32)
        gain_sum = gain_sum + jnp.sum(dr * (x * scale_of(x)), axis=0, keepdims=True)
        if b == 0:
            r_keep[...] = dr
        else:
            r_send[:, :D] = dr.astype(BF16)
            r_send[:, D:] = dqkv[rows, 2 * HT:]
    gain_g[...] = gain_sum


def attend_weights_kernel(ids, normed, dqkv, gain_one, gain_two, full, da2, dac, a_keep, a_send, b_keep, b_send,
                          scratch, rows_g, qkv):
    g, h, t = ids[0], ids[1], ids[2]
    rows_g[...] = jnp.zeros_like(rows_g)
    rows_g[0:1] = gain_one[...]
    rows_g[1:2] = gain_two[...]
    for k in range(4):
        lanes = aligned(g ^ k, HT)
        qkv[:, :3 * HT] = dot_rows(normed[:, lanes], dqkv[...])
        qkv[:, 3 * HT:] = dot_rows(rows_g[:, lanes].astype(BF16), eye(8, 128))
        scratch[...] = dot_rows(full[:HALF, lanes], da2[...]) + dot_rows(full[HALF:, lanes], dac[...])
        for e in range(2):
            target, at = LEAVING[(k, e)]
            target = (a_keep, a_send, b_keep, b_send)[target]
            target[at, :4 * ROWS] = qkv[aligned(h ^ e, 4 * ROWS)].astype(BF16)
            target[at, 4 * ROWS:] = line_tiles_in(scratch[aligned((h ^ e) * 4 + t, ROWS)]).astype(BF16)


def sum_first_kernel(a_keep, a_moved, b_keep, b_moved, a_own, a_send, b_own, b_send):
    for keep, moved, own, out in ((a_keep, a_moved, a_own, a_send), (b_keep, b_moved, b_own, b_send)):
        own[...] = (keep[0].astype(F32) + moved[0].astype(F32)).astype(BF16)
        out[...] = (keep[1].astype(F32) + moved[1].astype(F32)).astype(BF16)


def sum_second_kernel(b_own, b_moved, b_send):
    b_send[...] = (b_own[...].astype(F32) + b_moved[...].astype(F32)).astype(BF16)


def sum_third(a_own, a_moved, moved, total):
    total[...] = (a_own[...].astype(F32) + a_moved[...].astype(F32)) + moved[...].astype(F32)


def sum_hidden_kernel(ids, a_own, a_moved, moved, kept, send, down, total):
    t = ids[2]
    sum_third(a_own, a_moved, moved, total)
    for j in range(4):
        (kept if j < 2 else send)[j % 2] = total[aligned(t ^ j, ROWS)].astype(BF16)
    down[...] = tiles_out(total[4 * ROWS:])


def sum_qkv_kernel(ids, a_own, a_moved, moved, kept, send, out, total):
    t = ids[2]
    sum_third(a_own, a_moved, moved, total)
    for j in range(4):
        (kept if j < 2 else send)[j % 2] = total[aligned(t ^ j, ROWS)].astype(BF16)
    out[...] = line_tiles_out(total[4 * ROWS:])


def join_qkv_kernel(ids, kept, first, last, q, k, v, gains):
    t = ids[2]
    parts = (kept[0], first[0], last[0], last[1])
    for s, part in zip(ORDER, parts):
        for i, ref in enumerate((q, k, v)):
            ref[:, aligned(t ^ s, HT)] = part[:, i * HT:(i + 1) * HT].astype(F32)
    low = [part[:, 3 * HT:].astype(F32) for part in parts]
    gains[...] = (low[0] + low[1]) + (low[2] + low[3])


def join_hidden_kernel(ids, kept, first, last, gate, up, nat):
    t = ids[2]
    for s, part in zip(ORDER, (kept[0], first[0], last[0], last[1])):
        nat[t ^ s] = part.astype(F32)
    for m in range(4):
        for a, ref in enumerate((gate, up)):
            for i in range(8):
                to, at = (i * 4 + m) * FROWS, a * FT + i * FROWS
                ref[:, to:to + FROWS] = nat[m, :, at:at + FROWS]


def input_kernel(ids, keep, moved, x2, gains, grad_after, dv, dv_core, own, send, both):
    t = ids[2]
    x = x2[:M, :D].astype(F32)
    scale = scale_of(x)
    hat = x * scale
    dy = (keep[...] + moved[:, :D].astype(F32)) * gains[0:1, :]
    both[:, :D] = (grad_after[...] + scale * (dy - hat * jnp.mean(dy * hat, axis=-1, keepdims=True))).astype(BF16)
    parts = (dv[:M], moved[:, D:D + HT], dv_core[:M, D:], moved[:, D + HT:])
    for s, part in zip(ORDER, parts):
        both[:, aligned(4 + (t ^ s), HT)] = part
    own[...] = both[:FAST_L]
    send[...] = both[FAST_L:]


def home_kernel(ids, own, moved, v1, grad, v_out):
    h = ids[1]
    grad[h] = own[:, :D].astype(F32)
    grad[1 - h] = moved[:, :D].astype(F32)
    v_out[h] = v1[h] + own[:, D:].astype(F32)
    v_out[1 - h] = v1[1 - h] + moved[:, D:].astype(F32)


def result_kernel(keep, moved, after, own, send):
    out = after[:M] + (keep[...] + moved[...].astype(F32))
    own[...] = out[:FAST_L].astype(BF16)
    send[...] = out[FAST_L:].astype(BF16)


def result_home_kernel(ids, own, moved, out):
    h = ids[1]
    out[h] = own[...]
    out[1 - h] = moved[...]


def fast(plan, layer_in, first_layer_value, v1_acc, cotangent, seq_starts, norm1_gain, w_query, w_key, w_value,
         w_out, norm2_gain, w_gate, w_up, w_down):
    L = FAST_L
    g, gy = lax.axis_index("gx"), lax.axis_index("gy")
    h, t = gy // 4, gy % 4
    ids = jnp.stack([g, h, t]).astype(jnp.int32)

    def to_z(array):
        return send(array, plan.t_swap[2])

    def to_core(array):
        return send(array, plan.t_swap[1])

    def to_h(array):
        return send(array, plan.h_swap)

    def to_x(array):
        return send(array, plan.g_swap[1])

    def to_y(array):
        return send(array, plan.g_swap[2])

    def after_these(array, *others):
        return lax.optimization_barrier((array,) + others)[0]

    def spread(own, other, *first):
        a_pair = jnp.stack([own, to_x(own)])
        b_pair = jnp.stack([other, to_y(other)])
        a_pair, b_pair = lax.optimization_barrier((a_pair, b_pair) + first)[:2]
        return a_pair, to_y(a_pair), b_pair, to_x(b_pair)

    starts = pick(seq_starts, h)
    member = t ^ jnp.array(ORDER, jnp.int32)
    half = h ^ jnp.arange(2, dtype=jnp.int32)
    position = ((half[None, :] * 4 + member[:, None]) * L)[:, :, None] + jnp.arange(L, dtype=jnp.int32)
    position = position.reshape(N) + g * N
    begin = jnp.max(jnp.where(starts[None, :] <= position[:, None], starts[None, :], 0), axis=1)
    visible = (begin[:, None] == begin[None, :]) & (position[None, :] <= position[:, None])
    bias = jnp.where(visible, 0.0, NEG).astype(F32)
    frequency = 10000.0 ** (-(jnp.arange(HD // 2, dtype=F32) * 2.0 / HD))
    angles = (position - begin).astype(F32)[:, None] * frequency[None, :]
    cosine, sine = jnp.cos(angles), jnp.sin(angles)
    cs = jnp.tile(jnp.concatenate([cosine, cosine], axis=1), (1, 4))
    sn = jnp.tile(jnp.concatenate([-sine, sine], axis=1), (1, 4))

    q_send, q_keep, o_block, xv_send, c_send = call(
        pack_first, (shape((2, ROWS, WQ)), shape((2, ROWS, WQ)), shape((40, WQ)), shape((L, 2 * D)), shape((L, D))),
        [SMEM] + [VMEM] * 2 + [ANY] * 7,
        (ids, norm1_gain[None], norm2_gain[None], w_query, w_key, w_value, w_out, layer_in, first_layer_value, cotangent),
        [pltpu.VMEM((8, ROWS), F32), pltpu.VMEM((ROWS, D), BF16), pltpu.SemaphoreType.DMA((16,))], mib=63)
    q_first = to_z(q_send)
    xv_moved = to_h(xv_send)
    q_last = to_core(jnp.stack([q_keep[1], q_first[1]]))
    q_block = jnp.concatenate([q_keep[0], q_first[0], q_last[0], q_last[1], o_block], axis=0)
    q_other = to_h(q_block)
    xv_out, v_keep = call(pack_second, (shape((M, D + 2 * HT)), shape((2, M, HT))), [SMEM] + [ANY] * 3,
                          (ids, layer_in, first_layer_value, xv_moved), [pltpu.VMEM((M, D), BF16), pltpu.SemaphoreType.DMA((4,))], mib=63)
    x_two, v_two = call(pack_third, (shape((HALF, D + HT)), shape((HALF, HT))), [VMEM] * 3, (xv_out, to_z(xv_out), v_keep))
    x_core = to_core(x_two)
    q_other, cs, sn, bias, _ = lax.optimization_barrier((q_other, cs, sn, bias, xv_out))
    q_parts = spread(q_block, q_other, x_two)

    u_keep, u_send, d_block = call(
        pack_hidden, (shape((2, ROWS, 2 * FT)), shape((2, ROWS, 2 * FT)), shape((2 * ROWS, 2 * FT))), [SMEM] + [ANY] * 3,
        (after_these(ids, q_send), w_gate, w_up, w_down),
        [pltpu.VMEM((4, ROWS, 2 * FT), F32), pltpu.VMEM((ROWS, 4 * FT), BF16), pltpu.VMEM((ROWS, 4 * FT), BF16), pltpu.VMEM((FROWS, D), BF16),
         pltpu.SemaphoreType.DMA((3,))], mib=63)
    u_first = to_z(after_these(u_send, q_first))
    u_last = to_core(jnp.stack([u_keep[1], u_first[1]]))
    u_block = jnp.concatenate([u_keep[0], u_first[0], u_last[0], u_last[1], d_block], axis=0)
    u_other = to_h(after_these(u_block, q_other))
    c_moved = to_h(after_these(c_send, u_other))
    u_a = jnp.stack([u_block, to_x(after_these(u_block, q_parts[2]))])
    u_b = jnp.stack([u_other, to_y(u_other)])
    o_own = call(pack_out, shape((HT, D)), [ANY] * 4, q_parts, [pltpu.VMEM((8, 40, WQ), BF16), pltpu.SemaphoreType.DMA((8,))])
    o_first = to_z(o_own)
    q_parts = lax.optimization_barrier(q_parts + (u_a, u_b))[:4]
    qkv_w, normed_one, qkv, attn, attn_low, lse, gains = call(
        attend_kernel,
        (shape((D, WQ)), shape((N, D)), shape((N, 3 * HT)), shape((N, HT), F32), shape((N, HT)), shape((N, 4), F32), shape((8, D), F32)),
        [SMEM] + [VMEM] * 6 + [ANY] * 4, (ids, x_two, x_core, v_two, cs, sn, bias, *q_parts),
        [pltpu.SemaphoreType.DMA((32,))])
    a_two = jnp.concatenate([attn_low, to_z(attn_low)], axis=0)
    c_own = jnp.concatenate([pick(cotangent, h), after_these(c_moved, attn_low)], axis=0)
    o_two = jnp.concatenate([o_own, o_first], axis=0)
    o_core = to_core(after_these(o_two, attn_low))
    c_two = jnp.concatenate([c_own, to_z(after_these(c_own, a_two))], axis=0)
    c_core = to_core(c_two)
    u_parts = (u_a, to_y(u_a), u_b, to_x(u_b))
    a_core = to_core(a_two)
    attn_full, after, normed_two, out_w = call(
        after_kernel, (shape((N, D)), shape((N, D), F32), shape((N, D)), shape((HT, D))),
        [SMEM] + [VMEM] * 5 + [ANY] * 2, (ids, x_two, x_core, a_two, a_core, gains, o_two, o_core),
        [pltpu.VMEM((D, D), BF16), pltpu.SemaphoreType.DMA((32,))])
    hidden, dgu, out_keep, out_send, r_keep, r_send, gain_two_g, c_all = call(
        feed_kernel,
        (shape((N, FT)), shape((N, 2 * FT)), shape((HALF, D), F32), shape((HALF, D)), shape((HALF, D), F32), shape((HALF, D)),
         shape((1, D), F32), shape((N, D))),
        [SMEM] + [VMEM] * 4 + [ANY] * 4, (ids, normed_two, after, c_two, c_core, *u_parts),
        [pltpu.VMEM((D, 2 * FT), BF16), pltpu.VMEM((8 * FROWS, D), BF16), pltpu.VMEM((8 * FROWS, D), F32), pltpu.VMEM((8, 2 * ROWS, 2 * FT), BF16),
         pltpu.SemaphoreType.DMA((32,)), pltpu.SemaphoreType.DMA((8,))])

    kept, sent = call(fold_kernel, (shape((M, D), F32), shape((M, D))), [VMEM] * 2, (r_keep, to_core(r_send)))
    block = (2, 6 * ROWS, 2 * FT)
    a_keep, a_send, b_keep, b_send = call(
        feed_weights_kernel, (shape(block),) * 4, [SMEM] + [VMEM] * 4, (ids, normed_two, dgu, hidden, c_all),
        [pltpu.VMEM((HT, 2 * FT), F32), pltpu.VMEM((8 * FROWS, D), F32)])
    kept = after_these(kept, a_send)
    grad_after, branch = call(branch_kernel, (shape((M, D), F32), shape((M, D))), [VMEM] * 5,
                              (kept, to_z(sent), after, gains, c_two))
    b_two = jnp.concatenate([branch, to_z(branch)], axis=0)
    b_core = to_core(b_two)

    u_sums = (a_keep, to_y(a_send), b_keep, to_x(b_send))
    o_kept, o_sent = call(fold_kernel, (shape((M, D), F32), shape((M, D))), [VMEM] * 2,
                          (out_keep, to_core(after_these(out_send, b_two))))
    y_own, y_send = call(result_kernel, (shape((L, D)), shape((L, D))), [VMEM] * 3, (o_kept, to_z(o_sent), after))
    layer_out = call(result_home_kernel, shape((2, L, D)), [SMEM] + [VMEM] * 2, (ids, y_own, to_h(y_send)))

    b_core = after_these(b_core, o_sent)
    dqkv, r_keep, r_send, gain_one_g = call(
        attend_back_kernel,
        (shape((N, 3 * HT)), shape((HALF, D), F32), shape((HALF, D + HT)), shape((1, D), F32)),
        [SMEM] + [VMEM] * 12, (ids, b_two, b_core, out_w, qkv, attn, lse, bias, cs, sn, qkv_w, x_two, x_core),
        [pltpu.VMEM((N, HT), BF16), pltpu.VMEM((N, HT), F32), pltpu.VMEM((N, HT), F32)])
    dv_keep = dqkv[:HALF, 2 * HT:]
    r_core = after_these(to_core(r_send), y_send)
    kept, sent = call(fold_both_kernel, (shape((M, D), F32), shape((M, D + 2 * HT))), [VMEM] * 3, (r_keep, dv_keep, r_core))
    block = (2, 4 * ROWS + 40, WQ)
    a_keep, a_send, b_keep, b_send = call(
        attend_weights_kernel, (shape(block),) * 4,
        [SMEM] + [VMEM] * 7, (ids, normed_one, after_these(dqkv, sent), gain_one_g, gain_two_g, attn_full, b_two, b_core),
        [pltpu.VMEM((HT, D), F32), pltpu.VMEM((8, D), F32), pltpu.VMEM((HT, WQ), F32)])
    q_sums = (a_keep, to_y(a_send), b_keep, to_x(b_send))
    own, sent = call(input_kernel, (shape((L, 2 * D)), shape((L, 2 * D))), [SMEM] + [VMEM] * 7,
                     (ids, kept, to_z(sent), x_two, gains, grad_after, dv_keep, r_core), [pltpu.VMEM((M, 2 * D), BF16)])
    home = to_h(sent)
    input_grad, v1_out = call(home_kernel, (shape((2, L, D), F32),) * 2, [SMEM] + [VMEM] * 3, (ids, own, home, v1_acc))

    def finish(kernel, sums, rest, *first):
        dims = sums[0].shape[1:]
        a_own, a_send, b_own, b_send = call(sum_first_kernel, (shape(dims),) * 4, [VMEM] * 4, sums)
        b_send = call(sum_second_kernel, shape(dims), [VMEM] * 2, (b_own, to_y(b_send)))
        kept, sent, rows = call(kernel, (shape((2, ROWS, dims[1])), shape((2, ROWS, dims[1])), shape(rest, F32)), [SMEM] + [VMEM] * 3,
                                (ids, a_own, to_x(a_send), after_these(to_h(b_send), *first)), [pltpu.VMEM(dims, F32)])
        first = to_z(sent)
        return (ids, kept, first, to_core(jnp.stack([kept[1], first[1]]))), rows

    u_sums = lax.optimization_barrier(u_sums + (a_send,))[:4]
    q_sums = lax.optimization_barrier(q_sums + (sent,))[:4]
    parts, down_g = finish(sum_hidden_kernel, u_sums, (FROWS, D))
    gate_g, up_g = call(join_hidden_kernel, (shape((ROWS, 4 * FT), F32),) * 2, [SMEM] + [VMEM] * 3, parts,
                        [pltpu.VMEM((4, ROWS, 2 * FT), F32)])
    parts, out_g = finish(sum_qkv_kernel, q_sums, (ROWS, D), home)
    query_g, key_g, value_g, gain_g = call(
        join_qkv_kernel, (shape((ROWS, D), F32),) * 3 + (shape((ROWS, 128), F32),), [SMEM] + [VMEM] * 3, parts)
    return (layer_out, input_grad, v1_out, gain_g[:, 0], query_g, key_g, value_g, out_g, gain_g[:, 1], gate_g, up_g, down_g)


def local(plan, layer_in, *rest):
    kept = plan.G == FAST_G and plan.T == FAST_T and layer_in.shape == (2, FAST_L, D) and rest[12].shape == (FROWS, D)
    return (fast if kept else general)(plan, layer_in, *rest)


def solution(mesh):
    plan = Plan(mesh.shape["gx"], mesh.shape["gy"])
    tokens, rows, vector = P(None, ALL, None), P(ALL, None), P(ALL)
    return jax.shard_map(
        functools.partial(local, plan),
        mesh=mesh,
        in_specs=(tokens, tokens, tokens, tokens, P(), vector, rows, rows, rows, rows, vector, rows, rows, rows),
        out_specs=(tokens, tokens, tokens, vector, rows, rows, rows, rows, vector, rows, rows, rows),
        check_vma=False,
    )
```

```python
import functools

import jax
import jax.numpy as jnp
from jax import lax
from jax.experimental import pallas as pl
from jax.experimental.pallas import tpu as pltpu
from jax.sharding import PartitionSpec as P

H = 16
EPS = 1e-05
NEG = -1e30
SCALE = 0.125
ALL = ("gx", "gy")
F32 = jnp.float32
BF16 = jnp.bfloat16


class Plan:
    def __init__(self, n_gx, n_gy):
        self.G, self.T = n_gx, n_gy // 2
        every = [(g, h, t) for g in range(self.G) for h in range(2) for t in range(self.T)]
        at = lambda g, h, t: g * n_gy + h * self.T + t
        self.g_swap = {k: [(at(g, h, t), at(g ^ k, h, t)) for g, h, t in every] for k in range(1, self.G)}
        self.t_swap = {k: [(at(g, h, t), at(g, h, t ^ k)) for g, h, t in every] for k in range(1, self.T)}
        self.h_swap = [(at(g, h, t), at(g, 1 - h, t)) for g, h, t in every]
        self.bits = []
        bit = self.T // 2
        while bit:
            self.bits.append(bit)
            bit //= 2


def pick(array, index, axis=0):
    return lax.dynamic_index_in_dim(array, index, axis, keepdims=False)


def send(array, pairs):
    return lax.ppermute(array, ALL, pairs)


def dot(a, b):
    return lax.dot_general(a, b, (((1,), (0,)), ((), ())), preferred_element_type=F32)


def dot_rows(a, b):
    return lax.dot_general(a, b, (((0,), (0,)), ((), ())), preferred_element_type=F32)


def dot_cols(a, b):
    return lax.dot_general(a, b, (((1,), (1,)), ((), ())), preferred_element_type=F32)


def rotate(values, cosine, sine):
    half = values.shape[-1] // 2
    a, b = values[..., :half], values[..., half:]
    return jnp.concatenate([a * cosine - b * sine, b * cosine + a * sine], axis=-1)


def general(plan, layer_in, first_layer_value, v1_acc, cotangent, seq_starts, norm1_gain, w_query, w_key, w_value,
          w_out, norm2_gain, w_gate, w_up, w_down):
    G, T, bits = plan.G, plan.T, plan.bits
    micro, L, D = layer_in.shape
    FF = w_gate.shape[1]
    HT, FT, heads = D // T, FF // T, H // T
    HD = D // H
    M = 2 * L
    N = T * M
    rows, frows = w_query.shape[0], w_down.shape[0]
    g, gy = lax.axis_index("gx"), lax.axis_index("gy")
    h, t = gy // T, gy % T

    def to_t(array, bit):
        return send(array, plan.t_swap[bit])

    def to_g(array, k):
        return send(array, plan.g_swap[k]) if k else array

    def to_h(array):
        return send(array, plan.h_swap)

    def inward(array):
        return jnp.concatenate([pick(array, h), to_h(pick(array, 1 - h))], axis=0)

    def outward(array):
        own, other = array[:L], to_h(array[L:])
        return jnp.stack([jnp.where(h == 0, own, other), jnp.where(h == 0, other, own)])

    def gather_t(array):
        parts = {0: array}
        for bit in bits:
            order = sorted(parts)
            moved = to_t(jnp.concatenate([parts[j] for j in order], axis=0), bit)
            size = array.shape[0]
            for i, j in enumerate(order):
                parts[j ^ bit] = moved[i * size:(i + 1) * size]
        return [parts[j] for j in range(T)]

    def reduce_t(partial):
        blocks = partial.reshape((T, -1) + partial.shape[1:])
        for bit in reversed(bits):
            shape = blocks.shape
            split = blocks.reshape((shape[0] // 2, 2) + shape[1:])
            blocks = split[:, 0] + to_t(split[:, 1].astype(BF16), bit).astype(F32)
        return blocks[0]

    def exchange_t(parts):
        held = {j: [parts[j]] for j in range(T)}
        sources = [0]
        for bit in bits:
            out = [j for j in sorted(held) if j & bit]
            flat = [p for j in out for p in held[j]]
            moved = to_t(jnp.stack(flat), bit)
            n = len(sources)
            new = {}
            for i, j in enumerate(out):
                new[j ^ bit] = held[j ^ bit] + [moved[i * n + s] for s in range(n)]
            sources = sources + [s ^ bit for s in sources]
            held = new
        result = [None] * T
        for s, p in zip(sources, held[0]):
            result[s] = p
        return result

    def natural(parts):
        array = jnp.stack(parts)
        for bit in bits:
            split = array.reshape((-1, 2, bit) + array.shape[1:])
            array = jnp.where((t & bit) != 0, split[:, ::-1], split).reshape(array.shape)
        return array

    def gather_r(block):
        other = to_h(block)
        pair = jnp.where(h == 0, jnp.stack([block, other]), jnp.stack([other, block]))
        full = jnp.zeros((G,) + pair.shape, pair.dtype)
        for k in range(G):
            full = lax.dynamic_update_slice(full, to_g(pair, k)[None], (g ^ k,) + (0,) * pair.ndim)
        return full.reshape((G * 2 * block.shape[0],) + block.shape[1:])

    def gather_cols(slices):
        block = natural(exchange_t([pick(slices, t ^ j) for j in range(T)]))
        return gather_r(block.reshape(T * block.shape[1], -1))

    def reduce_r(grad):
        n, w = grad.shape[0] // (2 * G), grad.shape[1]
        grad = grad.astype(BF16).reshape(G, 2 * n, w)
        total = pick(grad, g).astype(F32)
        for k in range(1, G):
            total = total + to_g(pick(grad, g ^ k), k).astype(F32)
        total = total.reshape(2, n, w)
        return pick(total, h) + to_h(pick(total, 1 - h).astype(BF16)).astype(F32)

    def scatter_cols(grad):
        total = reduce_r(grad).reshape(T, rows, -1)
        low = total.astype(BF16)
        return natural(exchange_t([pick(low, t ^ j) for j in range(T)])).astype(F32)

    pad = jnp.zeros((rows, 126), BF16)
    gains_in = jnp.concatenate([norm1_gain[:, None], norm2_gain[:, None], pad], axis=1)

    def col_slices(w):
        return w.reshape(rows, T, HT).transpose(1, 0, 2)

    def hidden_slices(w):
        return w.reshape(rows, 2 * G, T, frows).transpose(2, 0, 1, 3).reshape(T, rows, FT)

    qkv_slices = jnp.concatenate([col_slices(w_query), col_slices(w_key), col_slices(w_value),
                                  jnp.broadcast_to(gains_in[None], (T, rows, 128))], axis=2)
    x_own = inward(layer_in)
    qkv_w = gather_cols(qkv_slices)
    x_all = jnp.concatenate(gather_t(x_own), axis=0)
    v_own = inward(first_layer_value).reshape(M, T, HT).transpose(1, 0, 2)
    v_all = jnp.concatenate(exchange_t([pick(v_own, t ^ j) for j in range(T)]), axis=0)
    gu_w = gather_cols(jnp.concatenate([hidden_slices(w_gate), hidden_slices(w_up)], axis=2))
    down_w = gather_r(w_down)
    c_own = inward(cotangent)
    c_all = jnp.concatenate(gather_t(c_own), axis=0)
    out_w = natural(gather_t(gather_r(w_out))).reshape(T, 2 * G, rows, D).transpose(1, 0, 2, 3).reshape(D, D)
    out_w = out_w.reshape(T, HT, D)

    gains = qkv_w[:, 3 * HT:3 * HT + 2].astype(F32).T
    gain_one, gain_two = gains[0], gains[1]
    query_w, key_w, value_w = qkv_w[:, :HT], qkv_w[:, HT:2 * HT], qkv_w[:, 2 * HT:3 * HT]
    gate_w, up_w = gu_w[:, :FT], gu_w[:, FT:]

    starts = pick(seq_starts, h)
    member = t ^ jnp.arange(T, dtype=jnp.int32)
    half = h ^ jnp.arange(2, dtype=jnp.int32)
    position = ((half[None, :] * T + member[:, None]) * L)[:, :, None] + jnp.arange(L, dtype=jnp.int32)
    position = position.reshape(N) + g * N
    begin = jnp.max(jnp.where(starts[None, :] <= position[:, None], starts[None, :], 0), axis=1)
    rel = (position - begin).astype(F32)
    visible = (begin[:, None] == begin[None, :]) & (position[None, :] <= position[:, None])
    frequency = 10000.0 ** (-(jnp.arange(HD // 2, dtype=F32) * 2.0 / HD))
    angles = rel[:, None] * frequency[None, :]
    cosine, sine = jnp.cos(angles)[:, None, :], jnp.sin(angles)[:, None, :]

    x = x_all.astype(F32)
    rstd_one = lax.rsqrt(jnp.mean(x * x, axis=-1, keepdims=True) + EPS)
    normed_one = (x * rstd_one * gain_one).astype(BF16)
    query = rotate(dot(normed_one, query_w).reshape(N, heads, HD), cosine, sine).astype(BF16)
    key = rotate(dot(normed_one, key_w).reshape(N, heads, HD), cosine, sine).astype(BF16)
    value = (0.5 * dot(normed_one, value_w) + 0.5 * v_all.astype(F32)).astype(BF16).reshape(N, heads, HD)
    scores = jnp.einsum("ihd,jhd->hij", query, key, preferred_element_type=F32) * SCALE
    scores = jnp.where(visible[None], scores, NEG)
    top = jnp.max(scores, axis=-1, keepdims=True)
    probs = jnp.exp(scores - top)
    denom = jnp.sum(probs, axis=-1, keepdims=True)
    probs = probs / denom
    probs_low = probs.astype(BF16)
    attn = jnp.einsum("hij,jhd->ihd", probs_low, value, preferred_element_type=F32)
    attn_low = attn.reshape(N, HT).astype(BF16)
    attn_parts = []
    for j, part in enumerate(gather_t(attn_low)):
        part = part.reshape(T, M, HT)
        attn_parts.append(jnp.concatenate([part[b ^ j] for b in range(T)], axis=0))
    after = x
    for j in range(T):
        after = after + dot(attn_parts[j], pick(out_w, t ^ j))
    rstd_two = lax.rsqrt(jnp.mean(after * after, axis=-1, keepdims=True) + EPS)
    hat_two = after * rstd_two
    normed_two = (hat_two * gain_two).astype(BF16)
    gate = dot(normed_two, gate_w)
    up = dot(normed_two, up_w)
    sig = jax.nn.sigmoid(gate)
    act = gate * sig
    hidden = (act * up).astype(BF16)

    grad_hidden = dot_cols(c_all, down_w)
    grad_gate = (grad_hidden * up * (sig * (1.0 + gate * (1.0 - sig)))).astype(BF16)
    grad_up = (grad_hidden * act).astype(BF16)
    grad_two_part = dot_cols(grad_gate, gate_w) + dot_cols(grad_up, up_w)
    gain_two_grad = jnp.sum(grad_two_part * hat_two, axis=0)
    grad_two = reduce_t(grad_two_part) * gain_two
    hat_own = hat_two[:M]
    grad_after = c_own.astype(F32) + rstd_two[:M] * (
        grad_two - hat_own * jnp.mean(grad_two * hat_own, axis=-1, keepdims=True))
    grad_branch = jnp.concatenate(gather_t(grad_after.astype(BF16)), axis=0)
    result = reduce_t(dot(hidden, down_w)) + after[:M]
    layer_out = outward(result.astype(BF16))
    grad_down = dot_rows(hidden, c_all)
    grad_gu = dot_rows(normed_two, jnp.concatenate([grad_gate, grad_up], axis=1))

    grad_attn = dot_cols(grad_branch, pick(out_w, t)).astype(BF16).reshape(N, heads, HD)
    delta = jnp.sum(grad_attn.astype(F32) * attn, axis=-1).T
    grad_probs = jnp.einsum("ihd,jhd->hij", grad_attn, value, preferred_element_type=F32)
    grad_scores = (probs * (grad_probs - delta[..., None])).astype(BF16)
    grad_query = jnp.einsum("hij,jhd->ihd", grad_scores, key, preferred_element_type=F32) * SCALE
    grad_key = jnp.einsum("hij,ihd->jhd", grad_scores, query, preferred_element_type=F32) * SCALE
    grad_blend = jnp.einsum("hij,ihd->jhd", probs_low, grad_attn, preferred_element_type=F32).reshape(N, HT)
    grad_query = rotate(grad_query, cosine, -sine).reshape(N, HT).astype(BF16)
    grad_key = rotate(grad_key, cosine, -sine).reshape(N, HT).astype(BF16)
    grad_value = (0.5 * grad_blend).astype(BF16)
    grad_one_part = dot_cols(grad_query, query_w) + dot_cols(grad_key, key_w) + dot_cols(grad_value, value_w)
    hat_one = x * rstd_one
    gain_one_grad = jnp.sum(grad_one_part * hat_one, axis=0)
    grad_one = reduce_t(grad_one_part) * gain_one
    hat_own = hat_one[:M]
    input_grad = grad_after + rstd_one[:M] * (
        grad_one - hat_own * jnp.mean(grad_one * hat_own, axis=-1, keepdims=True))
    input_grad = outward(input_grad.astype(BF16)).astype(F32)
    v_parts = natural(exchange_t([grad_value[j * M:(j + 1) * M] for j in range(T)]))
    v1_out = v1_acc + outward(v_parts.transpose(1, 0, 2).reshape(M, D)).astype(F32)

    attn_full = natural([p.T for p in attn_parts]).reshape(2 * G, T, rows, N)
    grad_out = dot(pick(attn_full, t, 1).reshape(2 * G * rows, N), grad_branch)
    grad_gains = jnp.stack([gain_one_grad, gain_two_grad], axis=1)
    grad_gains = jnp.concatenate([grad_gains, jnp.zeros((D, 126), F32)], axis=1)
    grad_qkv = dot_rows(normed_one, jnp.concatenate([grad_query, grad_key, grad_value], axis=1))
    down_g = reduce_r(grad_down)
    gu_g = scatter_cols(grad_gu)
    out_g = reduce_r(grad_out)
    qkv_g = scatter_cols(jnp.concatenate([grad_qkv, grad_gains], axis=1))

    def col_join(parts):
        return parts.transpose(1, 0, 2).reshape(rows, D)

    def hidden_join(parts):
        return parts.reshape(T, rows, 2 * G, frows).transpose(1, 2, 0, 3).reshape(rows, FF)

    gain_g = jnp.sum(qkv_g[:, :, 3 * HT:3 * HT + 2], axis=0)
    return (layer_out, input_grad, v1_out, gain_g[:, 0], col_join(qkv_g[:, :, :HT]), col_join(qkv_g[:, :, HT:2 * HT]),
            col_join(qkv_g[:, :, 2 * HT:3 * HT]), out_g, gain_g[:, 1], hidden_join(gu_g[:, :, :FT]),
            hidden_join(gu_g[:, :, FT:]), down_g)


FAST_G, FAST_T, FAST_L, D, HT, FT, FROWS, ROWS = 4, 4, 64, 1024, 256, 704, 88, 32
M, N = 2 * FAST_L, 8 * FAST_L
HALF = N // 2
WQ = 3 * HT + 128
ORDER = (0, 2, 1, 3)
HD = 64
ARRIVED = ((0, 0), (1, 0), (2, 0), (3, 0), (0, 1), (2, 1), (1, 1), (3, 1))
LEAVING = {(0, 0): (0, 0), (1, 0): (0, 1), (2, 0): (1, 0), (3, 0): (1, 1), (0, 1): (2, 0), (2, 1): (2, 1), (1, 1): (3, 0), (3, 1): (3, 1)}
VMEM = pl.BlockSpec(memory_space=pltpu.VMEM)
SMEM = pl.BlockSpec(memory_space=pltpu.SMEM)
ANY = pl.BlockSpec(memory_space=pltpu.HBM)


def shape(dims, dtype=BF16):
    return jax.ShapeDtypeStruct(dims, dtype)


def call(kernel, outs, specs, args, scratch=(), mib=40):
    return pl.pallas_call(
        kernel,
        out_shape=outs,
        in_specs=specs,
        out_specs=jax.tree.map(lambda _: VMEM, outs),
        scratch_shapes=list(scratch),
        compiler_params=pltpu.CompilerParams(vmem_limit_bytes=mib << 20),
        cost_estimate=pl.CostEstimate(flops=1, bytes_accessed=1, transcendentals=0),
    )(*args)


def aligned(index, size):
    return pl.ds(pl.multiple_of(index * size, size), size)


def eye(rows, lanes):
    return (lax.broadcasted_iota(jnp.int32, (rows, lanes), 0) == lax.broadcasted_iota(jnp.int32, (rows, lanes), 1)).astype(BF16)


def tiles_in(block):
    lines = [jnp.concatenate([block[j * 8:j * 8 + 8, i * 128:i * 128 + 128] for j in range(11)], axis=1) for i in range(8)]
    return jnp.concatenate(lines, axis=0)


def tiles_out(block):
    lines = [jnp.concatenate([block[i * 8:i * 8 + 8, j * 128:j * 128 + 128] for i in range(8)], axis=1) for j in range(11)]
    return jnp.concatenate(lines, axis=0)


def line_tiles_in(block):
    tiles = [block[j * 8:j * 8 + 8, i * 128:i * 128 + 128] for j in range(4) for i in range(8)]
    tiles += [jnp.zeros_like(tiles[0])] * 3
    return jnp.concatenate([jnp.concatenate(tiles[n * 7:n * 7 + 7], axis=1) for n in range(5)], axis=0)


def line_tiles_out(block):
    tiles = [block[n * 8:n * 8 + 8, i * 128:i * 128 + 128] for n in range(5) for i in range(7)]
    return jnp.concatenate([jnp.concatenate(tiles[j * 8:j * 8 + 8], axis=1) for j in range(4)], axis=0)


def pack_first(ids, gain_one, gain_two, wq, wk, wv, wo, x, v, c, out, keep, lines, xv_out, c_out, rows, whole, sem):
    h, t = ids[1], ids[2]
    copies = []
    for j in (2, 3, 0, 1):
        to = keep if j < 2 else out
        for i, w in enumerate((wq, wk, wv)):
            copies.append((w.at[:, aligned(t ^ j, HT)], to.at[j % 2, :, i * HT:(i + 1) * HT]))
    copies += [(wo, whole), (x.at[1 - h], xv_out.at[:, :D]), (v.at[1 - h], xv_out.at[:, D:]), (c.at[1 - h], c_out)]
    started = fetch(copies, sem)
    rows[...] = jnp.zeros_like(rows)
    rows[0:1] = gain_one[...].astype(F32)
    rows[1:2] = gain_two[...].astype(F32)
    gains = dot_rows(rows[...].astype(BF16), eye(8, 128)).astype(BF16)
    for j in range(4):
        (keep if j < 2 else out)[j % 2, :, 3 * HT:] = gains
    started[12].wait()
    lines[...] = line_tiles_in(whole[...].astype(F32)).astype(BF16)
    for n, copy in enumerate(started):
        if n != 12:
            copy.wait()


def pack_hidden(ids, wg, wu, wd, keep, out, down, nat, gate, up, whole, sem):
    t = ids[2]
    started = fetch([(wg, gate), (wu, up), (wd, whole)], sem)
    for a, w in enumerate((gate, up)):
        started[a].wait()
        for m in range(4):
            for i in range(8):
                at, to = (i * 4 + m) * FROWS, a * FT + i * FROWS
                nat[m, :, to:to + FROWS] = w[:, at:at + FROWS].astype(F32)
    for j in range(4):
        to = keep if j < 2 else out
        to[j % 2] = nat[t ^ j].astype(BF16)
    started[2].wait()
    down[...] = tiles_in(whole[...].astype(F32)).astype(BF16)


def pack_block(kept, first, last, tail, out, sem):
    width = ROWS
    parts = (kept.at[0], first.at[0], last.at[0], last.at[1], tail)
    started = fetch([(part, out.at[i * width:i * width + part.shape[0]]) for i, part in enumerate(parts)], sem)
    for copy in started:
        copy.wait()


def pack_pair(kept, first, out, sem):
    started = fetch([(kept.at[1], out.at[0]), (first.at[1], out.at[1])], sem)
    for copy in started:
        copy.wait()


def pack_out(b0, b1, b2, b3, out, raw, sem):
    started = fetch([((b0, b1, b2, b3)[n // 2].at[n % 2, 4 * ROWS:], raw.at[n]) for n in range(8)], sem)
    for n in range(8):
        started[n].wait()
        out[n * ROWS:(n + 1) * ROWS] = line_tiles_out(raw[n].astype(F32)).astype(BF16)


def pack_second(ids, x, v, moved, xv_out, v_keep, own, sem):
    h, t = ids[1], ids[2]
    started = fetch([(x.at[h], xv_out.at[:FAST_L, :D]), (v.at[h], own.at[:FAST_L]),
                     (moved.at[:, :D], xv_out.at[FAST_L:, :D]), (moved.at[:, D:], own.at[FAST_L:])], sem)
    for copy in started:
        copy.wait()
    for j in range(2):
        v_keep[j] = own[:, aligned(t ^ j, HT)]
        xv_out[:, D + j * HT:D + (j + 1) * HT] = own[:, aligned(t ^ (j + 2), HT)]


def pack_third(mine, moved, v_keep, out, v_two):
    out[:M, :D] = mine[:, :D]
    out[M:, :D] = moved[:, :D]
    out[:M, D:] = v_keep[1]
    out[M:, D:] = moved[:, D + HT:]
    v_two[:M] = v_keep[0]
    v_two[M:] = moved[:, D:D + HT]


def fetch(copies, sem):
    started = []
    for i, (source, target) in enumerate(copies):
        copy = pltpu.make_async_copy(source, target, sem.at[i])
        copy.start()
        started.append(copy)
    return started


def swap_halves(u):
    width = u.shape[-1]
    lane = lax.broadcasted_iota(jnp.int32, u.shape, 1)
    up = pltpu.roll(u, width - HD // 2, 1)
    down = pltpu.roll(u, HD // 2, 1)
    return jnp.where(lane % HD < HD // 2, up, down)


def scale_of(x):
    return lax.rsqrt(jnp.mean(x * x, axis=-1, keepdims=True) + EPS)


def attend_kernel(ids, x2, xc, v2, cs, sn, bias, b0, b1, b2, b3, w, normed, qkv, attn, low, lse, gains, sem):
    g, h, t = ids[0], ids[1], ids[2]
    copies = []
    for n, (k, dh) in enumerate(ARRIVED):
        b = (b0, b1, b2, b3)[n // 2]
        for i, s in enumerate(ORDER):
            row = ((g ^ k) * 2 + (h ^ dh)) * 4 + (t ^ s)
            copies.append((b.at[n % 2, i * ROWS:(i + 1) * ROWS], w.at[aligned(row, ROWS)]))
    for copy in fetch(copies, sem):
        copy.wait()
    gains[...] = dot_cols(eye(8, 128), w[:, 3 * HT:])
    gain = gains[0:1, :]
    for b in range(2):
        rows = slice(b * HALF, (b + 1) * HALF)
        source = x2 if b == 0 else xc
        x = source[:, :D].astype(F32)
        r = (x * scale_of(x) * gain).astype(BF16)
        normed[rows] = r
        out = dot(r, w[:, :3 * HT])
        for i in range(2):
            u = out[:, i * HT:(i + 1) * HT]
            qkv[rows, i * HT:(i + 1) * HT] = (u * cs[rows] + swap_halves(u) * sn[rows]).astype(BF16)
        value = v2[...] if b == 0 else xc[:, D:]
        qkv[rows, 2 * HT:] = (0.5 * out[:, 2 * HT:] + 0.5 * value.astype(F32)).astype(BF16)
    for b in range(2):
        rows = slice(b * HALF, (b + 1) * HALF)
        outs, tops = [], []
        for i in range(4):
            lanes = slice(i * HD, (i + 1) * HD)
            q = qkv[rows, lanes]
            k = qkv[:, HT + i * HD:HT + (i + 1) * HD]
            v = qkv[:, 2 * HT + i * HD:2 * HT + (i + 1) * HD]
            s = dot_cols(q, k) * SCALE + bias[rows]
            top = jnp.max(s, axis=-1, keepdims=True)
            p = jnp.exp(s - top)
            total = jnp.sum(p, axis=-1, keepdims=True)
            outs.append(dot(p.astype(BF16), v) / total)
            tops.append(top + jnp.log(total))
        o = jnp.concatenate(outs, axis=1)
        attn[rows] = o
        low[rows] = o.astype(BF16)
        lse[rows] = jnp.concatenate(tops, axis=1)


def after_kernel(ids, x2, xc, o2, oc, gains, co2, coc, full, after, normed, own_w, w, sem):
    g, h, t = ids[0], ids[1], ids[2]
    copies = []
    for i, s in enumerate(ORDER):
        source = co2 if i < 2 else coc
        for n, (k, dh) in enumerate(ARRIVED):
            row = ((g ^ k) * 2 + (h ^ dh)) * 4 + (t ^ s)
            at = (i % 2) * HT + n * ROWS
            copies.append((source.at[at:at + ROWS], w.at[aligned(row, ROWS)]))
    started = fetch(copies, sem)
    for i, s in enumerate(ORDER):
        source = o2 if i < 2 else oc
        for p in range(4):
            q = ORDER.index(ORDER[p] ^ s)
            full[p * M:(p + 1) * M, aligned(t ^ s, HT)] = source[(i % 2) * N + q * M:(i % 2) * N + (q + 1) * M]
    for copy in started:
        copy.wait()
    own_w[...] = w[aligned(t, HT)]
    gain = gains[1:2, :]
    for b in range(2):
        rows = slice(b * HALF, (b + 1) * HALF)
        source = x2 if b == 0 else xc
        a = source[:, :D].astype(F32) + dot(full[rows], w[...])
        after[rows] = a
        normed[rows] = (a * scale_of(a) * gain).astype(BF16)


def feed_kernel(ids, normed, after, c2, cc, u0, u1, u2, u3,
                hidden, dgu, out_keep, out_send, r_keep, r_send, gain_g, c_all, w, wd, wide, raw, sem, sem_d):
    g, h, t = ids[0], ids[1], ids[2]
    copies, copies_d = [], []
    for n, (k, dh) in enumerate(ARRIVED):
        b = (u0, u1, u2, u3)[n // 2]
        for i, s in enumerate(ORDER):
            row = ((g ^ k) * 2 + (h ^ dh)) * 4 + (t ^ s)
            copies.append((b.at[n % 2, i * ROWS:(i + 1) * ROWS], w.at[aligned(row, ROWS)]))
        copies_d.append((b.at[n % 2, 4 * ROWS:], raw.at[n]))
    started, started_d = fetch(copies, sem), fetch(copies_d, sem_d)
    for p in range(4):
        c_all[p * M:(p + 1) * M] = (c2 if p < 2 else cc)[(p % 2) * M:(p % 2 + 1) * M]
    for copy in started_d:
        copy.wait()
    for n, (k, dh) in enumerate(ARRIVED):
        wide[aligned((g ^ k) * 2 + (h ^ dh), FROWS)] = tiles_out(raw[n].astype(F32))
    wd[...] = wide[...].astype(BF16)
    for copy in started:
        copy.wait()
    gain_sum = jnp.zeros((1, D), F32)
    for b in range(2):
        rows = slice(b * HALF, (b + 1) * HALF)
        gu = dot(normed[rows], w[...])
        gate, up = gu[:, :FT], gu[:, FT:]
        sig = 1.0 / (1.0 + jnp.exp(-gate))
        act = gate * sig
        hid = (act * up).astype(BF16)
        hidden[rows] = hid
        dh = dot_cols(c_all[rows], wd[...])
        dgate = (dh * up * (sig * (1.0 + gate * (1.0 - sig)))).astype(BF16)
        dup = (dh * act).astype(BF16)
        dgu[rows, :FT] = dgate
        dgu[rows, FT:] = dup
        dr = dot_cols(dgu[rows], w[...])
        out = dot(hid, wd[...])
        a = after[rows]
        gain_sum = gain_sum + jnp.sum(dr * (a * scale_of(a)), axis=0, keepdims=True)
        if b == 0:
            r_keep[...] = dr
            out_keep[...] = out
        else:
            r_send[...] = dr.astype(BF16)
            out_send[...] = out.astype(BF16)
    gain_g[...] = gain_sum


def feed_weights_kernel(ids, normed, dgu, hidden, c_all, a_keep, a_send, b_keep, b_send, gu, full):
    g, h = ids[0], ids[1]
    full[...] = dot_rows(hidden[...], c_all[...])
    for k in range(4):
        gu[...] = dot_rows(normed[:, aligned(g ^ k, HT)], dgu[...])
        for e in range(2):
            target, at = LEAVING[(k, e)]
            target = (a_keep, a_send, b_keep, b_send)[target]
            target[at, :4 * ROWS] = gu[aligned(h ^ e, 4 * ROWS)].astype(BF16)
            target[at, 4 * ROWS:] = tiles_in(full[aligned((g ^ k) * 2 + (h ^ e), FROWS)]).astype(BF16)


def fold_kernel(keep, moved, kept, send):
    kept[...] = keep[:M] + moved[:M].astype(F32)
    send[...] = (keep[M:] + moved[M:].astype(F32)).astype(BF16)


def fold_both_kernel(keep, dv, moved, kept, send):
    kept[...] = keep[:M] + moved[:M, :D].astype(F32)
    send[:, :D] = (keep[M:] + moved[M:, :D].astype(F32)).astype(BF16)
    send[:, D:D + HT] = dv[M:]
    send[:, D + HT:] = moved[M:, D:]


def branch_kernel(keep, moved, after, gains, c2, grad_after, low):
    a = after[:M]
    scale = scale_of(a)
    hat = a * scale
    dy = (keep[...] + moved[...].astype(F32)) * gains[1:2, :]
    d = c2[:M].astype(F32) + scale * (dy - hat * jnp.mean(dy * hat, axis=-1, keepdims=True))
    grad_after[...] = d
    low[...] = d.astype(BF16)


def attend_back_kernel(ids, da2, dac, wo, qkv, attn, lse, bias, cs, sn, w, x2, xc,
                       dqkv, r_keep, r_send, gain_g, do, dk, dv):
    for b in range(2):
        rows = slice(b * HALF, (b + 1) * HALF)
        do[rows] = dot_cols((da2 if b == 0 else dac)[...], wo[...]).astype(BF16)
    for b in range(2):
        rows = slice(b * HALF, (b + 1) * HALF)
        dqs = []
        for i in range(4):
            lanes = slice(i * HD, (i + 1) * HD)
            q = qkv[rows, lanes]
            k = qkv[:, HT + i * HD:HT + (i + 1) * HD]
            v = qkv[:, 2 * HT + i * HD:2 * HT + (i + 1) * HD]
            d = do[rows, lanes]
            delta = jnp.sum(d.astype(F32) * attn[rows, lanes], axis=-1, keepdims=True)
            p = jnp.exp(dot_cols(q, k) * SCALE + bias[rows] - lse[rows, i:i + 1])
            ds = (p * (dot_cols(d, v) - delta)).astype(BF16)
            dqs.append(dot(ds, k))
            dki, dvi = dot_rows(ds, q), dot_rows(p.astype(BF16), d)
            if b == 0:
                dk[:, lanes], dv[:, lanes] = dki, dvi
            else:
                dk[:, lanes], dv[:, lanes] = dk[:, lanes] + dki, dv[:, lanes] + dvi
        u = jnp.concatenate(dqs, axis=1) * SCALE
        dqkv[rows, :HT] = (u * cs[rows] - swap_halves(u) * sn[rows]).astype(BF16)
    gain_sum = jnp.zeros((1, D), F32)
    for b in range(2):
        rows = slice(b * HALF, (b + 1) * HALF)
        u = dk[rows] * SCALE
        dqkv[rows, HT:2 * HT] = (u * cs[rows] - swap_halves(u) * sn[rows]).astype(BF16)
        dqkv[rows, 2 * HT:] = (0.5 * dv[rows]).astype(BF16)
        dr = dot_cols(dqkv[rows], w[:, :3 * HT])
        x = (x2 if b == 0 else xc)[:, :D].astype(F32)
        gain_sum = gain_sum + jnp.sum(dr * (x * scale_of(x)), axis=0, keepdims=True)
        if b == 0:
            r_keep[...] = dr
        else:
            r_send[:, :D] = dr.astype(BF16)
            r_send[:, D:] = dqkv[rows, 2 * HT:]
    gain_g[...] = gain_sum


def attend_weights_kernel(ids, normed, dqkv, gain_one, gain_two, full, da2, dac, a_keep, a_send, b_keep, b_send,
                          scratch, rows_g, qkv):
    g, h, t = ids[0], ids[1], ids[2]
    rows_g[...] = jnp.zeros_like(rows_g)
    rows_g[0:1] = gain_one[...]
    rows_g[1:2] = gain_two[...]
    for k in range(4):
        lanes = aligned(g ^ k, HT)
        qkv[:, :3 * HT] = dot_rows(normed[:, lanes], dqkv[...])
        qkv[:, 3 * HT:] = dot_rows(rows_g[:, lanes].astype(BF16), eye(8, 128))
        scratch[...] = dot_rows(full[:HALF, lanes], da2[...]) + dot_rows(full[HALF:, lanes], dac[...])
        for e in range(2):
            target, at = LEAVING[(k, e)]
            target = (a_keep, a_send, b_keep, b_send)[target]
            target[at, :4 * ROWS] = qkv[aligned(h ^ e, 4 * ROWS)].astype(BF16)
            target[at, 4 * ROWS:] = line_tiles_in(scratch[aligned((h ^ e) * 4 + t, ROWS)]).astype(BF16)


def sum_first_kernel(a_keep, a_moved, b_keep, b_moved, a_own, a_send, b_own, b_send):
    for keep, moved, own, out in ((a_keep, a_moved, a_own, a_send), (b_keep, b_moved, b_own, b_send)):
        own[...] = (keep[0].astype(F32) + moved[0].astype(F32)).astype(BF16)
        out[...] = (keep[1].astype(F32) + moved[1].astype(F32)).astype(BF16)


def sum_second_kernel(b_own, b_moved, b_send):
    b_send[...] = (b_own[...].astype(F32) + b_moved[...].astype(F32)).astype(BF16)


def sum_third(a_own, a_moved, moved, total):
    total[...] = (a_own[...].astype(F32) + a_moved[...].astype(F32)) + moved[...].astype(F32)


def sum_hidden_kernel(ids, a_own, a_moved, moved, kept, send, down, total):
    t = ids[2]
    sum_third(a_own, a_moved, moved, total)
    for j in range(4):
        (kept if j < 2 else send)[j % 2] = total[aligned(t ^ j, ROWS)].astype(BF16)
    down[...] = tiles_out(total[4 * ROWS:])


def sum_qkv_kernel(ids, a_own, a_moved, moved, kept, send, out, total):
    t = ids[2]
    sum_third(a_own, a_moved, moved, total)
    for j in range(4):
        (kept if j < 2 else send)[j % 2] = total[aligned(t ^ j, ROWS)].astype(BF16)
    out[...] = line_tiles_out(total[4 * ROWS:])


def join_qkv_kernel(ids, kept, first, last, q, k, v, gains):
    t = ids[2]
    parts = (kept[0], first[0], last[0], last[1])
    for s, part in zip(ORDER, parts):
        for i, ref in enumerate((q, k, v)):
            ref[:, aligned(t ^ s, HT)] = part[:, i * HT:(i + 1) * HT].astype(F32)
    low = [part[:, 3 * HT:].astype(F32) for part in parts]
    gains[...] = (low[0] + low[1]) + (low[2] + low[3])


def join_hidden_kernel(ids, kept, first, last, gate, up, nat):
    t = ids[2]
    for s, part in zip(ORDER, (kept[0], first[0], last[0], last[1])):
        nat[t ^ s] = part.astype(F32)
    for m in range(4):
        for a, ref in enumerate((gate, up)):
            for i in range(8):
                to, at = (i * 4 + m) * FROWS, a * FT + i * FROWS
                ref[:, to:to + FROWS] = nat[m, :, at:at + FROWS]


def input_kernel(ids, keep, moved, x2, gains, grad_after, dv, dv_core, own, send, both):
    t = ids[2]
    x = x2[:M, :D].astype(F32)
    scale = scale_of(x)
    hat = x * scale
    dy = (keep[...] + moved[:, :D].astype(F32)) * gains[0:1, :]
    both[:, :D] = (grad_after[...] + scale * (dy - hat * jnp.mean(dy * hat, axis=-1, keepdims=True))).astype(BF16)
    parts = (dv[:M], moved[:, D:D + HT], dv_core[:M, D:], moved[:, D + HT:])
    for s, part in zip(ORDER, parts):
        both[:, aligned(4 + (t ^ s), HT)] = part
    own[...] = both[:FAST_L]
    send[...] = both[FAST_L:]


def home_kernel(ids, own, moved, v1, grad, v_out):
    h = ids[1]
    grad[h] = own[:, :D].astype(F32)
    grad[1 - h] = moved[:, :D].astype(F32)
    v_out[h] = v1[h] + own[:, D:].astype(F32)
    v_out[1 - h] = v1[1 - h] + moved[:, D:].astype(F32)


def result_kernel(keep, moved, after, own, send):
    out = after[:M] + (keep[...] + moved[...].astype(F32))
    own[...] = out[:FAST_L].astype(BF16)
    send[...] = out[FAST_L:].astype(BF16)


def result_home_kernel(ids, own, moved, out):
    h = ids[1]
    out[h] = own[...]
    out[1 - h] = moved[...]


def fast(plan, layer_in, first_layer_value, v1_acc, cotangent, seq_starts, norm1_gain, w_query, w_key, w_value,
         w_out, norm2_gain, w_gate, w_up, w_down):
    L = FAST_L
    g, gy = lax.axis_index("gx"), lax.axis_index("gy")
    h, t = gy // 4, gy % 4
    ids = jnp.stack([g, h, t]).astype(jnp.int32)

    def to_z(array):
        return send(array, plan.t_swap[2])

    def to_core(array):
        return send(array, plan.t_swap[1])

    def to_h(array):
        return send(array, plan.h_swap)

    def to_x(array):
        return send(array, plan.g_swap[1])

    def to_y(array):
        return send(array, plan.g_swap[2])

    def after_these(array, *others):
        return lax.optimization_barrier((array,) + others)[0]

    def fenced(part, *inputs):
        results = jax.eval_shape(part, *inputs)
        nothing = lambda *_: jax.tree.map(lambda a: jnp.zeros(a.shape, a.dtype), results)
        return lax.cond(ids[0] >= 0, part, nothing, *inputs)

    def spread(own, other, *first):
        a_pair = jnp.stack([own, to_x(own)])
        b_pair = jnp.stack([other, to_y(other)])
        a_pair, b_pair = lax.optimization_barrier((a_pair, b_pair) + first)[:2]
        return a_pair, to_y(a_pair), b_pair, to_x(b_pair)

    def pair_of(kept, first):
        return call(pack_pair, shape(kept.shape), [ANY] * 2, (kept, first), [pltpu.SemaphoreType.DMA((2,))])

    def block_of(kept, first, last, tail):
        return call(pack_block, shape((4 * ROWS + tail.shape[0], tail.shape[1])), [ANY] * 4, (kept, first, last, tail),
                    [pltpu.SemaphoreType.DMA((5,))])

    q_send, q_keep, o_block, xv_send, c_send = call(
        pack_first, (shape((2, ROWS, WQ)), shape((2, ROWS, WQ)), shape((40, WQ)), shape((L, 2 * D)), shape((L, D))),
        [SMEM] + [VMEM] * 2 + [ANY] * 7,
        (ids, norm1_gain[None], norm2_gain[None], w_query, w_key, w_value, w_out, layer_in, first_layer_value, cotangent),
        [pltpu.VMEM((8, ROWS), F32), pltpu.VMEM((ROWS, D), BF16), pltpu.SemaphoreType.DMA((16,))], mib=63)
    q_first = to_z(q_send)
    xv_moved = to_h(xv_send)
    q_last = to_core(pair_of(q_keep, q_first))
    q_block = block_of(q_keep, q_first, q_last, o_block)
    q_other = to_h(q_block)

    starts = pick(after_these(seq_starts, q_block), h)
    member = t ^ jnp.array(ORDER, jnp.int32)
    half = h ^ jnp.arange(2, dtype=jnp.int32)
    position = ((half[None, :] * 4 + member[:, None]) * L)[:, :, None] + jnp.arange(L, dtype=jnp.int32)
    position = position.reshape(N) + g * N
    begin = jnp.max(jnp.where(starts[None, :] <= position[:, None], starts[None, :], 0), axis=1)
    visible = (begin[:, None] == begin[None, :]) & (position[None, :] <= position[:, None])
    bias = jnp.where(visible, 0.0, NEG).astype(F32)
    lane = jnp.arange(HT, dtype=jnp.int32)
    frequency = 10000.0 ** (-((lane % (HD // 2)).astype(F32) * 2.0 / HD))
    angles = (position - begin).astype(F32)[:, None] * frequency[None, :]
    cs = jnp.cos(angles)
    sn = jnp.sin(angles) * jnp.where(lane % HD < HD // 2, -1.0, 1.0)[None, :]

    xv_out, v_keep = call(pack_second, (shape((M, D + 2 * HT)), shape((2, M, HT))), [SMEM] + [ANY] * 3,
                          (ids, layer_in, first_layer_value, xv_moved), [pltpu.VMEM((M, D), BF16), pltpu.SemaphoreType.DMA((4,))], mib=63)
    x_two, v_two = call(pack_third, (shape((HALF, D + HT)), shape((HALF, HT))), [VMEM] * 3, (xv_out, to_z(xv_out), v_keep))
    x_core = to_core(x_two)
    q_other, cs, sn, bias, _ = lax.optimization_barrier((q_other, cs, sn, bias, xv_out))
    q_parts = spread(q_block, q_other, x_two)

    u_keep, u_send, d_block = call(
        pack_hidden, (shape((2, ROWS, 2 * FT)), shape((2, ROWS, 2 * FT)), shape((2 * ROWS, 2 * FT))), [SMEM] + [ANY] * 3,
        (after_these(ids, q_send), w_gate, w_up, w_down),
        [pltpu.VMEM((4, ROWS, 2 * FT), F32), pltpu.VMEM((ROWS, 4 * FT), BF16), pltpu.VMEM((ROWS, 4 * FT), BF16), pltpu.VMEM((FROWS, D), BF16),
         pltpu.SemaphoreType.DMA((3,))], mib=63)
    u_first = to_z(u_send)
    u_last = to_core(pair_of(u_keep, after_these(u_first, q_block)))
    u_block = block_of(u_keep, u_first, u_last, d_block)
    u_other = to_h(after_these(u_block, q_block))
    c_moved = to_h(after_these(c_send, u_other))
    u_a = jnp.stack([u_block, to_x(after_these(u_block, q_parts[2]))])
    u_b = jnp.stack([u_other, to_y(u_other)])
    o_own = call(pack_out, shape((HT, D)), [ANY] * 4, q_parts, [pltpu.VMEM((8, 40, WQ), BF16), pltpu.SemaphoreType.DMA((8,))])
    o_first = to_z(o_own)
    c_own = jnp.concatenate([pick(cotangent, h), after_these(c_moved, o_own)], axis=0)
    q_parts = lax.optimization_barrier(q_parts + (u_a, u_b, c_own))[:4]
    c_two = jnp.concatenate([c_own, to_z(c_own)], axis=0)
    c_core = to_core(c_two)
    qkv_w, normed_one, qkv, attn, attn_low, lse, gains = call(
        attend_kernel,
        (shape((D, WQ)), shape((N, D)), shape((N, 3 * HT)), shape((N, HT), F32), shape((N, HT)), shape((N, 4), F32), shape((8, D), F32)),
        [SMEM] + [VMEM] * 6 + [ANY] * 4, (ids, x_two, x_core, v_two, cs, sn, bias, *q_parts),
        [pltpu.SemaphoreType.DMA((32,))])
    a_two = jnp.concatenate([attn_low, to_z(after_these(attn_low, c_two))], axis=0)
    a_core = to_core(after_these(a_two, c_core))
    o_two = jnp.concatenate([o_own, o_first], axis=0)
    o_core = to_core(after_these(o_two, attn_low))
    u_parts = (u_a, to_y(u_a), u_b, to_x(u_b))
    a_core = to_core(a_two)
    attn_full, after, normed_two, out_w = call(
        after_kernel, (shape((N, D)), shape((N, D), F32), shape((N, D)), shape((HT, D))),
        [SMEM] + [VMEM] * 5 + [ANY] * 2, (ids, x_two, x_core, a_two, a_core, gains, o_two, o_core),
        [pltpu.VMEM((D, D), BF16), pltpu.SemaphoreType.DMA((32,))])
    hidden, dgu, out_keep, out_send, r_keep, r_send, gain_two_g, c_all = call(
        feed_kernel,
        (shape((N, FT)), shape((N, 2 * FT)), shape((HALF, D), F32), shape((HALF, D)), shape((HALF, D), F32), shape((HALF, D)),
         shape((1, D), F32), shape((N, D))),
        [SMEM] + [VMEM] * 4 + [ANY] * 4, (ids, normed_two, after, c_two, c_core, *u_parts),
        [pltpu.VMEM((D, 2 * FT), BF16), pltpu.VMEM((8 * FROWS, D), BF16), pltpu.VMEM((8 * FROWS, D), F32), pltpu.VMEM((8, 2 * ROWS, 2 * FT), BF16),
         pltpu.SemaphoreType.DMA((32,)), pltpu.SemaphoreType.DMA((8,))])

    r_core = to_core(r_send)
    block = (2, 6 * ROWS, 2 * FT)
    a_keep, a_send, b_keep, b_send = call(
        feed_weights_kernel, (shape(block),) * 4, [SMEM] + [VMEM] * 4, (ids, normed_two, dgu, hidden, c_all),
        [pltpu.VMEM((HT, 2 * FT), F32), pltpu.VMEM((8 * FROWS, D), F32)])
    u_sums = (a_keep, to_y(a_send), b_keep, to_x(b_send))

    def middle(r_keep, r_core, after, gains, c_two):
        kept, sent = call(fold_kernel, (shape((M, D), F32), shape((M, D))), [VMEM] * 2, (r_keep, r_core))
        grad_after, branch = call(branch_kernel, (shape((M, D), F32), shape((M, D))), [VMEM] * 5, (kept, to_z(sent), after, gains, c_two))
        b_two = jnp.concatenate([branch, to_z(branch)], axis=0)
        return grad_after, b_two, to_core(b_two)

    grad_after, b_two, b_core = fenced(middle, r_keep, after_these(r_core, a_send), after, gains, c_two)

    def second_sum(a_own, a_send, b_own, b_send):
        return a_own, a_send, call(sum_second_kernel, shape(b_own.shape), [VMEM] * 2, (b_own, to_y(b_send)))

    def first_sum(sums):
        return call(sum_first_kernel, (shape(sums[0].shape[1:]),) * 4, [VMEM] * 4, sums)

    u_sums = first_sum(lax.optimization_barrier(u_sums + (b_core,))[:4])
    b_core = after_these(b_core, u_sums[3])
    def attend_back(*inputs):
        return tuple(call(
            attend_back_kernel,
            (shape((N, 3 * HT)), shape((HALF, D), F32), shape((HALF, D + HT)), shape((1, D), F32)),
            [SMEM] + [VMEM] * 12, (ids,) + inputs,
            [pltpu.VMEM((N, HT), BF16), pltpu.VMEM((N, HT), F32), pltpu.VMEM((N, HT), F32)], mib=60))

    dqkv, r_keep, r_send, gain_one_g = fenced(attend_back, b_two, b_core, out_w, qkv, attn, lse, bias, cs, sn, qkv_w, x_two, x_core)
    u_sums = second_sum(*u_sums)
    r_send = after_these(r_send, u_sums[2])
    o_kept, o_sent = call(fold_kernel, (shape((M, D), F32), shape((M, D))), [VMEM] * 2,
                          (out_keep, to_core(after_these(out_send, b_two))))
    y_own, y_send = call(result_kernel, (shape((L, D)), shape((L, D))), [VMEM] * 3, (o_kept, to_z(o_sent), after))
    layer_out = call(result_home_kernel, shape((2, L, D)), [SMEM] + [VMEM] * 2, (ids, y_own, to_h(y_send)))
    dv_keep = dqkv[:HALF, 2 * HT:]
    r_core = to_core(r_send)
    kept, sent = call(fold_both_kernel, (shape((M, D), F32), shape((M, D + 2 * HT))), [VMEM] * 3, (r_keep, dv_keep, r_core))
    block = (2, 4 * ROWS + 40, WQ)
    a_keep, a_send, b_keep, b_send = call(
        attend_weights_kernel, (shape(block),) * 4,
        [SMEM] + [VMEM] * 7, (ids, normed_one, after_these(dqkv, sent), gain_one_g, gain_two_g, attn_full, b_two, b_core),
        [pltpu.VMEM((HT, D), F32), pltpu.VMEM((8, D), F32), pltpu.VMEM((HT, WQ), F32)])
    q_sums = (a_keep, to_y(a_send), b_keep, to_x(b_send))
    own, sent = call(input_kernel, (shape((L, 2 * D)), shape((L, 2 * D))), [SMEM] + [VMEM] * 7,
                     (ids, kept, to_z(sent), x_two, gains, grad_after, dv_keep, r_core), [pltpu.VMEM((M, 2 * D), BF16)])
    home = to_h(sent)
    input_grad, v1_out = call(home_kernel, (shape((2, L, D), F32),) * 2, [SMEM] + [VMEM] * 3, (ids, own, home, v1_acc))

    def finish(kernel, sums, rest, *first):
        a_own, a_send, b_send = sums
        dims = a_own.shape
        kept, sent, rows = call(kernel, (shape((2, ROWS, dims[1])), shape((2, ROWS, dims[1])), shape(rest, F32)), [SMEM] + [VMEM] * 3,
                                (ids, a_own, to_x(a_send), after_these(to_h(b_send), *first)), [pltpu.VMEM(dims, F32)])
        first = to_z(sent)
        return (ids, kept, first, to_core(pair_of(kept, first))), rows

    q_sums = second_sum(*first_sum(lax.optimization_barrier(q_sums + (sent,))[:4]))
    parts, down_g = finish(sum_hidden_kernel, u_sums, (FROWS, D))
    gate_g, up_g = call(join_hidden_kernel, (shape((ROWS, 4 * FT), F32),) * 2, [SMEM] + [VMEM] * 3, parts,
                        [pltpu.VMEM((4, ROWS, 2 * FT), F32)])
    parts, out_g = finish(sum_qkv_kernel, q_sums, (ROWS, D), home, gate_g)
    query_g, key_g, value_g, gain_g = call(
        join_qkv_kernel, (shape((ROWS, D), F32),) * 3 + (shape((ROWS, 128), F32),), [SMEM] + [VMEM] * 3, parts)
    return (layer_out, input_grad, v1_out, gain_g[:, 0], query_g, key_g, value_g, out_g, gain_g[:, 1], gate_g, up_g, down_g)


def local(plan, layer_in, *rest):
    kept = plan.G == FAST_G and plan.T == FAST_T and layer_in.shape == (2, FAST_L, D) and rest[12].shape == (FROWS, D)
    return (fast if kept else general)(plan, layer_in, *rest)


def solution(mesh):
    plan = Plan(mesh.shape["gx"], mesh.shape["gy"])
    tokens, rows, vector = P(None, ALL, None), P(ALL, None), P(ALL)
    return jax.shard_map(
        functools.partial(local, plan),
        mesh=mesh,
        in_specs=(tokens, tokens, tokens, tokens, P(), vector, rows, rows, rows, rows, vector, rows, rows, rows),
        out_specs=(tokens, tokens, tokens, vector, rows, rows, rows, rows, vector, rows, rows, rows),
        check_vma=False,
    )
```

```python
import functools

import jax
import jax.numpy as jnp
from jax import lax
from jax.experimental import pallas as pl
from jax.experimental.pallas import tpu as pltpu
from jax.sharding import PartitionSpec as P

H = 16
EPS = 1e-05
NEG = -1e30
SCALE = 0.125
ALL = ("gx", "gy")
F32 = jnp.float32
BF16 = jnp.bfloat16


class Plan:
    def __init__(self, n_gx, n_gy):
        self.G, self.T = n_gx, n_gy // 2
        every = [(g, h, t) for g in range(self.G) for h in range(2) for t in range(self.T)]
        at = lambda g, h, t: g * n_gy + h * self.T + t
        self.g_swap = {k: [(at(g, h, t), at(g ^ k, h, t)) for g, h, t in every] for k in range(1, self.G)}
        self.t_swap = {k: [(at(g, h, t), at(g, h, t ^ k)) for g, h, t in every] for k in range(1, self.T)}
        self.h_swap = [(at(g, h, t), at(g, 1 - h, t)) for g, h, t in every]
        self.bits = []
        bit = self.T // 2
        while bit:
            self.bits.append(bit)
            bit //= 2


def pick(array, index, axis=0):
    return lax.dynamic_index_in_dim(array, index, axis, keepdims=False)


def send(array, pairs):
    return lax.ppermute(array, ALL, pairs)


def dot(a, b):
    return lax.dot_general(a, b, (((1,), (0,)), ((), ())), preferred_element_type=F32)


def dot_rows(a, b):
    return lax.dot_general(a, b, (((0,), (0,)), ((), ())), preferred_element_type=F32)


def dot_cols(a, b):
    return lax.dot_general(a, b, (((1,), (1,)), ((), ())), preferred_element_type=F32)


def rotate(values, cosine, sine):
    half = values.shape[-1] // 2
    a, b = values[..., :half], values[..., half:]
    return jnp.concatenate([a * cosine - b * sine, b * cosine + a * sine], axis=-1)


def general(plan, layer_in, first_layer_value, v1_acc, cotangent, seq_starts, norm1_gain, w_query, w_key, w_value,
          w_out, norm2_gain, w_gate, w_up, w_down):
    G, T, bits = plan.G, plan.T, plan.bits
    micro, L, D = layer_in.shape
    FF = w_gate.shape[1]
    HT, FT, heads = D // T, FF // T, H // T
    HD = D // H
    M = 2 * L
    N = T * M
    rows, frows = w_query.shape[0], w_down.shape[0]
    g, gy = lax.axis_index("gx"), lax.axis_index("gy")
    h, t = gy // T, gy % T

    def to_t(array, bit):
        return send(array, plan.t_swap[bit])

    def to_g(array, k):
        return send(array, plan.g_swap[k]) if k else array

    def to_h(array):
        return send(array, plan.h_swap)

    def inward(array):
        return jnp.concatenate([pick(array, h), to_h(pick(array, 1 - h))], axis=0)

    def outward(array):
        own, other = array[:L], to_h(array[L:])
        return jnp.stack([jnp.where(h == 0, own, other), jnp.where(h == 0, other, own)])

    def gather_t(array):
        parts = {0: array}
        for bit in bits:
            order = sorted(parts)
            moved = to_t(jnp.concatenate([parts[j] for j in order], axis=0), bit)
            size = array.shape[0]
            for i, j in enumerate(order):
                parts[j ^ bit] = moved[i * size:(i + 1) * size]
        return [parts[j] for j in range(T)]

    def reduce_t(partial):
        blocks = partial.reshape((T, -1) + partial.shape[1:])
        for bit in reversed(bits):
            shape = blocks.shape
            split = blocks.reshape((shape[0] // 2, 2) + shape[1:])
            blocks = split[:, 0] + to_t(split[:, 1].astype(BF16), bit).astype(F32)
        return blocks[0]

    def exchange_t(parts):
        held = {j: [parts[j]] for j in range(T)}
        sources = [0]
        for bit in bits:
            out = [j for j in sorted(held) if j & bit]
            flat = [p for j in out for p in held[j]]
            moved = to_t(jnp.stack(flat), bit)
            n = len(sources)
            new = {}
            for i, j in enumerate(out):
                new[j ^ bit] = held[j ^ bit] + [moved[i * n + s] for s in range(n)]
            sources = sources + [s ^ bit for s in sources]
            held = new
        result = [None] * T
        for s, p in zip(sources, held[0]):
            result[s] = p
        return result

    def natural(parts):
        array = jnp.stack(parts)
        for bit in bits:
            split = array.reshape((-1, 2, bit) + array.shape[1:])
            array = jnp.where((t & bit) != 0, split[:, ::-1], split).reshape(array.shape)
        return array

    def gather_r(block):
        other = to_h(block)
        pair = jnp.where(h == 0, jnp.stack([block, other]), jnp.stack([other, block]))
        full = jnp.zeros((G,) + pair.shape, pair.dtype)
        for k in range(G):
            full = lax.dynamic_update_slice(full, to_g(pair, k)[None], (g ^ k,) + (0,) * pair.ndim)
        return full.reshape((G * 2 * block.shape[0],) + block.shape[1:])

    def gather_cols(slices):
        block = natural(exchange_t([pick(slices, t ^ j) for j in range(T)]))
        return gather_r(block.reshape(T * block.shape[1], -1))

    def reduce_r(grad):
        n, w = grad.shape[0] // (2 * G), grad.shape[1]
        grad = grad.astype(BF16).reshape(G, 2 * n, w)
        total = pick(grad, g).astype(F32)
        for k in range(1, G):
            total = total + to_g(pick(grad, g ^ k), k).astype(F32)
        total = total.reshape(2, n, w)
        return pick(total, h) + to_h(pick(total, 1 - h).astype(BF16)).astype(F32)

    def scatter_cols(grad):
        total = reduce_r(grad).reshape(T, rows, -1)
        low = total.astype(BF16)
        return natural(exchange_t([pick(low, t ^ j) for j in range(T)])).astype(F32)

    pad = jnp.zeros((rows, 126), BF16)
    gains_in = jnp.concatenate([norm1_gain[:, None], norm2_gain[:, None], pad], axis=1)

    def col_slices(w):
        return w.reshape(rows, T, HT).transpose(1, 0, 2)

    def hidden_slices(w):
        return w.reshape(rows, 2 * G, T, frows).transpose(2, 0, 1, 3).reshape(T, rows, FT)

    qkv_slices = jnp.concatenate([col_slices(w_query), col_slices(w_key), col_slices(w_value),
                                  jnp.broadcast_to(gains_in[None], (T, rows, 128))], axis=2)
    x_own = inward(layer_in)
    qkv_w = gather_cols(qkv_slices)
    x_all = jnp.concatenate(gather_t(x_own), axis=0)
    v_own = inward(first_layer_value).reshape(M, T, HT).transpose(1, 0, 2)
    v_all = jnp.concatenate(exchange_t([pick(v_own, t ^ j) for j in range(T)]), axis=0)
    gu_w = gather_cols(jnp.concatenate([hidden_slices(w_gate), hidden_slices(w_up)], axis=2))
    down_w = gather_r(w_down)
    c_own = inward(cotangent)
    c_all = jnp.concatenate(gather_t(c_own), axis=0)
    out_w = natural(gather_t(gather_r(w_out))).reshape(T, 2 * G, rows, D).transpose(1, 0, 2, 3).reshape(D, D)
    out_w = out_w.reshape(T, HT, D)

    gains = qkv_w[:, 3 * HT:3 * HT + 2].astype(F32).T
    gain_one, gain_two = gains[0], gains[1]
    query_w, key_w, value_w = qkv_w[:, :HT], qkv_w[:, HT:2 * HT], qkv_w[:, 2 * HT:3 * HT]
    gate_w, up_w = gu_w[:, :FT], gu_w[:, FT:]

    starts = pick(seq_starts, h)
    member = t ^ jnp.arange(T, dtype=jnp.int32)
    half = h ^ jnp.arange(2, dtype=jnp.int32)
    position = ((half[None, :] * T + member[:, None]) * L)[:, :, None] + jnp.arange(L, dtype=jnp.int32)
    position = position.reshape(N) + g * N
    begin = jnp.max(jnp.where(starts[None, :] <= position[:, None], starts[None, :], 0), axis=1)
    rel = (position - begin).astype(F32)
    visible = (begin[:, None] == begin[None, :]) & (position[None, :] <= position[:, None])
    frequency = 10000.0 ** (-(jnp.arange(HD // 2, dtype=F32) * 2.0 / HD))
    angles = rel[:, None] * frequency[None, :]
    cosine, sine = jnp.cos(angles)[:, None, :], jnp.sin(angles)[:, None, :]

    x = x_all.astype(F32)
    rstd_one = lax.rsqrt(jnp.mean(x * x, axis=-1, keepdims=True) + EPS)
    normed_one = (x * rstd_one * gain_one).astype(BF16)
    query = rotate(dot(normed_one, query_w).reshape(N, heads, HD), cosine, sine).astype(BF16)
    key = rotate(dot(normed_one, key_w).reshape(N, heads, HD), cosine, sine).astype(BF16)
    value = (0.5 * dot(normed_one, value_w) + 0.5 * v_all.astype(F32)).astype(BF16).reshape(N, heads, HD)
    scores = jnp.einsum("ihd,jhd->hij", query, key, preferred_element_type=F32) * SCALE
    scores = jnp.where(visible[None], scores, NEG)
    top = jnp.max(scores, axis=-1, keepdims=True)
    probs = jnp.exp(scores - top)
    denom = jnp.sum(probs, axis=-1, keepdims=True)
    probs = probs / denom
    probs_low = probs.astype(BF16)
    attn = jnp.einsum("hij,jhd->ihd", probs_low, value, preferred_element_type=F32)
    attn_low = attn.reshape(N, HT).astype(BF16)
    attn_parts = []
    for j, part in enumerate(gather_t(attn_low)):
        part = part.reshape(T, M, HT)
        attn_parts.append(jnp.concatenate([part[b ^ j] for b in range(T)], axis=0))
    after = x
    for j in range(T):
        after = after + dot(attn_parts[j], pick(out_w, t ^ j))
    rstd_two = lax.rsqrt(jnp.mean(after * after, axis=-1, keepdims=True) + EPS)
    hat_two = after * rstd_two
    normed_two = (hat_two * gain_two).astype(BF16)
    gate = dot(normed_two, gate_w)
    up = dot(normed_two, up_w)
    sig = jax.nn.sigmoid(gate)
    act = gate * sig
    hidden = (act * up).astype(BF16)

    grad_hidden = dot_cols(c_all, down_w)
    grad_gate = (grad_hidden * up * (sig * (1.0 + gate * (1.0 - sig)))).astype(BF16)
    grad_up = (grad_hidden * act).astype(BF16)
    grad_two_part = dot_cols(grad_gate, gate_w) + dot_cols(grad_up, up_w)
    gain_two_grad = jnp.sum(grad_two_part * hat_two, axis=0)
    grad_two = reduce_t(grad_two_part) * gain_two
    hat_own = hat_two[:M]
    grad_after = c_own.astype(F32) + rstd_two[:M] * (
        grad_two - hat_own * jnp.mean(grad_two * hat_own, axis=-1, keepdims=True))
    grad_branch = jnp.concatenate(gather_t(grad_after.astype(BF16)), axis=0)
    result = reduce_t(dot(hidden, down_w)) + after[:M]
    layer_out = outward(result.astype(BF16))
    grad_down = dot_rows(hidden, c_all)
    grad_gu = dot_rows(normed_two, jnp.concatenate([grad_gate, grad_up], axis=1))

    grad_attn = dot_cols(grad_branch, pick(out_w, t)).astype(BF16).reshape(N, heads, HD)
    delta = jnp.sum(grad_attn.astype(F32) * attn, axis=-1).T
    grad_probs = jnp.einsum("ihd,jhd->hij", grad_attn, value, preferred_element_type=F32)
    grad_scores = (probs * (grad_probs - delta[..., None])).astype(BF16)
    grad_query = jnp.einsum("hij,jhd->ihd", grad_scores, key, preferred_element_type=F32) * SCALE
    grad_key = jnp.einsum("hij,ihd->jhd", grad_scores, query, preferred_element_type=F32) * SCALE
    grad_blend = jnp.einsum("hij,ihd->jhd", probs_low, grad_attn, preferred_element_type=F32).reshape(N, HT)
    grad_query = rotate(grad_query, cosine, -sine).reshape(N, HT).astype(BF16)
    grad_key = rotate(grad_key, cosine, -sine).reshape(N, HT).astype(BF16)
    grad_value = (0.5 * grad_blend).astype(BF16)
    grad_one_part = dot_cols(grad_query, query_w) + dot_cols(grad_key, key_w) + dot_cols(grad_value, value_w)
    hat_one = x * rstd_one
    gain_one_grad = jnp.sum(grad_one_part * hat_one, axis=0)
    grad_one = reduce_t(grad_one_part) * gain_one
    hat_own = hat_one[:M]
    input_grad = grad_after + rstd_one[:M] * (
        grad_one - hat_own * jnp.mean(grad_one * hat_own, axis=-1, keepdims=True))
    input_grad = outward(input_grad.astype(BF16)).astype(F32)
    v_parts = natural(exchange_t([grad_value[j * M:(j + 1) * M] for j in range(T)]))
    v1_out = v1_acc + outward(v_parts.transpose(1, 0, 2).reshape(M, D)).astype(F32)

    attn_full = natural([p.T for p in attn_parts]).reshape(2 * G, T, rows, N)
    grad_out = dot(pick(attn_full, t, 1).reshape(2 * G * rows, N), grad_branch)
    grad_gains = jnp.stack([gain_one_grad, gain_two_grad], axis=1)
    grad_gains = jnp.concatenate([grad_gains, jnp.zeros((D, 126), F32)], axis=1)
    grad_qkv = dot_rows(normed_one, jnp.concatenate([grad_query, grad_key, grad_value], axis=1))
    down_g = reduce_r(grad_down)
    gu_g = scatter_cols(grad_gu)
    out_g = reduce_r(grad_out)
    qkv_g = scatter_cols(jnp.concatenate([grad_qkv, grad_gains], axis=1))

    def col_join(parts):
        return parts.transpose(1, 0, 2).reshape(rows, D)

    def hidden_join(parts):
        return parts.reshape(T, rows, 2 * G, frows).transpose(1, 2, 0, 3).reshape(rows, FF)

    gain_g = jnp.sum(qkv_g[:, :, 3 * HT:3 * HT + 2], axis=0)
    return (layer_out, input_grad, v1_out, gain_g[:, 0], col_join(qkv_g[:, :, :HT]), col_join(qkv_g[:, :, HT:2 * HT]),
            col_join(qkv_g[:, :, 2 * HT:3 * HT]), out_g, gain_g[:, 1], hidden_join(gu_g[:, :, :FT]),
            hidden_join(gu_g[:, :, FT:]), down_g)


FAST_G, FAST_T, FAST_L, D, HT, FT, FROWS, ROWS = 4, 4, 64, 1024, 256, 704, 88, 32
M, N = 2 * FAST_L, 8 * FAST_L
HALF = N // 2
WQ = 3 * HT + 128
ORDER = (0, 2, 1, 3)
HD = 64
ARRIVED = ((0, 0), (1, 0), (2, 0), (3, 0), (0, 1), (2, 1), (1, 1), (3, 1))
LEAVING = {(0, 0): (0, 0), (1, 0): (0, 1), (2, 0): (1, 0), (3, 0): (1, 1), (0, 1): (2, 0), (2, 1): (2, 1), (1, 1): (3, 0), (3, 1): (3, 1)}
VMEM = pl.BlockSpec(memory_space=pltpu.VMEM)
SMEM = pl.BlockSpec(memory_space=pltpu.SMEM)
ANY = pl.BlockSpec(memory_space=pltpu.HBM)


def shape(dims, dtype=BF16):
    return jax.ShapeDtypeStruct(dims, dtype)


def call(kernel, outs, specs, args, scratch=(), mib=40):
    return pl.pallas_call(
        kernel,
        out_shape=outs,
        in_specs=specs,
        out_specs=jax.tree.map(lambda _: VMEM, outs),
        scratch_shapes=list(scratch),
        compiler_params=pltpu.CompilerParams(vmem_limit_bytes=mib << 20),
        cost_estimate=pl.CostEstimate(flops=1, bytes_accessed=1, transcendentals=0),
    )(*args)


def aligned(index, size):
    return pl.ds(pl.multiple_of(index * size, size), size)


def eye(rows, lanes):
    return (lax.broadcasted_iota(jnp.int32, (rows, lanes), 0) == lax.broadcasted_iota(jnp.int32, (rows, lanes), 1)).astype(BF16)


def tiles_in(block):
    lines = [jnp.concatenate([block[j * 8:j * 8 + 8, i * 128:i * 128 + 128] for j in range(11)], axis=1) for i in range(8)]
    return jnp.concatenate(lines, axis=0)


def tiles_out(block):
    lines = [jnp.concatenate([block[i * 8:i * 8 + 8, j * 128:j * 128 + 128] for i in range(8)], axis=1) for j in range(11)]
    return jnp.concatenate(lines, axis=0)


def line_tiles_in(block):
    tiles = [block[j * 8:j * 8 + 8, i * 128:i * 128 + 128] for j in range(4) for i in range(8)]
    tiles += [jnp.zeros_like(tiles[0])] * 3
    return jnp.concatenate([jnp.concatenate(tiles[n * 7:n * 7 + 7], axis=1) for n in range(5)], axis=0)


def line_tiles_out(block):
    tiles = [block[n * 8:n * 8 + 8, i * 128:i * 128 + 128] for n in range(5) for i in range(7)]
    return jnp.concatenate([jnp.concatenate(tiles[j * 8:j * 8 + 8], axis=1) for j in range(4)], axis=0)


def pack_first(ids, gain_one, gain_two, wq, wk, wv, wo, x, v, c, out, keep, lines, xv_out, c_out, rows, whole, sem):
    h, t = ids[1], ids[2]
    copies = []
    for j in (2, 3, 0, 1):
        to = keep if j < 2 else out
        for i, w in enumerate((wq, wk, wv)):
            copies.append((w.at[:, aligned(t ^ j, HT)], to.at[j % 2, :, i * HT:(i + 1) * HT]))
    copies += [(wo, whole), (x.at[1 - h], xv_out.at[:, :D]), (v.at[1 - h], xv_out.at[:, D:]), (c.at[1 - h], c_out)]
    started = fetch(copies, sem)
    rows[...] = jnp.zeros_like(rows)
    rows[0:1] = gain_one[...].astype(F32)
    rows[1:2] = gain_two[...].astype(F32)
    gains = dot_rows(rows[...].astype(BF16), eye(8, 128)).astype(BF16)
    for j in range(4):
        (keep if j < 2 else out)[j % 2, :, 3 * HT:] = gains
    started[12].wait()
    lines[...] = line_tiles_in(whole[...].astype(F32)).astype(BF16)
    for n, copy in enumerate(started):
        if n != 12:
            copy.wait()


def pack_hidden(ids, wg, wu, wd, keep, out, down, nat, gate, up, whole, sem):
    t = ids[2]
    started = fetch([(wg, gate), (wu, up), (wd, whole)], sem)
    for a, w in enumerate((gate, up)):
        started[a].wait()
        for m in range(4):
            for i in range(8):
                at, to = (i * 4 + m) * FROWS, a * FT + i * FROWS
                nat[m, :, to:to + FROWS] = w[:, at:at + FROWS].astype(F32)
    for j in range(4):
        to = keep if j < 2 else out
        to[j % 2] = nat[t ^ j].astype(BF16)
    started[2].wait()
    down[...] = tiles_in(whole[...].astype(F32)).astype(BF16)


def pack_block(kept, first, last, tail, out, sem):
    width = ROWS
    parts = (kept.at[0], first.at[0], last.at[0], last.at[1], tail)
    started = fetch([(part, out.at[i * width:i * width + part.shape[0]]) for i, part in enumerate(parts)], sem)
    for copy in started:
        copy.wait()


def pack_pair(kept, first, out, sem):
    started = fetch([(kept.at[1], out.at[0]), (first.at[1], out.at[1])], sem)
    for copy in started:
        copy.wait()


def pack_out(b0, b1, b2, b3, out, raw, sem):
    started = fetch([((b0, b1, b2, b3)[n // 2].at[n % 2, 4 * ROWS:], raw.at[n]) for n in range(8)], sem)
    for n in range(8):
        started[n].wait()
        out[n * ROWS:(n + 1) * ROWS] = line_tiles_out(raw[n].astype(F32)).astype(BF16)


def pack_second(ids, x, v, moved, xv_out, v_keep, own, sem):
    h, t = ids[1], ids[2]
    started = fetch([(x.at[h], xv_out.at[:FAST_L, :D]), (v.at[h], own.at[:FAST_L]),
                     (moved.at[:, :D], xv_out.at[FAST_L:, :D]), (moved.at[:, D:], own.at[FAST_L:])], sem)
    for copy in started:
        copy.wait()
    for j in range(2):
        v_keep[j] = own[:, aligned(t ^ j, HT)]
        xv_out[:, D + j * HT:D + (j + 1) * HT] = own[:, aligned(t ^ (j + 2), HT)]


def pack_third(mine, moved, v_keep, out, v_two):
    out[:M, :D] = mine[:, :D]
    out[M:, :D] = moved[:, :D]
    out[:M, D:] = v_keep[1]
    out[M:, D:] = moved[:, D + HT:]
    v_two[:M] = v_keep[0]
    v_two[M:] = moved[:, D:D + HT]


def fetch(copies, sem):
    started = []
    for i, (source, target) in enumerate(copies):
        copy = pltpu.make_async_copy(source, target, sem.at[i])
        copy.start()
        started.append(copy)
    return started


def swap_halves(u):
    width = u.shape[-1]
    lane = lax.broadcasted_iota(jnp.int32, u.shape, 1)
    up = pltpu.roll(u, width - HD // 2, 1)
    down = pltpu.roll(u, HD // 2, 1)
    return jnp.where(lane % HD < HD // 2, up, down)


def scale_of(x):
    return lax.rsqrt(jnp.mean(x * x, axis=-1, keepdims=True) + EPS)


def attend_kernel(ids, x2, xc, v2, cs, sn, bias, b0, b1, b2, b3, w, normed, qkv, attn, low, lse, gains, sem):
    g, h, t = ids[0], ids[1], ids[2]
    copies = []
    for n, (k, dh) in enumerate(ARRIVED):
        b = (b0, b1, b2, b3)[n // 2]
        for i, s in enumerate(ORDER):
            row = ((g ^ k) * 2 + (h ^ dh)) * 4 + (t ^ s)
            copies.append((b.at[n % 2, i * ROWS:(i + 1) * ROWS], w.at[aligned(row, ROWS)]))
    for copy in fetch(copies, sem):
        copy.wait()
    gains[...] = dot_cols(eye(8, 128), w[:, 3 * HT:])
    gain = gains[0:1, :]
    for b in range(2):
        rows = slice(b * HALF, (b + 1) * HALF)
        source = x2 if b == 0 else xc
        x = source[:, :D].astype(F32)
        r = (x * scale_of(x) * gain).astype(BF16)
        normed[rows] = r
        out = dot(r, w[:, :3 * HT])
        for i in range(2):
            u = out[:, i * HT:(i + 1) * HT]
            qkv[rows, i * HT:(i + 1) * HT] = (u * cs[rows] + swap_halves(u) * sn[rows]).astype(BF16)
        value = v2[...] if b == 0 else xc[:, D:]
        qkv[rows, 2 * HT:] = (0.5 * out[:, 2 * HT:] + 0.5 * value.astype(F32)).astype(BF16)
    for b in range(2):
        rows = slice(b * HALF, (b + 1) * HALF)
        outs, tops = [], []
        for i in range(4):
            lanes = slice(i * HD, (i + 1) * HD)
            q = qkv[rows, lanes]
            k = qkv[:, HT + i * HD:HT + (i + 1) * HD]
            v = qkv[:, 2 * HT + i * HD:2 * HT + (i + 1) * HD]
            s = dot_cols(q, k) * SCALE + bias[rows].astype(F32)
            top = jnp.max(s, axis=-1, keepdims=True)
            p = jnp.exp(s - top)
            total = jnp.sum(p, axis=-1, keepdims=True)
            outs.append(dot(p.astype(BF16), v) / total)
            tops.append(top + jnp.log(total))
        o = jnp.concatenate(outs, axis=1)
        attn[rows] = o
        low[rows] = o.astype(BF16)
        lse[rows] = jnp.concatenate(tops, axis=1)


def after_kernel(ids, x2, xc, o2, oc, gains, co2, coc, full, after, normed, own_w, w, sem):
    g, h, t = ids[0], ids[1], ids[2]
    copies = []
    for i, s in enumerate(ORDER):
        source = co2 if i < 2 else coc
        for n, (k, dh) in enumerate(ARRIVED):
            row = ((g ^ k) * 2 + (h ^ dh)) * 4 + (t ^ s)
            at = (i % 2) * HT + n * ROWS
            copies.append((source.at[at:at + ROWS], w.at[aligned(row, ROWS)]))
    started = fetch(copies, sem)
    for i, s in enumerate(ORDER):
        source = o2 if i < 2 else oc
        for p in range(4):
            q = ORDER.index(ORDER[p] ^ s)
            full[p * M:(p + 1) * M, aligned(t ^ s, HT)] = source[(i % 2) * N + q * M:(i % 2) * N + (q + 1) * M]
    for copy in started:
        copy.wait()
    own_w[...] = w[aligned(t, HT)]
    gain = gains[1:2, :]
    for b in range(2):
        rows = slice(b * HALF, (b + 1) * HALF)
        source = x2 if b == 0 else xc
        a = source[:, :D].astype(F32) + dot(full[rows], w[...])
        if b == 0:
            after[...] = a[:M]
        normed[rows] = (a * scale_of(a) * gain).astype(BF16)


def feed_kernel(ids, normed, gains, c2, cc, u0, u1, u2, u3, out_keep, out_send, r_keep, r_send, gain_g, a_keep, a_send, b_keep, b_send,
                w, wd, wide, raw, hidden, dgu, gu_g, sem, sem_d):
    g, h, t = ids[0], ids[1], ids[2]
    copies, copies_d = [], []
    for n, (k, dh) in enumerate(ARRIVED):
        b = (u0, u1, u2, u3)[n // 2]
        for i, s in enumerate(ORDER):
            row = ((g ^ k) * 2 + (h ^ dh)) * 4 + (t ^ s)
            copies.append((b.at[n % 2, i * ROWS:(i + 1) * ROWS], w.at[aligned(row, ROWS)]))
        copies_d.append((b.at[n % 2, 4 * ROWS:], raw.at[n]))
    started_d, started = fetch(copies_d, sem_d), fetch(copies, sem)
    for n, (k, dh) in enumerate(ARRIVED):
        started_d[n].wait()
        wide[aligned((g ^ k) * 2 + (h ^ dh), FROWS)] = tiles_out(raw[n].astype(F32))
    wd[...] = wide[...].astype(BF16)
    for copy in started:
        copy.wait()
    gain_sum = jnp.zeros((1, D), F32)
    for b in range(2):
        rows = slice(b * HALF, (b + 1) * HALF)
        c = (c2 if b == 0 else cc)[...]
        gu = dot(normed[rows], w[...])
        gate, up = gu[:, :FT], gu[:, FT:]
        sig = 1.0 / (1.0 + jnp.exp(-gate))
        act = gate * sig
        hid = (act * up).astype(BF16)
        hidden[rows] = hid
        dh = dot_cols(c, wd[...])
        dgu[rows, :FT] = (dh * up * (sig * (1.0 + gate * (1.0 - sig)))).astype(BF16)
        dgu[rows, FT:] = (dh * act).astype(BF16)
        dr = dot_cols(dgu[rows], w[...])
        out = dot(hid, wd[...])
        gain_sum = gain_sum + jnp.sum(dr * normed[rows].astype(F32), axis=0, keepdims=True)
        (r_keep if b == 0 else r_send)[...] = dr.astype(BF16)
        (out_keep if b == 0 else out_send)[...] = out.astype(BF16)
    gain_g[...] = gain_sum / gains[1:2, :]
    wide[...] = dot_rows(hidden[:HALF], c2[...]) + dot_rows(hidden[HALF:], cc[...])
    for k in range(4):
        gu_g[...] = dot_rows(normed[:, aligned(g ^ k, HT)], dgu[...])
        for e in range(2):
            target, at = LEAVING[(k, e)]
            target = (a_keep, a_send, b_keep, b_send)[target]
            target[at, :4 * ROWS] = gu_g[aligned(h ^ e, 4 * ROWS)].astype(BF16)
            target[at, 4 * ROWS:] = tiles_in(wide[aligned((g ^ k) * 2 + (h ^ e), FROWS)]).astype(BF16)


def fold_kernel(keep, moved, kept, send):
    kept[...] = keep[:M].astype(F32) + moved[:M].astype(F32)
    send[...] = (keep[M:].astype(F32) + moved[M:].astype(F32)).astype(BF16)


def fold_both_kernel(keep, dv, moved, kept, send):
    kept[...] = keep[:M].astype(F32) + moved[:M, :D].astype(F32)
    send[:, :D] = (keep[M:].astype(F32) + moved[M:, :D].astype(F32)).astype(BF16)
    send[:, D:D + HT] = dv[M:]
    send[:, D + HT:] = moved[M:, D:]


def branch_kernel(keep, moved, after, gains, c2, grad_after, low):
    a = after[...]
    scale = scale_of(a)
    hat = a * scale
    dy = (keep[...] + moved[...].astype(F32)) * gains[1:2, :]
    d = c2[:M].astype(F32) + scale * (dy - hat * jnp.mean(dy * hat, axis=-1, keepdims=True))
    grad_after[...] = d
    low[...] = d.astype(BF16)


def attend_back_kernel(ids, da2, dac, wo, qkv, attn, lse, bias, cs, sn, w, normed, gains, gain_two, full,
                       r_keep, r_send, dv_keep, a_keep, a_send, b_keep, b_send, do, dk, dv, dqkv, scratch, rows_g, qkv_g):
    g, h, t = ids[0], ids[1], ids[2]
    for b in range(2):
        rows = slice(b * HALF, (b + 1) * HALF)
        do[rows] = dot_cols((da2 if b == 0 else dac)[...], wo[...]).astype(BF16)
    for b in range(2):
        rows = slice(b * HALF, (b + 1) * HALF)
        dqs = []
        for i in range(4):
            lanes = slice(i * HD, (i + 1) * HD)
            q = qkv[rows, lanes]
            k = qkv[:, HT + i * HD:HT + (i + 1) * HD]
            v = qkv[:, 2 * HT + i * HD:2 * HT + (i + 1) * HD]
            d = do[rows, lanes]
            delta = jnp.sum(d.astype(F32) * attn[rows, lanes], axis=-1, keepdims=True)
            p = jnp.exp(dot_cols(q, k) * SCALE + bias[rows].astype(F32) - lse[rows, i:i + 1])
            ds = (p * (dot_cols(d, v) - delta)).astype(BF16)
            dqs.append(dot(ds, k))
            dki, dvi = dot_rows(ds, q), dot_rows(p.astype(BF16), d)
            if b == 0:
                dk[:, lanes], dv[:, lanes] = dki, dvi
            else:
                dk[:, lanes], dv[:, lanes] = dk[:, lanes] + dki, dv[:, lanes] + dvi
        u = jnp.concatenate(dqs, axis=1) * SCALE
        dqkv[rows, :HT] = (u * cs[rows] - swap_halves(u) * sn[rows]).astype(BF16)
    gain_sum = jnp.zeros((1, D), F32)
    for b in range(2):
        rows = slice(b * HALF, (b + 1) * HALF)
        u = dk[rows] * SCALE
        dqkv[rows, HT:2 * HT] = (u * cs[rows] - swap_halves(u) * sn[rows]).astype(BF16)
        dqkv[rows, 2 * HT:] = (0.5 * dv[rows]).astype(BF16)
        dr = dot_cols(dqkv[rows], w[:, :3 * HT])
        gain_sum = gain_sum + jnp.sum(dr * normed[rows].astype(F32), axis=0, keepdims=True)
        if b == 0:
            r_keep[...] = dr.astype(BF16)
            dv_keep[...] = dqkv[rows, 2 * HT:]
        else:
            r_send[:, :D] = dr.astype(BF16)
            r_send[:, D:] = dqkv[rows, 2 * HT:]
    rows_g[...] = jnp.zeros_like(rows_g)
    rows_g[0:1] = gain_sum / gains[0:1, :]
    rows_g[1:2] = gain_two[...]
    for k in range(4):
        lanes = aligned(g ^ k, HT)
        qkv_g[:, :3 * HT] = dot_rows(normed[:, lanes], dqkv[...])
        qkv_g[:, 3 * HT:] = dot_rows(rows_g[:, lanes].astype(BF16), eye(8, 128))
        scratch[...] = dot_rows(full[:HALF, lanes], da2[...]) + dot_rows(full[HALF:, lanes], dac[...])
        for e in range(2):
            target, at = LEAVING[(k, e)]
            target = (a_keep, a_send, b_keep, b_send)[target]
            target[at, :4 * ROWS] = qkv_g[aligned(h ^ e, 4 * ROWS)].astype(BF16)
            target[at, 4 * ROWS:] = line_tiles_in(scratch[aligned((h ^ e) * 4 + t, ROWS)]).astype(BF16)


def sum_first_kernel(a_keep, a_moved, b_keep, b_moved, a_own, a_send, b_own, b_send):
    for keep, moved, own, out in ((a_keep, a_moved, a_own, a_send), (b_keep, b_moved, b_own, b_send)):
        own[...] = (keep[0].astype(F32) + moved[0].astype(F32)).astype(BF16)
        out[...] = (keep[1].astype(F32) + moved[1].astype(F32)).astype(BF16)


def sum_second_kernel(b_own, b_moved, b_send):
    b_send[...] = (b_own[...].astype(F32) + b_moved[...].astype(F32)).astype(BF16)


def sum_third(a_own, a_moved, moved, total):
    total[...] = (a_own[...].astype(F32) + a_moved[...].astype(F32)) + moved[...].astype(F32)


def sum_hidden_kernel(ids, a_own, a_moved, moved, kept, send, down, total):
    t = ids[2]
    sum_third(a_own, a_moved, moved, total)
    for j in range(4):
        (kept if j < 2 else send)[j % 2] = total[aligned(t ^ j, ROWS)].astype(BF16)
    down[...] = tiles_out(total[4 * ROWS:])


def sum_qkv_kernel(ids, a_own, a_moved, moved, kept, send, out, total):
    t = ids[2]
    sum_third(a_own, a_moved, moved, total)
    for j in range(4):
        (kept if j < 2 else send)[j % 2] = total[aligned(t ^ j, ROWS)].astype(BF16)
    out[...] = line_tiles_out(total[4 * ROWS:])


def join_qkv_kernel(ids, kept, first, last, q, k, v, gains):
    t = ids[2]
    parts = (kept[0], first[0], last[0], last[1])
    for s, part in zip(ORDER, parts):
        for i, ref in enumerate((q, k, v)):
            ref[:, aligned(t ^ s, HT)] = part[:, i * HT:(i + 1) * HT].astype(F32)
    low = [part[:, 3 * HT:].astype(F32) for part in parts]
    gains[...] = (low[0] + low[1]) + (low[2] + low[3])


def join_hidden_kernel(ids, kept, first, last, gate, up, nat):
    t = ids[2]
    for s, part in zip(ORDER, (kept[0], first[0], last[0], last[1])):
        nat[t ^ s] = part.astype(F32)
    for m in range(4):
        for a, ref in enumerate((gate, up)):
            for i in range(8):
                to, at = (i * 4 + m) * FROWS, a * FT + i * FROWS
                ref[:, to:to + FROWS] = nat[m, :, at:at + FROWS]


def input_kernel(ids, keep, moved, x2, gains, grad_after, dv, dv_core, own, send, both):
    t = ids[2]
    x = x2[:M, :D].astype(F32)
    scale = scale_of(x)
    hat = x * scale
    dy = (keep[...] + moved[:, :D].astype(F32)) * gains[0:1, :]
    both[:, :D] = (grad_after[...] + scale * (dy - hat * jnp.mean(dy * hat, axis=-1, keepdims=True))).astype(BF16)
    parts = (dv[:M], moved[:, D:D + HT], dv_core[:M, D:], moved[:, D + HT:])
    for s, part in zip(ORDER, parts):
        both[:, aligned(4 + (t ^ s), HT)] = part
    own[...] = both[:FAST_L]
    send[...] = both[FAST_L:]


def home_kernel(ids, own, moved, v1, grad, v_out):
    h = ids[1]
    grad[h] = own[:, :D].astype(F32)
    grad[1 - h] = moved[:, :D].astype(F32)
    v_out[h] = v1[h] + own[:, D:].astype(F32)
    v_out[1 - h] = v1[1 - h] + moved[:, D:].astype(F32)


def result_kernel(keep, moved, after, own, send):
    out = after[...] + (keep[...] + moved[...].astype(F32))
    own[...] = out[:FAST_L].astype(BF16)
    send[...] = out[FAST_L:].astype(BF16)


def result_home_kernel(ids, own, moved, out):
    h = ids[1]
    out[h] = own[...]
    out[1 - h] = moved[...]


def fast(plan, layer_in, first_layer_value, v1_acc, cotangent, seq_starts, norm1_gain, w_query, w_key, w_value,
         w_out, norm2_gain, w_gate, w_up, w_down):
    L = FAST_L
    g, gy = lax.axis_index("gx"), lax.axis_index("gy")
    h, t = gy // 4, gy % 4
    ids = jnp.stack([g, h, t]).astype(jnp.int32)

    def to_z(array):
        return send(array, plan.t_swap[2])

    def to_core(array):
        return send(array, plan.t_swap[1])

    def to_h(array):
        return send(array, plan.h_swap)

    def to_x(array):
        return send(array, plan.g_swap[1])

    def to_y(array):
        return send(array, plan.g_swap[2])

    def after_these(array, *others):
        return lax.optimization_barrier((array,) + others)[0]

    def fenced(part, *inputs):
        results = jax.eval_shape(part, *inputs)
        nothing = lambda *_: jax.tree.map(lambda a: jnp.zeros(a.shape, a.dtype), results)
        return lax.cond(ids[0] >= 0, part, nothing, *inputs)

    def spread(own, other, *first):
        a_pair = jnp.stack([own, to_x(own)])
        b_pair = jnp.stack([other, to_y(other)])
        a_pair, b_pair = lax.optimization_barrier((a_pair, b_pair) + first)[:2]
        return a_pair, to_y(a_pair), b_pair, to_x(b_pair)

    def pair_of(kept, first):
        return call(pack_pair, shape(kept.shape), [ANY] * 2, (kept, first), [pltpu.SemaphoreType.DMA((2,))])

    def block_of(kept, first, last, tail):
        return call(pack_block, shape((4 * ROWS + tail.shape[0], tail.shape[1])), [ANY] * 4, (kept, first, last, tail),
                    [pltpu.SemaphoreType.DMA((5,))])

    q_send, q_keep, o_block, xv_send, c_send = call(
        pack_first, (shape((2, ROWS, WQ)), shape((2, ROWS, WQ)), shape((40, WQ)), shape((L, 2 * D)), shape((L, D))),
        [SMEM] + [VMEM] * 2 + [ANY] * 7,
        (ids, norm1_gain[None], norm2_gain[None], w_query, w_key, w_value, w_out, layer_in, first_layer_value, cotangent),
        [pltpu.VMEM((8, ROWS), F32), pltpu.VMEM((ROWS, D), BF16), pltpu.SemaphoreType.DMA((16,))], mib=63)
    q_first = to_z(q_send)
    xv_moved = to_h(xv_send)
    q_last = to_core(pair_of(q_keep, q_first))
    q_block = block_of(q_keep, q_first, q_last, o_block)
    q_other = to_h(q_block)

    starts = pick(after_these(seq_starts, q_block), h)
    member = t ^ jnp.array(ORDER, jnp.int32)
    half = h ^ jnp.arange(2, dtype=jnp.int32)
    position = ((half[None, :] * 4 + member[:, None]) * L)[:, :, None] + jnp.arange(L, dtype=jnp.int32)
    position = position.reshape(N) + g * N
    begin = jnp.max(jnp.where(starts[None, :] <= position[:, None], starts[None, :], 0), axis=1)
    visible = (begin[:, None] == begin[None, :]) & (position[None, :] <= position[:, None])
    bias = jnp.where(visible, 0.0, NEG).astype(BF16)
    lane = jnp.arange(HT, dtype=jnp.int32)
    frequency = 10000.0 ** (-((lane % (HD // 2)).astype(F32) * 2.0 / HD))
    angles = (position - begin).astype(F32)[:, None] * frequency[None, :]
    cs = jnp.cos(angles)
    sn = jnp.sin(angles) * jnp.where(lane % HD < HD // 2, -1.0, 1.0)[None, :]

    xv_out, v_keep = call(pack_second, (shape((M, D + 2 * HT)), shape((2, M, HT))), [SMEM] + [ANY] * 3,
                          (ids, layer_in, first_layer_value, xv_moved), [pltpu.VMEM((M, D), BF16), pltpu.SemaphoreType.DMA((4,))], mib=63)
    x_two, v_two = call(pack_third, (shape((HALF, D + HT)), shape((HALF, HT))), [VMEM] * 3, (xv_out, to_z(xv_out), v_keep))
    x_core = to_core(x_two)
    q_other, cs, sn, bias, _ = lax.optimization_barrier((q_other, cs, sn, bias, xv_out))
    q_parts = spread(q_block, q_other, x_two)

    u_keep, u_send, d_block = call(
        pack_hidden, (shape((2, ROWS, 2 * FT)), shape((2, ROWS, 2 * FT)), shape((2 * ROWS, 2 * FT))), [SMEM] + [ANY] * 3,
        (after_these(ids, q_send), w_gate, w_up, w_down),
        [pltpu.VMEM((4, ROWS, 2 * FT), F32), pltpu.VMEM((ROWS, 4 * FT), BF16), pltpu.VMEM((ROWS, 4 * FT), BF16), pltpu.VMEM((FROWS, D), BF16),
         pltpu.SemaphoreType.DMA((3,))], mib=63)
    u_first = to_z(u_send)
    u_last = to_core(pair_of(u_keep, after_these(u_first, q_block)))
    u_block = block_of(u_keep, u_first, u_last, d_block)
    u_other = to_h(after_these(u_block, q_block))
    c_moved = to_h(after_these(c_send, u_other))
    u_a = jnp.stack([u_block, to_x(after_these(u_block, q_parts[2]))])
    u_b = jnp.stack([u_other, to_y(u_other)])
    o_own = call(pack_out, shape((HT, D)), [ANY] * 4, q_parts, [pltpu.VMEM((8, 40, WQ), BF16), pltpu.SemaphoreType.DMA((8,))])
    o_first = to_z(o_own)
    c_own = jnp.concatenate([pick(cotangent, h), after_these(c_moved, o_own)], axis=0)
    q_parts = lax.optimization_barrier(q_parts + (u_a, u_b, c_own))[:4]
    c_two = jnp.concatenate([c_own, to_z(c_own)], axis=0)
    c_core = to_core(c_two)
    qkv_w, normed_one, qkv, attn, attn_low, lse, gains = call(
        attend_kernel,
        (shape((D, WQ)), shape((N, D)), shape((N, 3 * HT)), shape((N, HT), F32), shape((N, HT)), shape((N, 4), F32), shape((8, D), F32)),
        [SMEM] + [VMEM] * 6 + [ANY] * 4, (ids, x_two, x_core, v_two, cs, sn, bias, *q_parts),
        [pltpu.SemaphoreType.DMA((32,))])
    a_two = jnp.concatenate([attn_low, to_z(after_these(attn_low, c_two))], axis=0)
    o_two = jnp.concatenate([o_own, o_first], axis=0)
    o_core = to_core(after_these(o_two, attn_low))
    u_parts = (u_a, to_y(u_a), u_b, to_x(u_b))
    a_core = to_core(a_two)
    attn_full, after, normed_two, out_w = call(
        after_kernel, (shape((N, D)), shape((M, D), F32), shape((N, D)), shape((HT, D))),
        [SMEM] + [VMEM] * 5 + [ANY] * 2, (ids, x_two, x_core, a_two, a_core, gains, o_two, o_core),
        [pltpu.VMEM((D, D), BF16), pltpu.SemaphoreType.DMA((32,))])
    block = (2, 6 * ROWS, 2 * FT)
    out_keep, out_send, r_keep, r_send, gain_two_g, a_keep, a_send, b_keep, b_send = call(
        feed_kernel, (shape((HALF, D)),) * 4 + (shape((1, D), F32),) + (shape(block),) * 4,
        [SMEM] + [VMEM] * 4 + [ANY] * 4, (ids, normed_two, gains, c_two, c_core, *u_parts),
        [pltpu.VMEM((D, 2 * FT), BF16), pltpu.VMEM((8 * FROWS, D), BF16), pltpu.VMEM((8 * FROWS, D), F32), pltpu.VMEM((8, 2 * ROWS, 2 * FT), BF16),
         pltpu.VMEM((N, FT), BF16), pltpu.VMEM((N, 2 * FT), BF16), pltpu.VMEM((HT, 2 * FT), F32),
         pltpu.SemaphoreType.DMA((32,)), pltpu.SemaphoreType.DMA((8,))], mib=48)

    r_core = to_core(r_send)
    u_sums = (a_keep, to_y(a_send), b_keep, to_x(b_send))

    def middle(r_keep, r_core, after, gains, c_two, out_keep, o_core):
        kept, sent = call(fold_kernel, (shape((M, D), F32), shape((M, D))), [VMEM] * 2, (r_keep, r_core))
        grad_after, branch = call(branch_kernel, (shape((M, D), F32), shape((M, D))), [VMEM] * 5, (kept, to_z(sent), after, gains, c_two))
        b_two = jnp.concatenate([branch, to_z(branch)], axis=0)
        o_kept, o_sent = call(fold_kernel, (shape((M, D), F32), shape((M, D))), [VMEM] * 2, (out_keep, after_these(o_core, branch)))
        return grad_after, b_two, to_core(b_two), o_kept, o_sent

    grad_after, b_two, b_core, o_kept, o_sent = fenced(
        middle, r_keep, after_these(r_core, a_send), after, gains, c_two, out_keep, to_core(out_send))

    def second_sum(a_own, a_send, b_own, b_send):
        return a_own, a_send, call(sum_second_kernel, shape(b_own.shape), [VMEM] * 2, (b_own, to_y(b_send)))

    def first_sum(sums):
        return call(sum_first_kernel, (shape(sums[0].shape[1:]),) * 4, [VMEM] * 4, sums)

    u_sums = first_sum(lax.optimization_barrier(u_sums + (b_core,))[:4])
    b_core = after_these(b_core, u_sums[3])
    def attend_back(o_sent, *inputs):
        o_moved = to_z(o_sent)
        block = (2, 4 * ROWS + 40, WQ)
        return (o_moved,) + tuple(call(
            attend_back_kernel, (shape((HALF, D)), shape((HALF, D + HT)), shape((HALF, HT))) + (shape(block),) * 4,
            [SMEM] + [VMEM] * 14, (ids,) + inputs,
            [pltpu.VMEM((N, HT), BF16), pltpu.VMEM((N, HT), F32), pltpu.VMEM((N, HT), F32), pltpu.VMEM((N, 3 * HT), BF16),
             pltpu.VMEM((HT, D), F32), pltpu.VMEM((8, D), F32), pltpu.VMEM((HT, WQ), F32)], mib=60))

    o_moved, r_keep, r_send, dv_keep, a_keep, a_send, b_keep, b_send = fenced(
        attend_back, o_sent, b_two, b_core, out_w, qkv, attn, lse, bias, cs, sn, qkv_w, normed_one, gains, gain_two_g, attn_full)
    u_sums = second_sum(*u_sums)
    r_send = after_these(r_send, u_sums[2])
    y_own, y_send = call(result_kernel, (shape((L, D)), shape((L, D))), [VMEM] * 3, (o_kept, o_moved, after))
    layer_out = call(result_home_kernel, shape((2, L, D)), [SMEM] + [VMEM] * 2, (ids, y_own, to_h(y_send)))
    r_core = to_core(r_send)
    kept, sent = call(fold_both_kernel, (shape((M, D), F32), shape((M, D + 2 * HT))), [VMEM] * 3, (r_keep, dv_keep, r_core))
    a_send, b_send, _ = lax.optimization_barrier((a_send, b_send, sent))
    q_sums = (a_keep, to_y(a_send), b_keep, to_x(b_send))
    own, sent = call(input_kernel, (shape((L, 2 * D)), shape((L, 2 * D))), [SMEM] + [VMEM] * 7,
                     (ids, kept, to_z(sent), x_two, gains, grad_after, dv_keep, r_core), [pltpu.VMEM((M, 2 * D), BF16)])
    home = to_h(sent)
    input_grad, v1_out = call(home_kernel, (shape((2, L, D), F32),) * 2, [SMEM] + [VMEM] * 3, (ids, own, home, v1_acc))

    def finish(kernel, sums, rest, first=(), last=()):
        a_own, a_send, b_send = sums
        dims = a_own.shape
        kept, sent, rows = call(kernel, (shape((2, ROWS, dims[1])), shape((2, ROWS, dims[1])), shape(rest, F32)), [SMEM] + [VMEM] * 3,
                                (ids, a_own, to_x(a_send), after_these(to_h(b_send), *first)), [pltpu.VMEM(dims, F32)])
        first = to_z(sent)
        return (ids, kept, first, to_core(pair_of(kept, after_these(first, *last)))), rows

    a_own, a_send, b_own, b_send = first_sum(q_sums)
    q_sums = second_sum(a_own, a_send, after_these(b_own, home), b_send)
    parts, down_g = finish(sum_hidden_kernel, u_sums, (FROWS, D))
    gate_g, up_g = call(join_hidden_kernel, (shape((ROWS, 4 * FT), F32),) * 2, [SMEM] + [VMEM] * 3, parts,
                        [pltpu.VMEM((4, ROWS, 2 * FT), F32)])
    parts, out_g = finish(sum_qkv_kernel, q_sums, (ROWS, D), (gate_g,), (input_grad,))
    query_g, key_g, value_g, gain_g = call(
        join_qkv_kernel, (shape((ROWS, D), F32),) * 3 + (shape((ROWS, 128), F32),), [SMEM] + [VMEM] * 3, parts)
    return (layer_out, input_grad, v1_out, gain_g[:, 0], query_g, key_g, value_g, out_g, gain_g[:, 1], gate_g, up_g, down_g)


def local(plan, layer_in, *rest):
    kept = plan.G == FAST_G and plan.T == FAST_T and layer_in.shape == (2, FAST_L, D) and rest[12].shape == (FROWS, D)
    return (fast if kept else general)(plan, layer_in, *rest)


def solution(mesh):
    plan = Plan(mesh.shape["gx"], mesh.shape["gy"])
    tokens, rows, vector = P(None, ALL, None), P(ALL, None), P(ALL)
    return jax.shard_map(
        functools.partial(local, plan),
        mesh=mesh,
        in_specs=(tokens, tokens, tokens, tokens, P(), vector, rows, rows, rows, rows, vector, rows, rows, rows),
        out_specs=(tokens, tokens, tokens, vector, rows, rows, rows, rows, vector, rows, rows, rows),
        check_vma=False,
    )
```

```python
import functools

import jax
import jax.numpy as jnp
from jax import lax
from jax.experimental import pallas as pl
from jax.experimental.pallas import tpu as pltpu
from jax.sharding import PartitionSpec as P

H = 16
EPS = 1e-05
NEG = -1e30
SCALE = 0.125
ALL = ("gx", "gy")
F32 = jnp.float32
BF16 = jnp.bfloat16


class Plan:
    def __init__(self, n_gx, n_gy):
        self.G, self.T = n_gx, n_gy // 2
        every = [(g, h, t) for g in range(self.G) for h in range(2) for t in range(self.T)]
        at = lambda g, h, t: g * n_gy + h * self.T + t
        self.g_swap = {k: [(at(g, h, t), at(g ^ k, h, t)) for g, h, t in every] for k in range(1, self.G)}
        self.t_swap = {k: [(at(g, h, t), at(g, h, t ^ k)) for g, h, t in every] for k in range(1, self.T)}
        self.h_swap = [(at(g, h, t), at(g, 1 - h, t)) for g, h, t in every]
        self.bits = []
        bit = self.T // 2
        while bit:
            self.bits.append(bit)
            bit //= 2


def pick(array, index, axis=0):
    return lax.dynamic_index_in_dim(array, index, axis, keepdims=False)


def send(array, pairs):
    return lax.ppermute(array, ALL, pairs)


def dot(a, b):
    return lax.dot_general(a, b, (((1,), (0,)), ((), ())), preferred_element_type=F32)


def dot_rows(a, b):
    return lax.dot_general(a, b, (((0,), (0,)), ((), ())), preferred_element_type=F32)


def dot_cols(a, b):
    return lax.dot_general(a, b, (((1,), (1,)), ((), ())), preferred_element_type=F32)


def rotate(values, cosine, sine):
    half = values.shape[-1] // 2
    a, b = values[..., :half], values[..., half:]
    return jnp.concatenate([a * cosine - b * sine, b * cosine + a * sine], axis=-1)


def general(plan, layer_in, first_layer_value, v1_acc, cotangent, seq_starts, norm1_gain, w_query, w_key, w_value,
          w_out, norm2_gain, w_gate, w_up, w_down):
    G, T, bits = plan.G, plan.T, plan.bits
    micro, L, D = layer_in.shape
    FF = w_gate.shape[1]
    HT, FT, heads = D // T, FF // T, H // T
    HD = D // H
    M = 2 * L
    N = T * M
    rows, frows = w_query.shape[0], w_down.shape[0]
    g, gy = lax.axis_index("gx"), lax.axis_index("gy")
    h, t = gy // T, gy % T

    def to_t(array, bit):
        return send(array, plan.t_swap[bit])

    def to_g(array, k):
        return send(array, plan.g_swap[k]) if k else array

    def to_h(array):
        return send(array, plan.h_swap)

    def inward(array):
        return jnp.concatenate([pick(array, h), to_h(pick(array, 1 - h))], axis=0)

    def outward(array):
        own, other = array[:L], to_h(array[L:])
        return jnp.stack([jnp.where(h == 0, own, other), jnp.where(h == 0, other, own)])

    def gather_t(array):
        parts = {0: array}
        for bit in bits:
            order = sorted(parts)
            moved = to_t(jnp.concatenate([parts[j] for j in order], axis=0), bit)
            size = array.shape[0]
            for i, j in enumerate(order):
                parts[j ^ bit] = moved[i * size:(i + 1) * size]
        return [parts[j] for j in range(T)]

    def reduce_t(partial):
        blocks = partial.reshape((T, -1) + partial.shape[1:])
        for bit in reversed(bits):
            shape = blocks.shape
            split = blocks.reshape((shape[0] // 2, 2) + shape[1:])
            blocks = split[:, 0] + to_t(split[:, 1].astype(BF16), bit).astype(F32)
        return blocks[0]

    def exchange_t(parts):
        held = {j: [parts[j]] for j in range(T)}
        sources = [0]
        for bit in bits:
            out = [j for j in sorted(held) if j & bit]
            flat = [p for j in out for p in held[j]]
            moved = to_t(jnp.stack(flat), bit)
            n = len(sources)
            new = {}
            for i, j in enumerate(out):
                new[j ^ bit] = held[j ^ bit] + [moved[i * n + s] for s in range(n)]
            sources = sources + [s ^ bit for s in sources]
            held = new
        result = [None] * T
        for s, p in zip(sources, held[0]):
            result[s] = p
        return result

    def natural(parts):
        array = jnp.stack(parts)
        for bit in bits:
            split = array.reshape((-1, 2, bit) + array.shape[1:])
            array = jnp.where((t & bit) != 0, split[:, ::-1], split).reshape(array.shape)
        return array

    def gather_r(block):
        other = to_h(block)
        pair = jnp.where(h == 0, jnp.stack([block, other]), jnp.stack([other, block]))
        full = jnp.zeros((G,) + pair.shape, pair.dtype)
        for k in range(G):
            full = lax.dynamic_update_slice(full, to_g(pair, k)[None], (g ^ k,) + (0,) * pair.ndim)
        return full.reshape((G * 2 * block.shape[0],) + block.shape[1:])

    def gather_cols(slices):
        block = natural(exchange_t([pick(slices, t ^ j) for j in range(T)]))
        return gather_r(block.reshape(T * block.shape[1], -1))

    def reduce_r(grad):
        n, w = grad.shape[0] // (2 * G), grad.shape[1]
        grad = grad.astype(BF16).reshape(G, 2 * n, w)
        total = pick(grad, g).astype(F32)
        for k in range(1, G):
            total = total + to_g(pick(grad, g ^ k), k).astype(F32)
        total = total.reshape(2, n, w)
        return pick(total, h) + to_h(pick(total, 1 - h).astype(BF16)).astype(F32)

    def scatter_cols(grad):
        total = reduce_r(grad).reshape(T, rows, -1)
        low = total.astype(BF16)
        return natural(exchange_t([pick(low, t ^ j) for j in range(T)])).astype(F32)

    pad = jnp.zeros((rows, 126), BF16)
    gains_in = jnp.concatenate([norm1_gain[:, None], norm2_gain[:, None], pad], axis=1)

    def col_slices(w):
        return w.reshape(rows, T, HT).transpose(1, 0, 2)

    def hidden_slices(w):
        return w.reshape(rows, 2 * G, T, frows).transpose(2, 0, 1, 3).reshape(T, rows, FT)

    qkv_slices = jnp.concatenate([col_slices(w_query), col_slices(w_key), col_slices(w_value),
                                  jnp.broadcast_to(gains_in[None], (T, rows, 128))], axis=2)
    x_own = inward(layer_in)
    qkv_w = gather_cols(qkv_slices)
    x_all = jnp.concatenate(gather_t(x_own), axis=0)
    v_own = inward(first_layer_value).reshape(M, T, HT).transpose(1, 0, 2)
    v_all = jnp.concatenate(exchange_t([pick(v_own, t ^ j) for j in range(T)]), axis=0)
    gu_w = gather_cols(jnp.concatenate([hidden_slices(w_gate), hidden_slices(w_up)], axis=2))
    down_w = gather_r(w_down)
    c_own = inward(cotangent)
    c_all = jnp.concatenate(gather_t(c_own), axis=0)
    out_w = natural(gather_t(gather_r(w_out))).reshape(T, 2 * G, rows, D).transpose(1, 0, 2, 3).reshape(D, D)
    out_w = out_w.reshape(T, HT, D)

    gains = qkv_w[:, 3 * HT:3 * HT + 2].astype(F32).T
    gain_one, gain_two = gains[0], gains[1]
    query_w, key_w, value_w = qkv_w[:, :HT], qkv_w[:, HT:2 * HT], qkv_w[:, 2 * HT:3 * HT]
    gate_w, up_w = gu_w[:, :FT], gu_w[:, FT:]

    starts = pick(seq_starts, h)
    member = t ^ jnp.arange(T, dtype=jnp.int32)
    half = h ^ jnp.arange(2, dtype=jnp.int32)
    position = ((half[None, :] * T + member[:, None]) * L)[:, :, None] + jnp.arange(L, dtype=jnp.int32)
    position = position.reshape(N) + g * N
    begin = jnp.max(jnp.where(starts[None, :] <= position[:, None], starts[None, :], 0), axis=1)
    rel = (position - begin).astype(F32)
    visible = (begin[:, None] == begin[None, :]) & (position[None, :] <= position[:, None])
    frequency = 10000.0 ** (-(jnp.arange(HD // 2, dtype=F32) * 2.0 / HD))
    angles = rel[:, None] * frequency[None, :]
    cosine, sine = jnp.cos(angles)[:, None, :], jnp.sin(angles)[:, None, :]

    x = x_all.astype(F32)
    rstd_one = lax.rsqrt(jnp.mean(x * x, axis=-1, keepdims=True) + EPS)
    normed_one = (x * rstd_one * gain_one).astype(BF16)
    query = rotate(dot(normed_one, query_w).reshape(N, heads, HD), cosine, sine).astype(BF16)
    key = rotate(dot(normed_one, key_w).reshape(N, heads, HD), cosine, sine).astype(BF16)
    value = (0.5 * dot(normed_one, value_w) + 0.5 * v_all.astype(F32)).astype(BF16).reshape(N, heads, HD)
    scores = jnp.einsum("ihd,jhd->hij", query, key, preferred_element_type=F32) * SCALE
    scores = jnp.where(visible[None], scores, NEG)
    top = jnp.max(scores, axis=-1, keepdims=True)
    probs = jnp.exp(scores - top)
    denom = jnp.sum(probs, axis=-1, keepdims=True)
    probs = probs / denom
    probs_low = probs.astype(BF16)
    attn = jnp.einsum("hij,jhd->ihd", probs_low, value, preferred_element_type=F32)
    attn_low = attn.reshape(N, HT).astype(BF16)
    attn_parts = []
    for j, part in enumerate(gather_t(attn_low)):
        part = part.reshape(T, M, HT)
        attn_parts.append(jnp.concatenate([part[b ^ j] for b in range(T)], axis=0))
    after = x
    for j in range(T):
        after = after + dot(attn_parts[j], pick(out_w, t ^ j))
    rstd_two = lax.rsqrt(jnp.mean(after * after, axis=-1, keepdims=True) + EPS)
    hat_two = after * rstd_two
    normed_two = (hat_two * gain_two).astype(BF16)
    gate = dot(normed_two, gate_w)
    up = dot(normed_two, up_w)
    sig = jax.nn.sigmoid(gate)
    act = gate * sig
    hidden = (act * up).astype(BF16)

    grad_hidden = dot_cols(c_all, down_w)
    grad_gate = (grad_hidden * up * (sig * (1.0 + gate * (1.0 - sig)))).astype(BF16)
    grad_up = (grad_hidden * act).astype(BF16)
    grad_two_part = dot_cols(grad_gate, gate_w) + dot_cols(grad_up, up_w)
    gain_two_grad = jnp.sum(grad_two_part * hat_two, axis=0)
    grad_two = reduce_t(grad_two_part) * gain_two
    hat_own = hat_two[:M]
    grad_after = c_own.astype(F32) + rstd_two[:M] * (
        grad_two - hat_own * jnp.mean(grad_two * hat_own, axis=-1, keepdims=True))
    grad_branch = jnp.concatenate(gather_t(grad_after.astype(BF16)), axis=0)
    result = reduce_t(dot(hidden, down_w)) + after[:M]
    layer_out = outward(result.astype(BF16))
    grad_down = dot_rows(hidden, c_all)
    grad_gu = dot_rows(normed_two, jnp.concatenate([grad_gate, grad_up], axis=1))

    grad_attn = dot_cols(grad_branch, pick(out_w, t)).astype(BF16).reshape(N, heads, HD)
    delta = jnp.sum(grad_attn.astype(F32) * attn, axis=-1).T
    grad_probs = jnp.einsum("ihd,jhd->hij", grad_attn, value, preferred_element_type=F32)
    grad_scores = (probs * (grad_probs - delta[..., None])).astype(BF16)
    grad_query = jnp.einsum("hij,jhd->ihd", grad_scores, key, preferred_element_type=F32) * SCALE
    grad_key = jnp.einsum("hij,ihd->jhd", grad_scores, query, preferred_element_type=F32) * SCALE
    grad_blend = jnp.einsum("hij,ihd->jhd", probs_low, grad_attn, preferred_element_type=F32).reshape(N, HT)
    grad_query = rotate(grad_query, cosine, -sine).reshape(N, HT).astype(BF16)
    grad_key = rotate(grad_key, cosine, -sine).reshape(N, HT).astype(BF16)
    grad_value = (0.5 * grad_blend).astype(BF16)
    grad_one_part = dot_cols(grad_query, query_w) + dot_cols(grad_key, key_w) + dot_cols(grad_value, value_w)
    hat_one = x * rstd_one
    gain_one_grad = jnp.sum(grad_one_part * hat_one, axis=0)
    grad_one = reduce_t(grad_one_part) * gain_one
    hat_own = hat_one[:M]
    input_grad = grad_after + rstd_one[:M] * (
        grad_one - hat_own * jnp.mean(grad_one * hat_own, axis=-1, keepdims=True))
    input_grad = outward(input_grad.astype(BF16)).astype(F32)
    v_parts = natural(exchange_t([grad_value[j * M:(j + 1) * M] for j in range(T)]))
    v1_out = v1_acc + outward(v_parts.transpose(1, 0, 2).reshape(M, D)).astype(F32)

    attn_full = natural([p.T for p in attn_parts]).reshape(2 * G, T, rows, N)
    grad_out = dot(pick(attn_full, t, 1).reshape(2 * G * rows, N), grad_branch)
    grad_gains = jnp.stack([gain_one_grad, gain_two_grad], axis=1)
    grad_gains = jnp.concatenate([grad_gains, jnp.zeros((D, 126), F32)], axis=1)
    grad_qkv = dot_rows(normed_one, jnp.concatenate([grad_query, grad_key, grad_value], axis=1))
    down_g = reduce_r(grad_down)
    gu_g = scatter_cols(grad_gu)
    out_g = reduce_r(grad_out)
    qkv_g = scatter_cols(jnp.concatenate([grad_qkv, grad_gains], axis=1))

    def col_join(parts):
        return parts.transpose(1, 0, 2).reshape(rows, D)

    def hidden_join(parts):
        return parts.reshape(T, rows, 2 * G, frows).transpose(1, 2, 0, 3).reshape(rows, FF)

    gain_g = jnp.sum(qkv_g[:, :, 3 * HT:3 * HT + 2], axis=0)
    return (layer_out, input_grad, v1_out, gain_g[:, 0], col_join(qkv_g[:, :, :HT]), col_join(qkv_g[:, :, HT:2 * HT]),
            col_join(qkv_g[:, :, 2 * HT:3 * HT]), out_g, gain_g[:, 1], hidden_join(gu_g[:, :, :FT]),
            hidden_join(gu_g[:, :, FT:]), down_g)


FAST_G, FAST_T, FAST_L, D, HT, FT, FROWS, ROWS = 4, 4, 64, 1024, 256, 704, 88, 32
M, N = 2 * FAST_L, 8 * FAST_L
HALF = N // 2
WQ = 3 * HT + 128
ORDER = (0, 2, 1, 3)
HD = 64
ARRIVED = ((0, 0), (1, 0), (2, 0), (3, 0), (0, 1), (2, 1), (1, 1), (3, 1))
LEAVING = {(0, 0): (0, 0), (1, 0): (0, 1), (2, 0): (1, 0), (3, 0): (1, 1), (0, 1): (2, 0), (2, 1): (2, 1), (1, 1): (3, 0), (3, 1): (3, 1)}
VMEM = pl.BlockSpec(memory_space=pltpu.VMEM)
SMEM = pl.BlockSpec(memory_space=pltpu.SMEM)
ANY = pl.BlockSpec(memory_space=pltpu.HBM)


def shape(dims, dtype=BF16):
    return jax.ShapeDtypeStruct(dims, dtype)


def call(kernel, outs, specs, args, scratch=(), mib=40):
    return pl.pallas_call(
        kernel,
        out_shape=outs,
        in_specs=specs,
        out_specs=jax.tree.map(lambda _: VMEM, outs),
        scratch_shapes=list(scratch),
        compiler_params=pltpu.CompilerParams(vmem_limit_bytes=mib << 20),
        cost_estimate=pl.CostEstimate(flops=1, bytes_accessed=1, transcendentals=0),
    )(*args)


def aligned(index, size):
    return pl.ds(pl.multiple_of(index * size, size), size)


def eye(rows, lanes):
    return (lax.broadcasted_iota(jnp.int32, (rows, lanes), 0) == lax.broadcasted_iota(jnp.int32, (rows, lanes), 1)).astype(BF16)


def tiles_in(block):
    lines = [jnp.concatenate([block[j * 8:j * 8 + 8, i * 128:i * 128 + 128] for j in range(11)], axis=1) for i in range(8)]
    return jnp.concatenate(lines, axis=0)


def tiles_out(block):
    lines = [jnp.concatenate([block[i * 8:i * 8 + 8, j * 128:j * 128 + 128] for i in range(8)], axis=1) for j in range(11)]
    return jnp.concatenate(lines, axis=0)


def line_tiles_in(block):
    tiles = [block[j * 8:j * 8 + 8, i * 128:i * 128 + 128] for j in range(4) for i in range(8)]
    tiles += [jnp.zeros_like(tiles[0])] * 3
    return jnp.concatenate([jnp.concatenate(tiles[n * 7:n * 7 + 7], axis=1) for n in range(5)], axis=0)


def line_tiles_out(block):
    tiles = [block[n * 8:n * 8 + 8, i * 128:i * 128 + 128] for n in range(5) for i in range(7)]
    return jnp.concatenate([jnp.concatenate(tiles[j * 8:j * 8 + 8], axis=1) for j in range(4)], axis=0)


def pack_first(ids, gain_one, gain_two, wq, wk, wv, wo, x, v, c, out, keep, lines, xv_out, c_out, rows, whole, sem):
    h, t = ids[1], ids[2]
    copies = []
    for j in (2, 3, 0, 1):
        to = keep if j < 2 else out
        for i, w in enumerate((wq, wk, wv)):
            copies.append((w.at[:, aligned(t ^ j, HT)], to.at[j % 2, :, i * HT:(i + 1) * HT]))
    copies += [(wo, whole), (x.at[1 - h], xv_out.at[:, :D]), (v.at[1 - h], xv_out.at[:, D:]), (c.at[1 - h], c_out)]
    started = fetch(copies, sem)
    rows[...] = jnp.zeros_like(rows)
    rows[0:1] = gain_one[...].astype(F32)
    rows[1:2] = gain_two[...].astype(F32)
    gains = dot_rows(rows[...].astype(BF16), eye(8, 128)).astype(BF16)
    for j in range(4):
        (keep if j < 2 else out)[j % 2, :, 3 * HT:] = gains
    started[12].wait()
    lines[...] = line_tiles_in(whole[...].astype(F32)).astype(BF16)
    for n, copy in enumerate(started):
        if n != 12:
            copy.wait()


def pack_hidden(ids, wg, wu, wd, keep, out, down, nat, gate, up, whole, sem):
    t = ids[2]
    started = fetch([(wg, gate), (wu, up), (wd, whole)], sem)
    for a, w in enumerate((gate, up)):
        started[a].wait()
        for m in range(4):
            for i in range(8):
                at, to = (i * 4 + m) * FROWS, a * FT + i * FROWS
                nat[m, :, to:to + FROWS] = w[:, at:at + FROWS].astype(F32)
    for j in range(4):
        to = keep if j < 2 else out
        to[j % 2] = nat[t ^ j].astype(BF16)
    started[2].wait()
    down[...] = tiles_in(whole[...].astype(F32)).astype(BF16)


def pack_block(kept, first, last, tail, out, sem):
    width = ROWS
    parts = (kept.at[0], first.at[0], last.at[0], last.at[1], tail)
    started = fetch([(part, out.at[i * width:i * width + part.shape[0]]) for i, part in enumerate(parts)], sem)
    for copy in started:
        copy.wait()


def pack_pair(kept, first, out, sem):
    started = fetch([(kept.at[1], out.at[0]), (first.at[1], out.at[1])], sem)
    for copy in started:
        copy.wait()


def pack_out(b0, b1, b2, b3, out, raw, sem):
    started = fetch([((b0, b1, b2, b3)[n // 2].at[n % 2, 4 * ROWS:], raw.at[n]) for n in range(8)], sem)
    for n in range(8):
        started[n].wait()
        out[n * ROWS:(n + 1) * ROWS] = line_tiles_out(raw[n].astype(F32)).astype(BF16)


def pack_second(ids, x, v, moved, xv_out, v_keep, own, sem):
    h, t = ids[1], ids[2]
    started = fetch([(x.at[h], xv_out.at[:FAST_L, :D]), (v.at[h], own.at[:FAST_L]),
                     (moved.at[:, :D], xv_out.at[FAST_L:, :D]), (moved.at[:, D:], own.at[FAST_L:])], sem)
    for copy in started:
        copy.wait()
    for j in range(2):
        v_keep[j] = own[:, aligned(t ^ j, HT)]
        xv_out[:, D + j * HT:D + (j + 1) * HT] = own[:, aligned(t ^ (j + 2), HT)]


def pack_third(mine, moved, v_keep, out, v_two):
    out[:M, :D] = mine[:, :D]
    out[M:, :D] = moved[:, :D]
    out[:M, D:] = v_keep[1]
    out[M:, D:] = moved[:, D + HT:]
    v_two[:M] = v_keep[0]
    v_two[M:] = moved[:, D:D + HT]


def fetch(copies, sem):
    started = []
    for i, (source, target) in enumerate(copies):
        copy = pltpu.make_async_copy(source, target, sem.at[i])
        copy.start()
        started.append(copy)
    return started


def swap_halves(u):
    width = u.shape[-1]
    lane = lax.broadcasted_iota(jnp.int32, u.shape, 1)
    up = pltpu.roll(u, width - HD // 2, 1)
    down = pltpu.roll(u, HD // 2, 1)
    return jnp.where(lane % HD < HD // 2, up, down)


def scale_of(x):
    return lax.rsqrt(jnp.mean(x * x, axis=-1, keepdims=True) + EPS)


def attend_kernel(ids, x2, xc, v2, cs, sn, bias, b0, b1, b2, b3, w, normed, qkv, attn, low, lse, gains, sem):
    g, h, t = ids[0], ids[1], ids[2]
    copies = []
    for n, (k, dh) in enumerate(ARRIVED):
        b = (b0, b1, b2, b3)[n // 2]
        for i, s in enumerate(ORDER):
            row = ((g ^ k) * 2 + (h ^ dh)) * 4 + (t ^ s)
            copies.append((b.at[n % 2, i * ROWS:(i + 1) * ROWS], w.at[aligned(row, ROWS)]))
    for copy in fetch(copies, sem):
        copy.wait()
    gains[...] = dot_cols(eye(8, 128), w[:, 3 * HT:])
    gain = gains[0:1, :]
    for b in range(2):
        rows = slice(b * HALF, (b + 1) * HALF)
        source = x2 if b == 0 else xc
        x = source[:, :D].astype(F32)
        r = (x * scale_of(x) * gain).astype(BF16)
        normed[rows] = r
        out = dot(r, w[:, :3 * HT])
        for i in range(2):
            u = out[:, i * HT:(i + 1) * HT]
            qkv[rows, i * HT:(i + 1) * HT] = (u * cs[rows] + swap_halves(u) * sn[rows]).astype(BF16)
        value = v2[...] if b == 0 else xc[:, D:]
        qkv[rows, 2 * HT:] = (0.5 * out[:, 2 * HT:] + 0.5 * value.astype(F32)).astype(BF16)
    for b in range(2):
        rows = slice(b * HALF, (b + 1) * HALF)
        outs, tops = [], []
        for i in range(4):
            lanes = slice(i * HD, (i + 1) * HD)
            q = qkv[rows, lanes]
            k = qkv[:, HT + i * HD:HT + (i + 1) * HD]
            v = qkv[:, 2 * HT + i * HD:2 * HT + (i + 1) * HD]
            s = dot_cols(q, k) * SCALE + bias[rows].astype(F32)
            top = jnp.max(s, axis=-1, keepdims=True)
            p = jnp.exp(s - top)
            total = jnp.sum(p, axis=-1, keepdims=True)
            outs.append(dot(p.astype(BF16), v) / total)
            tops.append(top + jnp.log(total))
        o = jnp.concatenate(outs, axis=1)
        attn[rows] = o
        low[rows] = o.astype(BF16)
        lse[rows] = jnp.concatenate(tops, axis=1)


def after_kernel(ids, x2, xc, o2, oc, gains, co2, coc, full, after, normed, own_w, w, sem):
    g, h, t = ids[0], ids[1], ids[2]
    copies = []
    for i, s in enumerate(ORDER):
        source = co2 if i < 2 else coc
        for n, (k, dh) in enumerate(ARRIVED):
            row = ((g ^ k) * 2 + (h ^ dh)) * 4 + (t ^ s)
            at = (i % 2) * HT + n * ROWS
            copies.append((source.at[at:at + ROWS], w.at[aligned(row, ROWS)]))
    started = fetch(copies, sem)
    for i, s in enumerate(ORDER):
        source = o2 if i < 2 else oc
        for p in range(4):
            q = ORDER.index(ORDER[p] ^ s)
            full[p * M:(p + 1) * M, aligned(t ^ s, HT)] = source[(i % 2) * N + q * M:(i % 2) * N + (q + 1) * M]
    for copy in started:
        copy.wait()
    own_w[...] = w[aligned(t, HT)]
    gain = gains[1:2, :]
    for b in range(2):
        rows = slice(b * HALF, (b + 1) * HALF)
        source = x2 if b == 0 else xc
        a = source[:, :D].astype(F32) + dot(full[rows], w[...])
        if b == 0:
            after[...] = a[:M]
        normed[rows] = (a * scale_of(a) * gain).astype(BF16)


def feed_kernel(ids, normed, gains, c2, cc, u0, u1, u2, u3, out_keep, out_send, r_keep, r_send, gain_g, a_keep, a_send, b_keep, b_send,
                w, wd, wide, raw, hidden, dgu, gu_g, sem, sem_d):
    g, h, t = ids[0], ids[1], ids[2]
    copies, copies_d = [], []
    for n, (k, dh) in enumerate(ARRIVED):
        b = (u0, u1, u2, u3)[n // 2]
        for i, s in enumerate(ORDER):
            row = ((g ^ k) * 2 + (h ^ dh)) * 4 + (t ^ s)
            copies.append((b.at[n % 2, i * ROWS:(i + 1) * ROWS], w.at[aligned(row, ROWS)]))
        copies_d.append((b.at[n % 2, 4 * ROWS:], raw.at[n]))
    started_d, started = fetch(copies_d, sem_d), fetch(copies, sem)
    for n, (k, dh) in enumerate(ARRIVED):
        started_d[n].wait()
        wide[aligned((g ^ k) * 2 + (h ^ dh), FROWS)] = tiles_out(raw[n].astype(F32))
    wd[...] = wide[...].astype(BF16)
    for copy in started:
        copy.wait()
    gain_sum = jnp.zeros((1, D), F32)
    for b in range(2):
        rows = slice(b * HALF, (b + 1) * HALF)
        c = (c2 if b == 0 else cc)[...]
        gu = dot(normed[rows], w[...])
        gate, up = gu[:, :FT], gu[:, FT:]
        sig = 1.0 / (1.0 + jnp.exp(-gate))
        act = gate * sig
        hid = (act * up).astype(BF16)
        hidden[rows] = hid
        dh = dot_cols(c, wd[...])
        dgu[rows, :FT] = (dh * up * (sig * (1.0 + gate * (1.0 - sig)))).astype(BF16)
        dgu[rows, FT:] = (dh * act).astype(BF16)
        dr = dot_cols(dgu[rows], w[...])
        out = dot(hid, wd[...])
        gain_sum = gain_sum + jnp.sum(dr * normed[rows].astype(F32), axis=0, keepdims=True)
        (r_keep if b == 0 else r_send)[...] = dr.astype(BF16)
        (out_keep if b == 0 else out_send)[...] = out.astype(BF16)
    gain_g[...] = gain_sum / gains[1:2, :]
    wide[...] = dot_rows(hidden[:HALF], c2[...]) + dot_rows(hidden[HALF:], cc[...])
    for k in range(4):
        gu_g[...] = dot_rows(normed[:, aligned(g ^ k, HT)], dgu[...])
        for e in range(2):
            target, at = LEAVING[(k, e)]
            target = (a_keep, a_send, b_keep, b_send)[target]
            target[at, :4 * ROWS] = gu_g[aligned(h ^ e, 4 * ROWS)].astype(BF16)
            target[at, 4 * ROWS:] = tiles_in(wide[aligned((g ^ k) * 2 + (h ^ e), FROWS)]).astype(BF16)


def fold_kernel(keep, moved, kept, send):
    kept[...] = keep[:M].astype(F32) + moved[:M].astype(F32)
    send[...] = (keep[M:].astype(F32) + moved[M:].astype(F32)).astype(BF16)


def fold_both_kernel(keep, dv, moved, kept, send):
    kept[...] = keep[:M].astype(F32) + moved[:M, :D].astype(F32)
    send[:, :D] = (keep[M:].astype(F32) + moved[M:, :D].astype(F32)).astype(BF16)
    send[:, D:D + HT] = dv[M:]
    send[:, D + HT:] = moved[M:, D:]


def branch_kernel(keep, moved, after, gains, c2, grad_after, low):
    a = after[...]
    scale = scale_of(a)
    hat = a * scale
    dy = (keep[...] + moved[...].astype(F32)) * gains[1:2, :]
    d = c2[:M].astype(F32) + scale * (dy - hat * jnp.mean(dy * hat, axis=-1, keepdims=True))
    grad_after[...] = d
    low[...] = d.astype(BF16)


def attend_back_kernel(ids, da2, dac, wo, qkv, attn, lse, bias, cs, sn, w, normed, gains, gain_two, full,
                       r_keep, r_send, dv_keep, a_keep, a_send, b_keep, b_send, do, dk, dv, dqkv, scratch, rows_g, qkv_g):
    g, h, t = ids[0], ids[1], ids[2]
    for b in range(2):
        rows = slice(b * HALF, (b + 1) * HALF)
        do[rows] = dot_cols((da2 if b == 0 else dac)[...], wo[...]).astype(BF16)
    for b in range(2):
        rows = slice(b * HALF, (b + 1) * HALF)
        dqs = []
        for i in range(4):
            lanes = slice(i * HD, (i + 1) * HD)
            q = qkv[rows, lanes]
            k = qkv[:, HT + i * HD:HT + (i + 1) * HD]
            v = qkv[:, 2 * HT + i * HD:2 * HT + (i + 1) * HD]
            d = do[rows, lanes]
            delta = jnp.sum(d.astype(F32) * attn[rows, lanes], axis=-1, keepdims=True)
            p = jnp.exp(dot_cols(q, k) * SCALE + bias[rows].astype(F32) - lse[rows, i:i + 1])
            ds = (p * (dot_cols(d, v) - delta)).astype(BF16)
            dqs.append(dot(ds, k))
            dki, dvi = dot_rows(ds, q), dot_rows(p.astype(BF16), d)
            if b == 0:
                dk[:, lanes], dv[:, lanes] = dki, dvi
            else:
                dk[:, lanes], dv[:, lanes] = dk[:, lanes] + dki, dv[:, lanes] + dvi
        u = jnp.concatenate(dqs, axis=1) * SCALE
        dqkv[rows, :HT] = (u * cs[rows] - swap_halves(u) * sn[rows]).astype(BF16)
    gain_sum = jnp.zeros((1, D), F32)
    for b in range(2):
        rows = slice(b * HALF, (b + 1) * HALF)
        u = dk[rows] * SCALE
        dqkv[rows, HT:2 * HT] = (u * cs[rows] - swap_halves(u) * sn[rows]).astype(BF16)
        dqkv[rows, 2 * HT:] = (0.5 * dv[rows]).astype(BF16)
        dr = dot_cols(dqkv[rows], w[:, :3 * HT])
        gain_sum = gain_sum + jnp.sum(dr * normed[rows].astype(F32), axis=0, keepdims=True)
        if b == 0:
            r_keep[...] = dr.astype(BF16)
            dv_keep[...] = dqkv[rows, 2 * HT:]
        else:
            r_send[:, :D] = dr.astype(BF16)
            r_send[:, D:] = dqkv[rows, 2 * HT:]
    rows_g[...] = jnp.zeros_like(rows_g)
    rows_g[0:1] = gain_sum / gains[0:1, :]
    rows_g[1:2] = gain_two[...]
    for k in range(4):
        lanes = aligned(g ^ k, HT)
        qkv_g[:, :3 * HT] = dot_rows(normed[:, lanes], dqkv[...])
        qkv_g[:, 3 * HT:] = dot_rows(rows_g[:, lanes].astype(BF16), eye(8, 128))
        scratch[...] = dot_rows(full[:HALF, lanes], da2[...]) + dot_rows(full[HALF:, lanes], dac[...])
        for e in range(2):
            target, at = LEAVING[(k, e)]
            target = (a_keep, a_send, b_keep, b_send)[target]
            target[at, :4 * ROWS] = qkv_g[aligned(h ^ e, 4 * ROWS)].astype(BF16)
            target[at, 4 * ROWS:] = line_tiles_in(scratch[aligned((h ^ e) * 4 + t, ROWS)]).astype(BF16)


def sum_first_kernel(a_keep, a_moved, b_keep, b_moved, a_own, a_send, b_own, b_send):
    for keep, moved, own, out in ((a_keep, a_moved, a_own, a_send), (b_keep, b_moved, b_own, b_send)):
        own[...] = (keep[0].astype(F32) + moved[0].astype(F32)).astype(BF16)
        out[...] = (keep[1].astype(F32) + moved[1].astype(F32)).astype(BF16)


def sum_second_kernel(b_own, b_moved, b_send):
    b_send[...] = (b_own[...].astype(F32) + b_moved[...].astype(F32)).astype(BF16)


def sum_third(a_own, a_moved, moved, total):
    total[...] = (a_own[...].astype(F32) + a_moved[...].astype(F32)) + moved[...].astype(F32)


def sum_hidden_kernel(ids, a_own, a_moved, moved, kept, send, down, total):
    t = ids[2]
    sum_third(a_own, a_moved, moved, total)
    for j in range(4):
        (kept if j < 2 else send)[j % 2] = total[aligned(t ^ j, ROWS)].astype(BF16)
    down[...] = tiles_out(total[4 * ROWS:])


def sum_qkv_kernel(ids, a_own, a_moved, moved, kept, send, out, total):
    t = ids[2]
    sum_third(a_own, a_moved, moved, total)
    for j in range(4):
        (kept if j < 2 else send)[j % 2] = total[aligned(t ^ j, ROWS)].astype(BF16)
    out[...] = line_tiles_out(total[4 * ROWS:])


def join_qkv_kernel(ids, kept, first, last, q, k, v, gains):
    t = ids[2]
    parts = (kept[0], first[0], last[0], last[1])
    for s, part in zip(ORDER, parts):
        for i, ref in enumerate((q, k, v)):
            ref[:, aligned(t ^ s, HT)] = part[:, i * HT:(i + 1) * HT].astype(F32)
    low = [part[:, 3 * HT:].astype(F32) for part in parts]
    gains[...] = (low[0] + low[1]) + (low[2] + low[3])


def join_hidden_kernel(ids, kept, first, last, gate, up, nat):
    t = ids[2]
    for s, part in zip(ORDER, (kept[0], first[0], last[0], last[1])):
        nat[t ^ s] = part.astype(F32)
    for m in range(4):
        for a, ref in enumerate((gate, up)):
            for i in range(8):
                to, at = (i * 4 + m) * FROWS, a * FT + i * FROWS
                ref[:, to:to + FROWS] = nat[m, :, at:at + FROWS]


def input_kernel(ids, keep, moved, x2, gains, grad_after, dv, dv_core, own, send, both):
    t = ids[2]
    x = x2[:M, :D].astype(F32)
    scale = scale_of(x)
    hat = x * scale
    dy = (keep[...] + moved[:, :D].astype(F32)) * gains[0:1, :]
    both[:, :D] = (grad_after[...] + scale * (dy - hat * jnp.mean(dy * hat, axis=-1, keepdims=True))).astype(BF16)
    parts = (dv[:M], moved[:, D:D + HT], dv_core[:M, D:], moved[:, D + HT:])
    for s, part in zip(ORDER, parts):
        both[:, aligned(4 + (t ^ s), HT)] = part
    own[...] = both[:FAST_L]
    send[...] = both[FAST_L:]


def home_kernel(ids, own, moved, v1, grad, v_out):
    h = ids[1]
    grad[h] = own[:, :D].astype(F32)
    grad[1 - h] = moved[:, :D].astype(F32)
    v_out[h] = v1[h] + own[:, D:].astype(F32)
    v_out[1 - h] = v1[1 - h] + moved[:, D:].astype(F32)


def result_kernel(keep, moved, after, own, send):
    out = after[...] + (keep[...] + moved[...].astype(F32))
    own[...] = out[:FAST_L].astype(BF16)
    send[...] = out[FAST_L:].astype(BF16)


def result_home_kernel(ids, own, moved, out):
    h = ids[1]
    out[h] = own[...]
    out[1 - h] = moved[...]


def fast(plan, layer_in, first_layer_value, v1_acc, cotangent, seq_starts, norm1_gain, w_query, w_key, w_value,
         w_out, norm2_gain, w_gate, w_up, w_down):
    L = FAST_L
    g, gy = lax.axis_index("gx"), lax.axis_index("gy")
    h, t = gy // 4, gy % 4
    ids = jnp.stack([g, h, t]).astype(jnp.int32)

    def to_z(array):
        return send(array, plan.t_swap[2])

    def to_core(array):
        return send(array, plan.t_swap[1])

    def to_h(array):
        return send(array, plan.h_swap)

    def to_x(array):
        return send(array, plan.g_swap[1])

    def to_y(array):
        return send(array, plan.g_swap[2])

    def after_these(array, *others):
        return lax.optimization_barrier((array,) + others)[0]

    def fenced(part, *inputs):
        results = jax.eval_shape(part, *inputs)
        nothing = lambda *_: jax.tree.map(lambda a: jnp.zeros(a.shape, a.dtype), results)
        return lax.cond(ids[0] >= 0, part, nothing, *inputs)

    def spread(own, other, *first):
        a_pair = jnp.stack([own, to_x(own)])
        b_pair = jnp.stack([other, to_y(other)])
        a_pair, b_pair = lax.optimization_barrier((a_pair, b_pair) + first)[:2]
        return a_pair, to_y(a_pair), b_pair, to_x(b_pair)

    def pair_of(kept, first):
        return call(pack_pair, shape(kept.shape), [ANY] * 2, (kept, first), [pltpu.SemaphoreType.DMA((2,))])

    def block_of(kept, first, last, tail):
        return call(pack_block, shape((4 * ROWS + tail.shape[0], tail.shape[1])), [ANY] * 4, (kept, first, last, tail),
                    [pltpu.SemaphoreType.DMA((5,))])

    q_send, q_keep, o_block, xv_send, c_send = call(
        pack_first, (shape((2, ROWS, WQ)), shape((2, ROWS, WQ)), shape((40, WQ)), shape((L, 2 * D)), shape((L, D))),
        [SMEM] + [VMEM] * 2 + [ANY] * 7,
        (ids, norm1_gain[None], norm2_gain[None], w_query, w_key, w_value, w_out, layer_in, first_layer_value, cotangent),
        [pltpu.VMEM((8, ROWS), F32), pltpu.VMEM((ROWS, D), BF16), pltpu.SemaphoreType.DMA((16,))], mib=63)
    q_first = to_z(q_send)
    xv_moved = to_h(xv_send)
    q_last = to_core(pair_of(q_keep, q_first))
    q_block = block_of(q_keep, q_first, q_last, o_block)
    q_other = to_h(q_block)

    starts = pick(after_these(seq_starts, q_block), h)
    member = t ^ jnp.array(ORDER, jnp.int32)
    half = h ^ jnp.arange(2, dtype=jnp.int32)
    position = ((half[None, :] * 4 + member[:, None]) * L)[:, :, None] + jnp.arange(L, dtype=jnp.int32)
    position = position.reshape(N) + g * N
    begin = jnp.max(jnp.where(starts[None, :] <= position[:, None], starts[None, :], 0), axis=1)
    visible = (begin[:, None] == begin[None, :]) & (position[None, :] <= position[:, None])
    bias = jnp.where(visible, 0.0, NEG).astype(BF16)
    lane = jnp.arange(HT, dtype=jnp.int32)
    frequency = 10000.0 ** (-((lane % (HD // 2)).astype(F32) * 2.0 / HD))
    angles = (position - begin).astype(F32)[:, None] * frequency[None, :]
    cs = jnp.cos(angles)
    sn = jnp.sin(angles) * jnp.where(lane % HD < HD // 2, -1.0, 1.0)[None, :]

    u_keep, u_send, d_block = call(
        pack_hidden, (shape((2, ROWS, 2 * FT)), shape((2, ROWS, 2 * FT)), shape((2 * ROWS, 2 * FT))), [SMEM] + [ANY] * 3,
        (after_these(ids, q_send), w_gate, w_up, w_down),
        [pltpu.VMEM((4, ROWS, 2 * FT), F32), pltpu.VMEM((ROWS, 4 * FT), BF16), pltpu.VMEM((ROWS, 4 * FT), BF16), pltpu.VMEM((FROWS, D), BF16),
         pltpu.SemaphoreType.DMA((3,))], mib=63)
    u_first = to_z(u_send)
    u_last = to_core(pair_of(u_keep, after_these(u_first, q_block)))
    u_block = block_of(u_keep, u_first, u_last, d_block)

    xv_out, v_keep = call(pack_second, (shape((M, D + 2 * HT)), shape((2, M, HT))), [SMEM] + [ANY] * 3,
                          (after_these(ids, u_block), layer_in, first_layer_value, xv_moved), [pltpu.VMEM((M, D), BF16), pltpu.SemaphoreType.DMA((4,))], mib=63)
    x_two, v_two = call(pack_third, (shape((HALF, D + HT)), shape((HALF, HT))), [VMEM] * 3, (xv_out, to_z(xv_out), v_keep))
    x_core = to_core(x_two)
    q_other, cs, sn, bias, _ = lax.optimization_barrier((q_other, cs, sn, bias, xv_out))
    q_parts = spread(q_block, q_other, x_two)

    u_other = to_h(after_these(u_block, q_block))
    c_moved = to_h(after_these(c_send, u_other))
    u_a = jnp.stack([u_block, to_x(after_these(u_block, q_parts[2]))])
    u_b = jnp.stack([u_other, to_y(u_other)])
    o_own = call(pack_out, shape((HT, D)), [ANY] * 4, q_parts, [pltpu.VMEM((8, 40, WQ), BF16), pltpu.SemaphoreType.DMA((8,))])
    o_first = to_z(o_own)
    c_own = jnp.concatenate([pick(cotangent, h), after_these(c_moved, o_own)], axis=0)
    q_parts = lax.optimization_barrier(q_parts + (u_a, u_b, c_own))[:4]
    c_two = jnp.concatenate([c_own, to_z(c_own)], axis=0)
    c_core = to_core(c_two)
    qkv_w, normed_one, qkv, attn, attn_low, lse, gains = call(
        attend_kernel,
        (shape((D, WQ)), shape((N, D)), shape((N, 3 * HT)), shape((N, HT), F32), shape((N, HT)), shape((N, 4), F32), shape((8, D), F32)),
        [SMEM] + [VMEM] * 6 + [ANY] * 4, (ids, x_two, x_core, v_two, cs, sn, bias, *q_parts),
        [pltpu.SemaphoreType.DMA((32,))])
    a_two = jnp.concatenate([attn_low, to_z(after_these(attn_low, c_two))], axis=0)
    o_two = jnp.concatenate([o_own, o_first], axis=0)
    o_core = to_core(after_these(o_two, attn_low))
    u_parts = (u_a, to_y(u_a), u_b, to_x(u_b))
    a_core = to_core(a_two)
    attn_full, after, normed_two, out_w = call(
        after_kernel, (shape((N, D)), shape((M, D), F32), shape((N, D)), shape((HT, D))),
        [SMEM] + [VMEM] * 5 + [ANY] * 2, (ids, x_two, x_core, a_two, a_core, gains, o_two, o_core),
        [pltpu.VMEM((D, D), BF16), pltpu.SemaphoreType.DMA((32,))])
    block = (2, 6 * ROWS, 2 * FT)
    out_keep, out_send, r_keep, r_send, gain_two_g, a_keep, a_send, b_keep, b_send = call(
        feed_kernel, (shape((HALF, D)),) * 4 + (shape((1, D), F32),) + (shape(block),) * 4,
        [SMEM] + [VMEM] * 4 + [ANY] * 4, (ids, normed_two, gains, c_two, c_core, *u_parts),
        [pltpu.VMEM((D, 2 * FT), BF16), pltpu.VMEM((8 * FROWS, D), BF16), pltpu.VMEM((8 * FROWS, D), F32), pltpu.VMEM((8, 2 * ROWS, 2 * FT), BF16),
         pltpu.VMEM((N, FT), BF16), pltpu.VMEM((N, 2 * FT), BF16), pltpu.VMEM((HT, 2 * FT), F32),
         pltpu.SemaphoreType.DMA((32,)), pltpu.SemaphoreType.DMA((8,))], mib=48)

    r_core = to_core(r_send)
    u_sums = (a_keep, to_y(a_send), b_keep, to_x(b_send))

    def middle(r_keep, r_core, after, gains, c_two, out_keep, o_core):
        kept, sent = call(fold_kernel, (shape((M, D), F32), shape((M, D))), [VMEM] * 2, (r_keep, r_core))
        grad_after, branch = call(branch_kernel, (shape((M, D), F32), shape((M, D))), [VMEM] * 5, (kept, to_z(sent), after, gains, c_two))
        b_two = jnp.concatenate([branch, to_z(branch)], axis=0)
        o_kept, o_sent = call(fold_kernel, (shape((M, D), F32), shape((M, D))), [VMEM] * 2, (out_keep, after_these(o_core, branch)))
        return grad_after, b_two, to_core(b_two), o_kept, o_sent

    grad_after, b_two, b_core, o_kept, o_sent = fenced(
        middle, r_keep, after_these(r_core, a_send), after, gains, c_two, out_keep, to_core(out_send))

    def second_sum(a_own, a_send, b_own, b_send):
        return a_own, a_send, call(sum_second_kernel, shape(b_own.shape), [VMEM] * 2, (b_own, to_y(b_send)))

    def first_sum(sums):
        return call(sum_first_kernel, (shape(sums[0].shape[1:]),) * 4, [VMEM] * 4, sums)

    u_sums = first_sum(lax.optimization_barrier(u_sums + (b_core,))[:4])
    b_core = after_these(b_core, u_sums[3])
    def attend_back(o_sent, *inputs):
        o_moved = to_z(o_sent)
        block = (2, 4 * ROWS + 40, WQ)
        return (o_moved,) + tuple(call(
            attend_back_kernel, (shape((HALF, D)), shape((HALF, D + HT)), shape((HALF, HT))) + (shape(block),) * 4,
            [SMEM] + [VMEM] * 14, (ids,) + inputs,
            [pltpu.VMEM((N, HT), BF16), pltpu.VMEM((N, HT), F32), pltpu.VMEM((N, HT), F32), pltpu.VMEM((N, 3 * HT), BF16),
             pltpu.VMEM((HT, D), F32), pltpu.VMEM((8, D), F32), pltpu.VMEM((HT, WQ), F32)], mib=60))

    o_moved, r_keep, r_send, dv_keep, a_keep, a_send, b_keep, b_send = fenced(
        attend_back, o_sent, b_two, b_core, out_w, qkv, attn, lse, bias, cs, sn, qkv_w, normed_one, gains, gain_two_g, attn_full)
    u_sums = second_sum(*u_sums)
    r_send = after_these(r_send, u_sums[2])
    y_own, y_send = call(result_kernel, (shape((L, D)), shape((L, D))), [VMEM] * 3, (o_kept, o_moved, after))
    layer_out = call(result_home_kernel, shape((2, L, D)), [SMEM] + [VMEM] * 2, (ids, y_own, to_h(y_send)))
    r_core = to_core(r_send)
    kept, sent = call(fold_both_kernel, (shape((M, D), F32), shape((M, D + 2 * HT))), [VMEM] * 3, (r_keep, dv_keep, r_core))
    a_send, b_send, _ = lax.optimization_barrier((a_send, b_send, sent))
    q_sums = (a_keep, to_y(a_send), b_keep, to_x(b_send))
    own, sent = call(input_kernel, (shape((L, 2 * D)), shape((L, 2 * D))), [SMEM] + [VMEM] * 7,
                     (ids, kept, to_z(sent), x_two, gains, grad_after, dv_keep, r_core), [pltpu.VMEM((M, 2 * D), BF16)])
    home = to_h(sent)
    input_grad, v1_out = call(home_kernel, (shape((2, L, D), F32),) * 2, [SMEM] + [VMEM] * 3, (ids, own, home, v1_acc))

    def finish(kernel, sums, rest, first=(), last=()):
        a_own, a_send, b_send = sums
        dims = a_own.shape
        kept, sent, rows = call(kernel, (shape((2, ROWS, dims[1])), shape((2, ROWS, dims[1])), shape(rest, F32)), [SMEM] + [VMEM] * 3,
                                (ids, a_own, to_x(a_send), after_these(to_h(b_send), *first)), [pltpu.VMEM(dims, F32)])
        first = to_z(sent)
        return (ids, kept, first, to_core(pair_of(kept, after_these(first, *last)))), rows

    a_own, a_send, b_own, b_send = first_sum(q_sums)
    q_sums = second_sum(a_own, a_send, after_these(b_own, home), b_send)
    parts, down_g = finish(sum_hidden_kernel, u_sums, (FROWS, D))
    gate_g, up_g = call(join_hidden_kernel, (shape((ROWS, 4 * FT), F32),) * 2, [SMEM] + [VMEM] * 3, parts,
                        [pltpu.VMEM((4, ROWS, 2 * FT), F32)])
    parts, out_g = finish(sum_qkv_kernel, q_sums, (ROWS, D), (gate_g,), (input_grad,))
    query_g, key_g, value_g, gain_g = call(
        join_qkv_kernel, (shape((ROWS, D), F32),) * 3 + (shape((ROWS, 128), F32),), [SMEM] + [VMEM] * 3, parts)
    return (layer_out, input_grad, v1_out, gain_g[:, 0], query_g, key_g, value_g, out_g, gain_g[:, 1], gate_g, up_g, down_g)


def local(plan, layer_in, *rest):
    kept = plan.G == FAST_G and plan.T == FAST_T and layer_in.shape == (2, FAST_L, D) and rest[12].shape == (FROWS, D)
    return (fast if kept else general)(plan, layer_in, *rest)


def solution(mesh):
    plan = Plan(mesh.shape["gx"], mesh.shape["gy"])
    tokens, rows, vector = P(None, ALL, None), P(ALL, None), P(ALL)
    return jax.shard_map(
        functools.partial(local, plan),
        mesh=mesh,
        in_specs=(tokens, tokens, tokens, tokens, P(), vector, rows, rows, rows, rows, vector, rows, rows, rows),
        out_specs=(tokens, tokens, tokens, vector, rows, rows, rows, rows, vector, rows, rows, rows),
        check_vma=False,
    )
```

```python
import functools

import jax
import jax.numpy as jnp
from jax import lax
from jax.experimental import pallas as pl
from jax.experimental.pallas import tpu as pltpu
from jax.sharding import PartitionSpec as P

H = 16
EPS = 1e-05
NEG = -1e30
SCALE = 0.125
ALL = ("gx", "gy")
F32 = jnp.float32
BF16 = jnp.bfloat16


class Plan:
    def __init__(self, n_gx, n_gy):
        self.G, self.T = n_gx, n_gy // 2
        every = [(g, h, t) for g in range(self.G) for h in range(2) for t in range(self.T)]
        at = lambda g, h, t: g * n_gy + h * self.T + t
        self.g_swap = {k: [(at(g, h, t), at(g ^ k, h, t)) for g, h, t in every] for k in range(1, self.G)}
        self.t_swap = {k: [(at(g, h, t), at(g, h, t ^ k)) for g, h, t in every] for k in range(1, self.T)}
        self.h_swap = [(at(g, h, t), at(g, 1 - h, t)) for g, h, t in every]
        self.bits = []
        bit = self.T // 2
        while bit:
            self.bits.append(bit)
            bit //= 2


def pick(array, index, axis=0):
    return lax.dynamic_index_in_dim(array, index, axis, keepdims=False)


def send(array, pairs):
    return lax.ppermute(array, ALL, pairs)


def dot(a, b):
    return lax.dot_general(a, b, (((1,), (0,)), ((), ())), preferred_element_type=F32)


def dot_rows(a, b):
    return lax.dot_general(a, b, (((0,), (0,)), ((), ())), preferred_element_type=F32)


def dot_cols(a, b):
    return lax.dot_general(a, b, (((1,), (1,)), ((), ())), preferred_element_type=F32)


def rotate(values, cosine, sine):
    half = values.shape[-1] // 2
    a, b = values[..., :half], values[..., half:]
    return jnp.concatenate([a * cosine - b * sine, b * cosine + a * sine], axis=-1)


def general(plan, layer_in, first_layer_value, v1_acc, cotangent, seq_starts, norm1_gain, w_query, w_key, w_value,
          w_out, norm2_gain, w_gate, w_up, w_down):
    G, T, bits = plan.G, plan.T, plan.bits
    micro, L, D = layer_in.shape
    FF = w_gate.shape[1]
    HT, FT, heads = D // T, FF // T, H // T
    HD = D // H
    M = 2 * L
    N = T * M
    rows, frows = w_query.shape[0], w_down.shape[0]
    g, gy = lax.axis_index("gx"), lax.axis_index("gy")
    h, t = gy // T, gy % T

    def to_t(array, bit):
        return send(array, plan.t_swap[bit])

    def to_g(array, k):
        return send(array, plan.g_swap[k]) if k else array

    def to_h(array):
        return send(array, plan.h_swap)

    def inward(array):
        return jnp.concatenate([pick(array, h), to_h(pick(array, 1 - h))], axis=0)

    def outward(array):
        own, other = array[:L], to_h(array[L:])
        return jnp.stack([jnp.where(h == 0, own, other), jnp.where(h == 0, other, own)])

    def gather_t(array):
        parts = {0: array}
        for bit in bits:
            order = sorted(parts)
            moved = to_t(jnp.concatenate([parts[j] for j in order], axis=0), bit)
            size = array.shape[0]
            for i, j in enumerate(order):
                parts[j ^ bit] = moved[i * size:(i + 1) * size]
        return [parts[j] for j in range(T)]

    def reduce_t(partial):
        blocks = partial.reshape((T, -1) + partial.shape[1:])
        for bit in reversed(bits):
            shape = blocks.shape
            split = blocks.reshape((shape[0] // 2, 2) + shape[1:])
            blocks = split[:, 0] + to_t(split[:, 1].astype(BF16), bit).astype(F32)
        return blocks[0]

    def exchange_t(parts):
        held = {j: [parts[j]] for j in range(T)}
        sources = [0]
        for bit in bits:
            out = [j for j in sorted(held) if j & bit]
            flat = [p for j in out for p in held[j]]
            moved = to_t(jnp.stack(flat), bit)
            n = len(sources)
            new = {}
            for i, j in enumerate(out):
                new[j ^ bit] = held[j ^ bit] + [moved[i * n + s] for s in range(n)]
            sources = sources + [s ^ bit for s in sources]
            held = new
        result = [None] * T
        for s, p in zip(sources, held[0]):
            result[s] = p
        return result

    def natural(parts):
        array = jnp.stack(parts)
        for bit in bits:
            split = array.reshape((-1, 2, bit) + array.shape[1:])
            array = jnp.where((t & bit) != 0, split[:, ::-1], split).reshape(array.shape)
        return array

    def gather_r(block):
        other = to_h(block)
        pair = jnp.where(h == 0, jnp.stack([block, other]), jnp.stack([other, block]))
        full = jnp.zeros((G,) + pair.shape, pair.dtype)
        for k in range(G):
            full = lax.dynamic_update_slice(full, to_g(pair, k)[None], (g ^ k,) + (0,) * pair.ndim)
        return full.reshape((G * 2 * block.shape[0],) + block.shape[1:])

    def gather_cols(slices):
        block = natural(exchange_t([pick(slices, t ^ j) for j in range(T)]))
        return gather_r(block.reshape(T * block.shape[1], -1))

    def reduce_r(grad):
        n, w = grad.shape[0] // (2 * G), grad.shape[1]
        grad = grad.astype(BF16).reshape(G, 2 * n, w)
        total = pick(grad, g).astype(F32)
        for k in range(1, G):
            total = total + to_g(pick(grad, g ^ k), k).astype(F32)
        total = total.reshape(2, n, w)
        return pick(total, h) + to_h(pick(total, 1 - h).astype(BF16)).astype(F32)

    def scatter_cols(grad):
        total = reduce_r(grad).reshape(T, rows, -1)
        low = total.astype(BF16)
        return natural(exchange_t([pick(low, t ^ j) for j in range(T)])).astype(F32)

    pad = jnp.zeros((rows, 126), BF16)
    gains_in = jnp.concatenate([norm1_gain[:, None], norm2_gain[:, None], pad], axis=1)

    def col_slices(w):
        return w.reshape(rows, T, HT).transpose(1, 0, 2)

    def hidden_slices(w):
        return w.reshape(rows, 2 * G, T, frows).transpose(2, 0, 1, 3).reshape(T, rows, FT)

    qkv_slices = jnp.concatenate([col_slices(w_query), col_slices(w_key), col_slices(w_value),
                                  jnp.broadcast_to(gains_in[None], (T, rows, 128))], axis=2)
    x_own = inward(layer_in)
    qkv_w = gather_cols(qkv_slices)
    x_all = jnp.concatenate(gather_t(x_own), axis=0)
    v_own = inward(first_layer_value).reshape(M, T, HT).transpose(1, 0, 2)
    v_all = jnp.concatenate(exchange_t([pick(v_own, t ^ j) for j in range(T)]), axis=0)
    gu_w = gather_cols(jnp.concatenate([hidden_slices(w_gate), hidden_slices(w_up)], axis=2))
    down_w = gather_r(w_down)
    c_own = inward(cotangent)
    c_all = jnp.concatenate(gather_t(c_own), axis=0)
    out_w = natural(gather_t(gather_r(w_out))).reshape(T, 2 * G, rows, D).transpose(1, 0, 2, 3).reshape(D, D)
    out_w = out_w.reshape(T, HT, D)

    gains = qkv_w[:, 3 * HT:3 * HT + 2].astype(F32).T
    gain_one, gain_two = gains[0], gains[1]
    query_w, key_w, value_w = qkv_w[:, :HT], qkv_w[:, HT:2 * HT], qkv_w[:, 2 * HT:3 * HT]
    gate_w, up_w = gu_w[:, :FT], gu_w[:, FT:]

    starts = pick(seq_starts, h)
    member = t ^ jnp.arange(T, dtype=jnp.int32)
    half = h ^ jnp.arange(2, dtype=jnp.int32)
    position = ((half[None, :] * T + member[:, None]) * L)[:, :, None] + jnp.arange(L, dtype=jnp.int32)
    position = position.reshape(N) + g * N
    begin = jnp.max(jnp.where(starts[None, :] <= position[:, None], starts[None, :], 0), axis=1)
    rel = (position - begin).astype(F32)
    visible = (begin[:, None] == begin[None, :]) & (position[None, :] <= position[:, None])
    frequency = 10000.0 ** (-(jnp.arange(HD // 2, dtype=F32) * 2.0 / HD))
    angles = rel[:, None] * frequency[None, :]
    cosine, sine = jnp.cos(angles)[:, None, :], jnp.sin(angles)[:, None, :]

    x = x_all.astype(F32)
    rstd_one = lax.rsqrt(jnp.mean(x * x, axis=-1, keepdims=True) + EPS)
    normed_one = (x * rstd_one * gain_one).astype(BF16)
    query = rotate(dot(normed_one, query_w).reshape(N, heads, HD), cosine, sine).astype(BF16)
    key = rotate(dot(normed_one, key_w).reshape(N, heads, HD), cosine, sine).astype(BF16)
    value = (0.5 * dot(normed_one, value_w) + 0.5 * v_all.astype(F32)).astype(BF16).reshape(N, heads, HD)
    scores = jnp.einsum("ihd,jhd->hij", query, key, preferred_element_type=F32) * SCALE
    scores = jnp.where(visible[None], scores, NEG)
    top = jnp.max(scores, axis=-1, keepdims=True)
    probs = jnp.exp(scores - top)
    denom = jnp.sum(probs, axis=-1, keepdims=True)
    probs = probs / denom
    probs_low = probs.astype(BF16)
    attn = jnp.einsum("hij,jhd->ihd", probs_low, value, preferred_element_type=F32)
    attn_low = attn.reshape(N, HT).astype(BF16)
    attn_parts = []
    for j, part in enumerate(gather_t(attn_low)):
        part = part.reshape(T, M, HT)
        attn_parts.append(jnp.concatenate([part[b ^ j] for b in range(T)], axis=0))
    after = x
    for j in range(T):
        after = after + dot(attn_parts[j], pick(out_w, t ^ j))
    rstd_two = lax.rsqrt(jnp.mean(after * after, axis=-1, keepdims=True) + EPS)
    hat_two = after * rstd_two
    normed_two = (hat_two * gain_two).astype(BF16)
    gate = dot(normed_two, gate_w)
    up = dot(normed_two, up_w)
    sig = jax.nn.sigmoid(gate)
    act = gate * sig
    hidden = (act * up).astype(BF16)

    grad_hidden = dot_cols(c_all, down_w)
    grad_gate = (grad_hidden * up * (sig * (1.0 + gate * (1.0 - sig)))).astype(BF16)
    grad_up = (grad_hidden * act).astype(BF16)
    grad_two_part = dot_cols(grad_gate, gate_w) + dot_cols(grad_up, up_w)
    gain_two_grad = jnp.sum(grad_two_part * hat_two, axis=0)
    grad_two = reduce_t(grad_two_part) * gain_two
    hat_own = hat_two[:M]
    grad_after = c_own.astype(F32) + rstd_two[:M] * (
        grad_two - hat_own * jnp.mean(grad_two * hat_own, axis=-1, keepdims=True))
    grad_branch = jnp.concatenate(gather_t(grad_after.astype(BF16)), axis=0)
    result = reduce_t(dot(hidden, down_w)) + after[:M]
    layer_out = outward(result.astype(BF16))
    grad_down = dot_rows(hidden, c_all)
    grad_gu = dot_rows(normed_two, jnp.concatenate([grad_gate, grad_up], axis=1))

    grad_attn = dot_cols(grad_branch, pick(out_w, t)).astype(BF16).reshape(N, heads, HD)
    delta = jnp.sum(grad_attn.astype(F32) * attn, axis=-1).T
    grad_probs = jnp.einsum("ihd,jhd->hij", grad_attn, value, preferred_element_type=F32)
    grad_scores = (probs * (grad_probs - delta[..., None])).astype(BF16)
    grad_query = jnp.einsum("hij,jhd->ihd", grad_scores, key, preferred_element_type=F32) * SCALE
    grad_key = jnp.einsum("hij,ihd->jhd", grad_scores, query, preferred_element_type=F32) * SCALE
    grad_blend = jnp.einsum("hij,ihd->jhd", probs_low, grad_attn, preferred_element_type=F32).reshape(N, HT)
    grad_query = rotate(grad_query, cosine, -sine).reshape(N, HT).astype(BF16)
    grad_key = rotate(grad_key, cosine, -sine).reshape(N, HT).astype(BF16)
    grad_value = (0.5 * grad_blend).astype(BF16)
    grad_one_part = dot_cols(grad_query, query_w) + dot_cols(grad_key, key_w) + dot_cols(grad_value, value_w)
    hat_one = x * rstd_one
    gain_one_grad = jnp.sum(grad_one_part * hat_one, axis=0)
    grad_one = reduce_t(grad_one_part) * gain_one
    hat_own = hat_one[:M]
    input_grad = grad_after + rstd_one[:M] * (
        grad_one - hat_own * jnp.mean(grad_one * hat_own, axis=-1, keepdims=True))
    input_grad = outward(input_grad.astype(BF16)).astype(F32)
    v_parts = natural(exchange_t([grad_value[j * M:(j + 1) * M] for j in range(T)]))
    v1_out = v1_acc + outward(v_parts.transpose(1, 0, 2).reshape(M, D)).astype(F32)

    attn_full = natural([p.T for p in attn_parts]).reshape(2 * G, T, rows, N)
    grad_out = dot(pick(attn_full, t, 1).reshape(2 * G * rows, N), grad_branch)
    grad_gains = jnp.stack([gain_one_grad, gain_two_grad], axis=1)
    grad_gains = jnp.concatenate([grad_gains, jnp.zeros((D, 126), F32)], axis=1)
    grad_qkv = dot_rows(normed_one, jnp.concatenate([grad_query, grad_key, grad_value], axis=1))
    down_g = reduce_r(grad_down)
    gu_g = scatter_cols(grad_gu)
    out_g = reduce_r(grad_out)
    qkv_g = scatter_cols(jnp.concatenate([grad_qkv, grad_gains], axis=1))

    def col_join(parts):
        return parts.transpose(1, 0, 2).reshape(rows, D)

    def hidden_join(parts):
        return parts.reshape(T, rows, 2 * G, frows).transpose(1, 2, 0, 3).reshape(rows, FF)

    gain_g = jnp.sum(qkv_g[:, :, 3 * HT:3 * HT + 2], axis=0)
    return (layer_out, input_grad, v1_out, gain_g[:, 0], col_join(qkv_g[:, :, :HT]), col_join(qkv_g[:, :, HT:2 * HT]),
            col_join(qkv_g[:, :, 2 * HT:3 * HT]), out_g, gain_g[:, 1], hidden_join(gu_g[:, :, :FT]),
            hidden_join(gu_g[:, :, FT:]), down_g)


FAST_G, FAST_T, FAST_L, D, HT, FT, FROWS, ROWS = 4, 4, 64, 1024, 256, 704, 88, 32
M, N = 2 * FAST_L, 8 * FAST_L
HALF = N // 2
WQ = 3 * HT + 128
ORDER = (0, 2, 1, 3)
HD = 64
ARRIVED = ((0, 0), (1, 0), (2, 0), (3, 0), (0, 1), (2, 1), (1, 1), (3, 1))
LEAVING = {(0, 0): (0, 0), (1, 0): (0, 1), (2, 0): (1, 0), (3, 0): (1, 1), (0, 1): (2, 0), (2, 1): (2, 1), (1, 1): (3, 0), (3, 1): (3, 1)}
VMEM = pl.BlockSpec(memory_space=pltpu.VMEM)
SMEM = pl.BlockSpec(memory_space=pltpu.SMEM)
ANY = pl.BlockSpec(memory_space=pltpu.HBM)


def shape(dims, dtype=BF16):
    return jax.ShapeDtypeStruct(dims, dtype)


def call(kernel, outs, specs, args, scratch=(), mib=40):
    return pl.pallas_call(
        kernel,
        out_shape=outs,
        in_specs=specs,
        out_specs=jax.tree.map(lambda _: VMEM, outs),
        scratch_shapes=list(scratch),
        compiler_params=pltpu.CompilerParams(vmem_limit_bytes=mib << 20),
        cost_estimate=pl.CostEstimate(flops=1, bytes_accessed=1, transcendentals=0),
    )(*args)


def aligned(index, size):
    return pl.ds(pl.multiple_of(index * size, size), size)


def eye(rows, lanes):
    return (lax.broadcasted_iota(jnp.int32, (rows, lanes), 0) == lax.broadcasted_iota(jnp.int32, (rows, lanes), 1)).astype(BF16)


def tiles_in(block):
    lines = [jnp.concatenate([block[j * 8:j * 8 + 8, i * 128:i * 128 + 128] for j in range(11)], axis=1) for i in range(8)]
    return jnp.concatenate(lines, axis=0)


def tiles_out(block):
    lines = [jnp.concatenate([block[i * 8:i * 8 + 8, j * 128:j * 128 + 128] for i in range(8)], axis=1) for j in range(11)]
    return jnp.concatenate(lines, axis=0)


def line_tiles_in(block):
    tiles = [block[j * 8:j * 8 + 8, i * 128:i * 128 + 128] for j in range(4) for i in range(8)]
    tiles += [jnp.zeros_like(tiles[0])] * 3
    return jnp.concatenate([jnp.concatenate(tiles[n * 7:n * 7 + 7], axis=1) for n in range(5)], axis=0)


def line_tiles_out(block):
    tiles = [block[n * 8:n * 8 + 8, i * 128:i * 128 + 128] for n in range(5) for i in range(7)]
    return jnp.concatenate([jnp.concatenate(tiles[j * 8:j * 8 + 8], axis=1) for j in range(4)], axis=0)


def pack_first(ids, gain_one, gain_two, wq, wk, wv, wo, x, v, c, out, keep, lines, xv_out, c_out, rows, whole, sem):
    h, t = ids[1], ids[2]
    copies = []
    for j in (2, 3, 0, 1):
        to = keep if j < 2 else out
        for i, w in enumerate((wq, wk, wv)):
            copies.append((w.at[:, aligned(t ^ j, HT)], to.at[j % 2, :, i * HT:(i + 1) * HT]))
    copies += [(wo, whole), (x.at[1 - h], xv_out.at[:, :D]), (v.at[1 - h], xv_out.at[:, D:]), (c.at[1 - h], c_out)]
    started = fetch(copies, sem)
    rows[...] = jnp.zeros_like(rows)
    rows[0:1] = gain_one[...].astype(F32)
    rows[1:2] = gain_two[...].astype(F32)
    gains = dot_rows(rows[...].astype(BF16), eye(8, 128)).astype(BF16)
    for j in range(4):
        (keep if j < 2 else out)[j % 2, :, 3 * HT:] = gains
    started[12].wait()
    lines[...] = line_tiles_in(whole[...].astype(F32)).astype(BF16)
    for n, copy in enumerate(started):
        if n != 12:
            copy.wait()


def pack_hidden(ids, wg, wu, wd, keep, out, down, nat, gate, up, whole, sem):
    t = ids[2]
    started = fetch([(wg, gate), (wu, up), (wd, whole)], sem)
    for a, w in enumerate((gate, up)):
        started[a].wait()
        for m in range(4):
            for i in range(8):
                at, to = (i * 4 + m) * FROWS, a * FT + i * FROWS
                nat[m, :, to:to + FROWS] = w[:, at:at + FROWS].astype(F32)
    for j in range(4):
        to = keep if j < 2 else out
        to[j % 2] = nat[t ^ j].astype(BF16)
    started[2].wait()
    down[...] = tiles_in(whole[...].astype(F32)).astype(BF16)


def pack_block(kept, first, last, tail, out, sem):
    width = ROWS
    parts = (kept.at[0], first.at[0], last.at[0], last.at[1], tail)
    started = fetch([(part, out.at[i * width:i * width + part.shape[0]]) for i, part in enumerate(parts)], sem)
    for copy in started:
        copy.wait()


def pack_pair(kept, first, out, sem):
    started = fetch([(kept.at[1], out.at[0]), (first.at[1], out.at[1])], sem)
    for copy in started:
        copy.wait()


def pack_out(b0, b1, b2, b3, out, raw, sem):
    started = fetch([((b0, b1, b2, b3)[n // 2].at[n % 2, 4 * ROWS:], raw.at[n]) for n in range(8)], sem)
    for n in range(8):
        started[n].wait()
        out[n * ROWS:(n + 1) * ROWS] = line_tiles_out(raw[n].astype(F32)).astype(BF16)


def pack_second(ids, x, v, moved, xv_out, v_keep, own, sem):
    h, t = ids[1], ids[2]
    started = fetch([(x.at[h], xv_out.at[:FAST_L, :D]), (v.at[h], own.at[:FAST_L]),
                     (moved.at[:, :D], xv_out.at[FAST_L:, :D]), (moved.at[:, D:], own.at[FAST_L:])], sem)
    for copy in started:
        copy.wait()
    for j in range(2):
        v_keep[j] = own[:, aligned(t ^ j, HT)]
        xv_out[:, D + j * HT:D + (j + 1) * HT] = own[:, aligned(t ^ (j + 2), HT)]


def pack_third(mine, moved, v_keep, out, v_two):
    out[:M, :D] = mine[:, :D]
    out[M:, :D] = moved[:, :D]
    out[:M, D:] = v_keep[1]
    out[M:, D:] = moved[:, D + HT:]
    v_two[:M] = v_keep[0]
    v_two[M:] = moved[:, D:D + HT]


def fetch(copies, sem):
    started = []
    for i, (source, target) in enumerate(copies):
        copy = pltpu.make_async_copy(source, target, sem.at[i])
        copy.start()
        started.append(copy)
    return started


def swap_halves(u):
    width = u.shape[-1]
    lane = lax.broadcasted_iota(jnp.int32, u.shape, 1)
    up = pltpu.roll(u, width - HD // 2, 1)
    down = pltpu.roll(u, HD // 2, 1)
    return jnp.where(lane % HD < HD // 2, up, down)


def scale_of(x):
    return lax.rsqrt(jnp.mean(x * x, axis=-1, keepdims=True) + EPS)


def attend_kernel(ids, x2, xc, v2, cs, sn, bias, b0, b1, b2, b3, w, normed, qkv, attn, low, lse, gains, sem):
    g, h, t = ids[0], ids[1], ids[2]
    copies = []
    for n, (k, dh) in enumerate(ARRIVED):
        b = (b0, b1, b2, b3)[n // 2]
        for i, s in enumerate(ORDER):
            row = ((g ^ k) * 2 + (h ^ dh)) * 4 + (t ^ s)
            copies.append((b.at[n % 2, i * ROWS:(i + 1) * ROWS], w.at[aligned(row, ROWS)]))
    for copy in fetch(copies, sem):
        copy.wait()
    gains[...] = dot_cols(eye(8, 128), w[:, 3 * HT:])
    gain = gains[0:1, :]
    for b in range(2):
        rows = slice(b * HALF, (b + 1) * HALF)
        source = x2 if b == 0 else xc
        x = source[:, :D].astype(F32)
        r = (x * scale_of(x) * gain).astype(BF16)
        normed[rows] = r
        out = dot(r, w[:, :3 * HT])
        for i in range(2):
            u = out[:, i * HT:(i + 1) * HT]
            qkv[rows, i * HT:(i + 1) * HT] = (u * cs[rows] + swap_halves(u) * sn[rows]).astype(BF16)
        value = v2[...] if b == 0 else xc[:, D:]
        qkv[rows, 2 * HT:] = (0.5 * out[:, 2 * HT:] + 0.5 * value.astype(F32)).astype(BF16)
    outs, tops = [], []
    mask = bias[...].astype(F32)
    for i in range(4):
        q, k, v = (qkv[:, n * HT + i * HD:n * HT + (i + 1) * HD] for n in range(3))
        s = dot_cols(q, k) * SCALE + mask
        top = jnp.max(s, axis=-1, keepdims=True)
        p = jnp.exp(s - top)
        total = jnp.sum(p, axis=-1, keepdims=True)
        outs.append(dot(p.astype(BF16), v) / total)
        tops.append(top + jnp.log(total))
    o = jnp.concatenate(outs, axis=1)
    attn[...] = o
    low[...] = o.astype(BF16)
    lse[...] = jnp.concatenate(tops, axis=1)


def after_kernel(ids, x2, xc, o2, oc, gains, co2, coc, full, after, normed, own_w, w, sem):
    g, h, t = ids[0], ids[1], ids[2]
    copies = []
    for i, s in enumerate(ORDER):
        source = co2 if i < 2 else coc
        for n, (k, dh) in enumerate(ARRIVED):
            row = ((g ^ k) * 2 + (h ^ dh)) * 4 + (t ^ s)
            at = (i % 2) * HT + n * ROWS
            copies.append((source.at[at:at + ROWS], w.at[aligned(row, ROWS)]))
    started = fetch(copies, sem)
    for i, s in enumerate(ORDER):
        source = o2 if i < 2 else oc
        for p in range(4):
            q = ORDER.index(ORDER[p] ^ s)
            full[p * M:(p + 1) * M, aligned(t ^ s, HT)] = source[(i % 2) * N + q * M:(i % 2) * N + (q + 1) * M]
    for copy in started:
        copy.wait()
    own_w[...] = w[aligned(t, HT)]
    gain = gains[1:2, :]
    for b in range(2):
        rows = slice(b * HALF, (b + 1) * HALF)
        source = x2 if b == 0 else xc
        a = source[:, :D].astype(F32) + dot(full[rows], w[...])
        if b == 0:
            after[...] = a[:M]
        normed[rows] = (a * scale_of(a) * gain).astype(BF16)


def feed_kernel(ids, normed, gains, c2, cc, u0, u1, u2, u3, out_keep, out_send, r_keep, r_send, gain_g, a_keep, a_send, b_keep, b_send,
                w, wd, wide, raw, hidden, dgu, gu_g, sem, sem_d):
    g, h, t = ids[0], ids[1], ids[2]
    copies, copies_d = [], []
    for n, (k, dh) in enumerate(ARRIVED):
        b = (u0, u1, u2, u3)[n // 2]
        for i, s in enumerate(ORDER):
            row = ((g ^ k) * 2 + (h ^ dh)) * 4 + (t ^ s)
            copies.append((b.at[n % 2, i * ROWS:(i + 1) * ROWS], w.at[aligned(row, ROWS)]))
        copies_d.append((b.at[n % 2, 4 * ROWS:], raw.at[n]))
    started_d, started = fetch(copies_d, sem_d), fetch(copies, sem)
    for n, (k, dh) in enumerate(ARRIVED):
        started_d[n].wait()
        wide[aligned((g ^ k) * 2 + (h ^ dh), FROWS)] = tiles_out(raw[n].astype(F32))
    wd[...] = wide[...].astype(BF16)
    for copy in started:
        copy.wait()
    gain_sum = jnp.zeros((1, D), F32)
    for b in range(2):
        rows = slice(b * HALF, (b + 1) * HALF)
        c = (c2 if b == 0 else cc)[...]
        gu = dot(normed[rows], w[...])
        gate, up = gu[:, :FT], gu[:, FT:]
        sig = 1.0 / (1.0 + jnp.exp(-gate))
        act = gate * sig
        hid = (act * up).astype(BF16)
        hidden[rows] = hid
        dh = dot_cols(c, wd[...])
        dgu[rows, :FT] = (dh * up * (sig * (1.0 + gate * (1.0 - sig)))).astype(BF16)
        dgu[rows, FT:] = (dh * act).astype(BF16)
        dr = dot_cols(dgu[rows], w[...])
        out = dot(hid, wd[...])
        gain_sum = gain_sum + jnp.sum(dr * normed[rows].astype(F32), axis=0, keepdims=True)
        (r_keep if b == 0 else r_send)[...] = dr.astype(BF16)
        (out_keep if b == 0 else out_send)[...] = out.astype(BF16)
    gain_g[...] = gain_sum / gains[1:2, :]
    wide[...] = dot_rows(hidden[:HALF], c2[...]) + dot_rows(hidden[HALF:], cc[...])
    for k in range(4):
        gu_g[...] = dot_rows(normed[:, aligned(g ^ k, HT)], dgu[...])
        for e in range(2):
            target, at = LEAVING[(k, e)]
            target = (a_keep, a_send, b_keep, b_send)[target]
            target[at, :4 * ROWS] = gu_g[aligned(h ^ e, 4 * ROWS)].astype(BF16)
            target[at, 4 * ROWS:] = tiles_in(wide[aligned((g ^ k) * 2 + (h ^ e), FROWS)]).astype(BF16)


def fold_kernel(keep, moved, kept, send):
    kept[...] = keep[:M].astype(F32) + moved[:M].astype(F32)
    send[...] = (keep[M:].astype(F32) + moved[M:].astype(F32)).astype(BF16)


def fold_both_kernel(keep, dv, moved, kept, send):
    kept[...] = keep[:M].astype(F32) + moved[:M, :D].astype(F32)
    send[:, :D] = (keep[M:].astype(F32) + moved[M:, :D].astype(F32)).astype(BF16)
    send[:, D:D + HT] = dv[M:]
    send[:, D + HT:] = moved[M:, D:]


def branch_kernel(keep, moved, after, gains, c2, grad_after, low):
    a = after[...]
    scale = scale_of(a)
    hat = a * scale
    dy = (keep[...] + moved[...].astype(F32)) * gains[1:2, :]
    d = c2[:M].astype(F32) + scale * (dy - hat * jnp.mean(dy * hat, axis=-1, keepdims=True))
    grad_after[...] = d
    low[...] = d.astype(BF16)


def attend_back_kernel(ids, da2, dac, wo, qkv, attn, lse, bias, cs, sn, w, normed, gains, gain_two, full,
                       r_keep, r_send, dv_keep, a_keep, a_send, b_keep, b_send, do, dk, dv, dqkv, scratch, rows_g, qkv_g):
    g, h, t = ids[0], ids[1], ids[2]
    for b in range(2):
        rows = slice(b * HALF, (b + 1) * HALF)
        do[rows] = dot_cols((da2 if b == 0 else dac)[...], wo[...]).astype(BF16)
    dqs = []
    mask = bias[...].astype(F32)
    for i in range(4):
        lanes = slice(i * HD, (i + 1) * HD)
        q, k, v = (qkv[:, n * HT + i * HD:n * HT + (i + 1) * HD] for n in range(3))
        d = do[:, lanes]
        delta = jnp.sum(d.astype(F32) * attn[:, lanes], axis=-1, keepdims=True)
        p = jnp.exp(dot_cols(q, k) * SCALE + mask - lse[:, i:i + 1])
        ds = (p * (dot_cols(d, v) - delta)).astype(BF16)
        dqs.append(dot(ds, k))
        dk[:, lanes], dv[:, lanes] = dot_rows(ds, q), dot_rows(p.astype(BF16), d)
    u = jnp.concatenate(dqs, axis=1) * SCALE
    dqkv[:, :HT] = (u * cs[...] - swap_halves(u) * sn[...]).astype(BF16)
    gain_sum = jnp.zeros((1, D), F32)
    for b in range(2):
        rows = slice(b * HALF, (b + 1) * HALF)
        u = dk[rows] * SCALE
        dqkv[rows, HT:2 * HT] = (u * cs[rows] - swap_halves(u) * sn[rows]).astype(BF16)
        dqkv[rows, 2 * HT:] = (0.5 * dv[rows]).astype(BF16)
        dr = dot_cols(dqkv[rows], w[:, :3 * HT])
        gain_sum = gain_sum + jnp.sum(dr * normed[rows].astype(F32), axis=0, keepdims=True)
        if b == 0:
            r_keep[...] = dr.astype(BF16)
            dv_keep[...] = dqkv[rows, 2 * HT:]
        else:
            r_send[:, :D] = dr.astype(BF16)
            r_send[:, D:] = dqkv[rows, 2 * HT:]
    rows_g[...] = jnp.zeros_like(rows_g)
    rows_g[0:1] = gain_sum / gains[0:1, :]
    rows_g[1:2] = gain_two[...]
    for k in range(4):
        lanes = aligned(g ^ k, HT)
        qkv_g[:, :3 * HT] = dot_rows(normed[:, lanes], dqkv[...])
        qkv_g[:, 3 * HT:] = dot_rows(rows_g[:, lanes].astype(BF16), eye(8, 128))
        scratch[...] = dot_rows(full[:HALF, lanes], da2[...]) + dot_rows(full[HALF:, lanes], dac[...])
        for e in range(2):
            target, at = LEAVING[(k, e)]
            target = (a_keep, a_send, b_keep, b_send)[target]
            target[at, :4 * ROWS] = qkv_g[aligned(h ^ e, 4 * ROWS)].astype(BF16)
            target[at, 4 * ROWS:] = line_tiles_in(scratch[aligned((h ^ e) * 4 + t, ROWS)]).astype(BF16)


def sum_first_kernel(a_keep, a_moved, b_keep, b_moved, a_own, a_send, b_own, b_send):
    for keep, moved, own, out in ((a_keep, a_moved, a_own, a_send), (b_keep, b_moved, b_own, b_send)):
        own[...] = (keep[0].astype(F32) + moved[0].astype(F32)).astype(BF16)
        out[...] = (keep[1].astype(F32) + moved[1].astype(F32)).astype(BF16)


def sum_second_kernel(b_own, b_moved, b_send):
    b_send[...] = (b_own[...].astype(F32) + b_moved[...].astype(F32)).astype(BF16)


def sum_third(a_own, a_moved, moved, total):
    total[...] = (a_own[...].astype(F32) + a_moved[...].astype(F32)) + moved[...].astype(F32)


def sum_hidden_kernel(ids, a_own, a_moved, moved, kept, send, down, total):
    t = ids[2]
    sum_third(a_own, a_moved, moved, total)
    for j in range(4):
        (kept if j < 2 else send)[j % 2] = total[aligned(t ^ j, ROWS)].astype(BF16)
    down[...] = tiles_out(total[4 * ROWS:])


def sum_qkv_kernel(ids, a_own, a_moved, moved, kept, send, out, total):
    t = ids[2]
    sum_third(a_own, a_moved, moved, total)
    for j in range(4):
        (kept if j < 2 else send)[j % 2] = total[aligned(t ^ j, ROWS)].astype(BF16)
    out[...] = line_tiles_out(total[4 * ROWS:])


def join_qkv_kernel(ids, kept, first, last, q, k, v, gains):
    t = ids[2]
    parts = (kept[0], first[0], last[0], last[1])
    for s, part in zip(ORDER, parts):
        for i, ref in enumerate((q, k, v)):
            ref[:, aligned(t ^ s, HT)] = part[:, i * HT:(i + 1) * HT].astype(F32)
    low = [part[:, 3 * HT:].astype(F32) for part in parts]
    gains[...] = (low[0] + low[1]) + (low[2] + low[3])


def join_hidden_kernel(ids, kept, first, last, gate, up, nat):
    t = ids[2]
    for s, part in zip(ORDER, (kept[0], first[0], last[0], last[1])):
        nat[t ^ s] = part.astype(F32)
    for m in range(4):
        for a, ref in enumerate((gate, up)):
            for i in range(8):
                to, at = (i * 4 + m) * FROWS, a * FT + i * FROWS
                ref[:, to:to + FROWS] = nat[m, :, at:at + FROWS]


def input_kernel(ids, keep, moved, x2, gains, grad_after, dv, dv_core, own, send, both):
    t = ids[2]
    x = x2[:M, :D].astype(F32)
    scale = scale_of(x)
    hat = x * scale
    dy = (keep[...] + moved[:, :D].astype(F32)) * gains[0:1, :]
    both[:, :D] = (grad_after[...] + scale * (dy - hat * jnp.mean(dy * hat, axis=-1, keepdims=True))).astype(BF16)
    parts = (dv[:M], moved[:, D:D + HT], dv_core[:M, D:], moved[:, D + HT:])
    for s, part in zip(ORDER, parts):
        both[:, aligned(4 + (t ^ s), HT)] = part
    own[...] = both[:FAST_L]
    send[...] = both[FAST_L:]


def home_kernel(ids, own, moved, v1, grad, v_out):
    h = ids[1]
    grad[h] = own[:, :D].astype(F32)
    grad[1 - h] = moved[:, :D].astype(F32)
    v_out[h] = v1[h] + own[:, D:].astype(F32)
    v_out[1 - h] = v1[1 - h] + moved[:, D:].astype(F32)


def result_kernel(keep, moved, after, own, send):
    out = after[...] + (keep[...] + moved[...].astype(F32))
    own[...] = out[:FAST_L].astype(BF16)
    send[...] = out[FAST_L:].astype(BF16)


def result_home_kernel(ids, own, moved, out):
    h = ids[1]
    out[h] = own[...]
    out[1 - h] = moved[...]


def fast(plan, layer_in, first_layer_value, v1_acc, cotangent, seq_starts, norm1_gain, w_query, w_key, w_value,
         w_out, norm2_gain, w_gate, w_up, w_down):
    L = FAST_L
    g, gy = lax.axis_index("gx"), lax.axis_index("gy")
    h, t = gy // 4, gy % 4
    ids = jnp.stack([g, h, t]).astype(jnp.int32)

    def to_z(array):
        return send(array, plan.t_swap[2])

    def to_core(array):
        return send(array, plan.t_swap[1])

    def to_h(array):
        return send(array, plan.h_swap)

    def to_x(array):
        return send(array, plan.g_swap[1])

    def to_y(array):
        return send(array, plan.g_swap[2])

    def after_these(array, *others):
        return lax.optimization_barrier((array,) + others)[0]

    def fenced(part, *inputs):
        results = jax.eval_shape(part, *inputs)
        nothing = lambda *_: jax.tree.map(lambda a: jnp.zeros(a.shape, a.dtype), results)
        return lax.cond(ids[0] >= 0, part, nothing, *inputs)

    def spread(own, other, *first):
        a_pair = jnp.stack([own, to_x(own)])
        b_pair = jnp.stack([other, to_y(other)])
        a_pair, b_pair = lax.optimization_barrier((a_pair, b_pair) + first)[:2]
        return a_pair, to_y(a_pair), b_pair, to_x(b_pair)

    def pair_of(kept, first):
        return call(pack_pair, shape(kept.shape), [ANY] * 2, (kept, first), [pltpu.SemaphoreType.DMA((2,))])

    def block_of(kept, first, last, tail):
        return call(pack_block, shape((4 * ROWS + tail.shape[0], tail.shape[1])), [ANY] * 4, (kept, first, last, tail),
                    [pltpu.SemaphoreType.DMA((5,))])

    q_send, q_keep, o_block, xv_send, c_send = call(
        pack_first, (shape((2, ROWS, WQ)), shape((2, ROWS, WQ)), shape((40, WQ)), shape((L, 2 * D)), shape((L, D))),
        [SMEM] + [VMEM] * 2 + [ANY] * 7,
        (ids, norm1_gain[None], norm2_gain[None], w_query, w_key, w_value, w_out, layer_in, first_layer_value, cotangent),
        [pltpu.VMEM((8, ROWS), F32), pltpu.VMEM((ROWS, D), BF16), pltpu.SemaphoreType.DMA((16,))], mib=63)
    q_first = to_z(q_send)
    xv_moved = to_h(xv_send)
    q_last = to_core(pair_of(q_keep, q_first))
    q_block = block_of(q_keep, q_first, q_last, o_block)
    q_other = to_h(q_block)

    starts = pick(after_these(seq_starts, q_block), h)
    member = t ^ jnp.array(ORDER, jnp.int32)
    half = h ^ jnp.arange(2, dtype=jnp.int32)
    position = ((half[None, :] * 4 + member[:, None]) * L)[:, :, None] + jnp.arange(L, dtype=jnp.int32)
    position = position.reshape(N) + g * N
    begin = jnp.max(jnp.where(starts[None, :] <= position[:, None], starts[None, :], 0), axis=1)
    visible = (begin[:, None] == begin[None, :]) & (position[None, :] <= position[:, None])
    bias = jnp.where(visible, 0.0, NEG).astype(BF16)
    lane = jnp.arange(HT, dtype=jnp.int32)
    frequency = 10000.0 ** (-((lane % (HD // 2)).astype(F32) * 2.0 / HD))
    angles = (position - begin).astype(F32)[:, None] * frequency[None, :]
    cs = jnp.cos(angles)
    sn = jnp.sin(angles) * jnp.where(lane % HD < HD // 2, -1.0, 1.0)[None, :]

    u_keep, u_send, d_block = call(
        pack_hidden, (shape((2, ROWS, 2 * FT)), shape((2, ROWS, 2 * FT)), shape((2 * ROWS, 2 * FT))), [SMEM] + [ANY] * 3,
        (after_these(ids, q_send), w_gate, w_up, w_down),
        [pltpu.VMEM((4, ROWS, 2 * FT), F32), pltpu.VMEM((ROWS, 4 * FT), BF16), pltpu.VMEM((ROWS, 4 * FT), BF16), pltpu.VMEM((FROWS, D), BF16),
         pltpu.SemaphoreType.DMA((3,))], mib=63)
    u_first = to_z(u_send)
    u_last = to_core(pair_of(u_keep, after_these(u_first, q_block)))
    u_block = block_of(u_keep, u_first, u_last, d_block)

    xv_out, v_keep = call(pack_second, (shape((M, D + 2 * HT)), shape((2, M, HT))), [SMEM] + [ANY] * 3,
                          (after_these(ids, u_block), layer_in, first_layer_value, xv_moved), [pltpu.VMEM((M, D), BF16), pltpu.SemaphoreType.DMA((4,))], mib=63)
    x_two, v_two = call(pack_third, (shape((HALF, D + HT)), shape((HALF, HT))), [VMEM] * 3, (xv_out, to_z(xv_out), v_keep))
    x_core = to_core(x_two)
    q_other, cs, sn, bias, _ = lax.optimization_barrier((q_other, cs, sn, bias, xv_out))
    q_parts = spread(q_block, q_other, x_two)

    u_other = to_h(after_these(u_block, q_block))
    c_moved = to_h(after_these(c_send, u_other))
    u_a = jnp.stack([u_block, to_x(after_these(u_block, q_parts[2]))])
    u_b = jnp.stack([u_other, to_y(u_other)])
    o_own = call(pack_out, shape((HT, D)), [ANY] * 4, q_parts, [pltpu.VMEM((8, 40, WQ), BF16), pltpu.SemaphoreType.DMA((8,))])
    o_first = to_z(o_own)
    c_own = jnp.concatenate([pick(cotangent, h), after_these(c_moved, o_own)], axis=0)
    q_parts = lax.optimization_barrier(q_parts + (u_a, u_b, c_own))[:4]
    c_two = jnp.concatenate([c_own, to_z(c_own)], axis=0)
    c_core = to_core(c_two)
    qkv_w, normed_one, qkv, attn, attn_low, lse, gains = call(
        attend_kernel,
        (shape((D, WQ)), shape((N, D)), shape((N, 3 * HT)), shape((N, HT), F32), shape((N, HT)), shape((N, 4), F32), shape((8, D), F32)),
        [SMEM] + [VMEM] * 6 + [ANY] * 4, (ids, x_two, x_core, v_two, cs, sn, bias, *q_parts),
        [pltpu.SemaphoreType.DMA((32,))])
    a_two = jnp.concatenate([attn_low, to_z(after_these(attn_low, c_two))], axis=0)
    o_two = jnp.concatenate([o_own, o_first], axis=0)
    o_core = to_core(after_these(o_two, attn_low))
    u_parts = (u_a, to_y(u_a), u_b, to_x(u_b))
    a_core = to_core(a_two)
    attn_full, after, normed_two, out_w = call(
        after_kernel, (shape((N, D)), shape((M, D), F32), shape((N, D)), shape((HT, D))),
        [SMEM] + [VMEM] * 5 + [ANY] * 2, (ids, x_two, x_core, a_two, a_core, gains, o_two, o_core),
        [pltpu.VMEM((D, D), BF16), pltpu.SemaphoreType.DMA((32,))])
    block = (2, 6 * ROWS, 2 * FT)
    out_keep, out_send, r_keep, r_send, gain_two_g, a_keep, a_send, b_keep, b_send = call(
        feed_kernel, (shape((HALF, D)),) * 4 + (shape((1, D), F32),) + (shape(block),) * 4,
        [SMEM] + [VMEM] * 4 + [ANY] * 4, (ids, normed_two, gains, c_two, c_core, *u_parts),
        [pltpu.VMEM((D, 2 * FT), BF16), pltpu.VMEM((8 * FROWS, D), BF16), pltpu.VMEM((8 * FROWS, D), F32), pltpu.VMEM((8, 2 * ROWS, 2 * FT), BF16),
         pltpu.VMEM((N, FT), BF16), pltpu.VMEM((N, 2 * FT), BF16), pltpu.VMEM((HT, 2 * FT), F32),
         pltpu.SemaphoreType.DMA((32,)), pltpu.SemaphoreType.DMA((8,))], mib=48)

    r_core = to_core(r_send)
    u_sums = (a_keep, to_y(a_send), b_keep, to_x(b_send))

    def middle(r_keep, r_core, after, gains, c_two, out_keep, o_core):
        kept, sent = call(fold_kernel, (shape((M, D), F32), shape((M, D))), [VMEM] * 2, (r_keep, r_core))
        grad_after, branch = call(branch_kernel, (shape((M, D), F32), shape((M, D))), [VMEM] * 5, (kept, to_z(sent), after, gains, c_two))
        b_two = jnp.concatenate([branch, to_z(branch)], axis=0)
        o_kept, o_sent = call(fold_kernel, (shape((M, D), F32), shape((M, D))), [VMEM] * 2, (out_keep, after_these(o_core, branch)))
        return grad_after, b_two, to_core(b_two), o_kept, o_sent

    grad_after, b_two, b_core, o_kept, o_sent = fenced(
        middle, r_keep, after_these(r_core, a_send), after, gains, c_two, out_keep, to_core(out_send))

    def second_sum(a_own, a_send, b_own, b_send):
        return a_own, a_send, call(sum_second_kernel, shape(b_own.shape), [VMEM] * 2, (b_own, to_y(b_send)))

    def first_sum(sums):
        return call(sum_first_kernel, (shape(sums[0].shape[1:]),) * 4, [VMEM] * 4, sums)

    u_sums = first_sum(lax.optimization_barrier(u_sums + (b_core,))[:4])
    b_core = after_these(b_core, u_sums[3])
    def attend_back(o_sent, *inputs):
        o_moved = to_z(o_sent)
        block = (2, 4 * ROWS + 40, WQ)
        return (o_moved,) + tuple(call(
            attend_back_kernel, (shape((HALF, D)), shape((HALF, D + HT)), shape((HALF, HT))) + (shape(block),) * 4,
            [SMEM] + [VMEM] * 14, (ids,) + inputs,
            [pltpu.VMEM((N, HT), BF16), pltpu.VMEM((N, HT), F32), pltpu.VMEM((N, HT), F32), pltpu.VMEM((N, 3 * HT), BF16),
             pltpu.VMEM((HT, D), F32), pltpu.VMEM((8, D), F32), pltpu.VMEM((HT, WQ), F32)], mib=60))

    o_moved, r_keep, r_send, dv_keep, a_keep, a_send, b_keep, b_send = fenced(
        attend_back, o_sent, b_two, b_core, out_w, qkv, attn, lse, bias, cs, sn, qkv_w, normed_one, gains, gain_two_g, attn_full)
    u_sums = second_sum(*u_sums)
    r_send = after_these(r_send, u_sums[2])
    y_own, y_send = call(result_kernel, (shape((L, D)), shape((L, D))), [VMEM] * 3, (o_kept, o_moved, after))
    layer_out = call(result_home_kernel, shape((2, L, D)), [SMEM] + [VMEM] * 2, (ids, y_own, to_h(y_send)))
    r_core = to_core(r_send)
    kept, sent = call(fold_both_kernel, (shape((M, D), F32), shape((M, D + 2 * HT))), [VMEM] * 3, (r_keep, dv_keep, r_core))
    a_send, b_send, _ = lax.optimization_barrier((a_send, b_send, sent))
    q_sums = (a_keep, to_y(a_send), b_keep, to_x(b_send))
    own, sent = call(input_kernel, (shape((L, 2 * D)), shape((L, 2 * D))), [SMEM] + [VMEM] * 7,
                     (ids, kept, to_z(sent), x_two, gains, grad_after, dv_keep, r_core), [pltpu.VMEM((M, 2 * D), BF16)])
    home = to_h(sent)
    input_grad, v1_out = call(home_kernel, (shape((2, L, D), F32),) * 2, [SMEM] + [VMEM] * 3, (ids, own, home, v1_acc))

    def finish(kernel, sums, rest, first=(), last=()):
        a_own, a_send, b_send = sums
        dims = a_own.shape
        kept, sent, rows = call(kernel, (shape((2, ROWS, dims[1])), shape((2, ROWS, dims[1])), shape(rest, F32)), [SMEM] + [VMEM] * 3,
                                (ids, a_own, to_x(a_send), after_these(to_h(b_send), *first)), [pltpu.VMEM(dims, F32)])
        first = to_z(sent)
        return (ids, kept, first, to_core(pair_of(kept, after_these(first, *last)))), rows

    a_own, a_send, b_own, b_send = first_sum(q_sums)
    q_sums = second_sum(a_own, a_send, after_these(b_own, home), b_send)
    parts, down_g = finish(sum_hidden_kernel, u_sums, (FROWS, D))
    gate_g, up_g = call(join_hidden_kernel, (shape((ROWS, 4 * FT), F32),) * 2, [SMEM] + [VMEM] * 3, parts,
                        [pltpu.VMEM((4, ROWS, 2 * FT), F32)])
    parts, out_g = finish(sum_qkv_kernel, q_sums, (ROWS, D), (gate_g,), (input_grad,))
    query_g, key_g, value_g, gain_g = call(
        join_qkv_kernel, (shape((ROWS, D), F32),) * 3 + (shape((ROWS, 128), F32),), [SMEM] + [VMEM] * 3, parts)
    return (layer_out, input_grad, v1_out, gain_g[:, 0], query_g, key_g, value_g, out_g, gain_g[:, 1], gate_g, up_g, down_g)


def local(plan, layer_in, *rest):
    kept = plan.G == FAST_G and plan.T == FAST_T and layer_in.shape == (2, FAST_L, D) and rest[12].shape == (FROWS, D)
    return (fast if kept else general)(plan, layer_in, *rest)


def solution(mesh):
    plan = Plan(mesh.shape["gx"], mesh.shape["gy"])
    tokens, rows, vector = P(None, ALL, None), P(ALL, None), P(ALL)
    return jax.shard_map(
        functools.partial(local, plan),
        mesh=mesh,
        in_specs=(tokens, tokens, tokens, tokens, P(), vector, rows, rows, rows, rows, vector, rows, rows, rows),
        out_specs=(tokens, tokens, tokens, vector, rows, rows, rows, rows, vector, rows, rows, rows),
        check_vma=False,
    )
```

```python
import functools

import jax
import jax.numpy as jnp
from jax import lax
from jax.experimental import pallas as pl
from jax.experimental.pallas import tpu as pltpu
from jax.sharding import PartitionSpec as P

H = 16
EPS = 1e-05
NEG = -1e30
SCALE = 0.125
ALL = ("gx", "gy")
F32 = jnp.float32
BF16 = jnp.bfloat16


class Plan:
    def __init__(self, n_gx, n_gy):
        self.G, self.T = n_gx, n_gy // 2
        every = [(g, h, t) for g in range(self.G) for h in range(2) for t in range(self.T)]
        at = lambda g, h, t: g * n_gy + h * self.T + t
        self.g_swap = {k: [(at(g, h, t), at(g ^ k, h, t)) for g, h, t in every] for k in range(1, self.G)}
        self.t_swap = {k: [(at(g, h, t), at(g, h, t ^ k)) for g, h, t in every] for k in range(1, self.T)}
        self.h_swap = [(at(g, h, t), at(g, 1 - h, t)) for g, h, t in every]
        self.bits = []
        bit = self.T // 2
        while bit:
            self.bits.append(bit)
            bit //= 2


def pick(array, index, axis=0):
    return lax.dynamic_index_in_dim(array, index, axis, keepdims=False)


def send(array, pairs):
    return lax.ppermute(array, ALL, pairs)


def dot(a, b):
    return lax.dot_general(a, b, (((1,), (0,)), ((), ())), preferred_element_type=F32)


def dot_rows(a, b):
    return lax.dot_general(a, b, (((0,), (0,)), ((), ())), preferred_element_type=F32)


def dot_cols(a, b):
    return lax.dot_general(a, b, (((1,), (1,)), ((), ())), preferred_element_type=F32)


def rotate(values, cosine, sine):
    half = values.shape[-1] // 2
    a, b = values[..., :half], values[..., half:]
    return jnp.concatenate([a * cosine - b * sine, b * cosine + a * sine], axis=-1)


def general(plan, layer_in, first_layer_value, v1_acc, cotangent, seq_starts, norm1_gain, w_query, w_key, w_value,
          w_out, norm2_gain, w_gate, w_up, w_down):
    G, T, bits = plan.G, plan.T, plan.bits
    micro, L, D = layer_in.shape
    FF = w_gate.shape[1]
    HT, FT, heads = D // T, FF // T, H // T
    HD = D // H
    M = 2 * L
    N = T * M
    rows, frows = w_query.shape[0], w_down.shape[0]
    g, gy = lax.axis_index("gx"), lax.axis_index("gy")
    h, t = gy // T, gy % T

    def to_t(array, bit):
        return send(array, plan.t_swap[bit])

    def to_g(array, k):
        return send(array, plan.g_swap[k]) if k else array

    def to_h(array):
        return send(array, plan.h_swap)

    def inward(array):
        return jnp.concatenate([pick(array, h), to_h(pick(array, 1 - h))], axis=0)

    def outward(array):
        own, other = array[:L], to_h(array[L:])
        return jnp.stack([jnp.where(h == 0, own, other), jnp.where(h == 0, other, own)])

    def gather_t(array):
        parts = {0: array}
        for bit in bits:
            order = sorted(parts)
            moved = to_t(jnp.concatenate([parts[j] for j in order], axis=0), bit)
            size = array.shape[0]
            for i, j in enumerate(order):
                parts[j ^ bit] = moved[i * size:(i + 1) * size]
        return [parts[j] for j in range(T)]

    def reduce_t(partial):
        blocks = partial.reshape((T, -1) + partial.shape[1:])
        for bit in reversed(bits):
            shape = blocks.shape
            split = blocks.reshape((shape[0] // 2, 2) + shape[1:])
            blocks = split[:, 0] + to_t(split[:, 1].astype(BF16), bit).astype(F32)
        return blocks[0]

    def exchange_t(parts):
        held = {j: [parts[j]] for j in range(T)}
        sources = [0]
        for bit in bits:
            out = [j for j in sorted(held) if j & bit]
            flat = [p for j in out for p in held[j]]
            moved = to_t(jnp.stack(flat), bit)
            n = len(sources)
            new = {}
            for i, j in enumerate(out):
                new[j ^ bit] = held[j ^ bit] + [moved[i * n + s] for s in range(n)]
            sources = sources + [s ^ bit for s in sources]
            held = new
        result = [None] * T
        for s, p in zip(sources, held[0]):
            result[s] = p
        return result

    def natural(parts):
        array = jnp.stack(parts)
        for bit in bits:
            split = array.reshape((-1, 2, bit) + array.shape[1:])
            array = jnp.where((t & bit) != 0, split[:, ::-1], split).reshape(array.shape)
        return array

    def gather_r(block):
        other = to_h(block)
        pair = jnp.where(h == 0, jnp.stack([block, other]), jnp.stack([other, block]))
        full = jnp.zeros((G,) + pair.shape, pair.dtype)
        for k in range(G):
            full = lax.dynamic_update_slice(full, to_g(pair, k)[None], (g ^ k,) + (0,) * pair.ndim)
        return full.reshape((G * 2 * block.shape[0],) + block.shape[1:])

    def gather_cols(slices):
        block = natural(exchange_t([pick(slices, t ^ j) for j in range(T)]))
        return gather_r(block.reshape(T * block.shape[1], -1))

    def reduce_r(grad):
        n, w = grad.shape[0] // (2 * G), grad.shape[1]
        grad = grad.astype(BF16).reshape(G, 2 * n, w)
        total = pick(grad, g).astype(F32)
        for k in range(1, G):
            total = total + to_g(pick(grad, g ^ k), k).astype(F32)
        total = total.reshape(2, n, w)
        return pick(total, h) + to_h(pick(total, 1 - h).astype(BF16)).astype(F32)

    def scatter_cols(grad):
        total = reduce_r(grad).reshape(T, rows, -1)
        low = total.astype(BF16)
        return natural(exchange_t([pick(low, t ^ j) for j in range(T)])).astype(F32)

    pad = jnp.zeros((rows, 126), BF16)
    gains_in = jnp.concatenate([norm1_gain[:, None], norm2_gain[:, None], pad], axis=1)

    def col_slices(w):
        return w.reshape(rows, T, HT).transpose(1, 0, 2)

    def hidden_slices(w):
        return w.reshape(rows, 2 * G, T, frows).transpose(2, 0, 1, 3).reshape(T, rows, FT)

    qkv_slices = jnp.concatenate([col_slices(w_query), col_slices(w_key), col_slices(w_value),
                                  jnp.broadcast_to(gains_in[None], (T, rows, 128))], axis=2)
    x_own = inward(layer_in)
    qkv_w = gather_cols(qkv_slices)
    x_all = jnp.concatenate(gather_t(x_own), axis=0)
    v_own = inward(first_layer_value).reshape(M, T, HT).transpose(1, 0, 2)
    v_all = jnp.concatenate(exchange_t([pick(v_own, t ^ j) for j in range(T)]), axis=0)
    gu_w = gather_cols(jnp.concatenate([hidden_slices(w_gate), hidden_slices(w_up)], axis=2))
    down_w = gather_r(w_down)
    c_own = inward(cotangent)
    c_all = jnp.concatenate(gather_t(c_own), axis=0)
    out_w = natural(gather_t(gather_r(w_out))).reshape(T, 2 * G, rows, D).transpose(1, 0, 2, 3).reshape(D, D)
    out_w = out_w.reshape(T, HT, D)

    gains = qkv_w[:, 3 * HT:3 * HT + 2].astype(F32).T
    gain_one, gain_two = gains[0], gains[1]
    query_w, key_w, value_w = qkv_w[:, :HT], qkv_w[:, HT:2 * HT], qkv_w[:, 2 * HT:3 * HT]
    gate_w, up_w = gu_w[:, :FT], gu_w[:, FT:]

    starts = pick(seq_starts, h)
    member = t ^ jnp.arange(T, dtype=jnp.int32)
    half = h ^ jnp.arange(2, dtype=jnp.int32)
    position = ((half[None, :] * T + member[:, None]) * L)[:, :, None] + jnp.arange(L, dtype=jnp.int32)
    position = position.reshape(N) + g * N
    begin = jnp.max(jnp.where(starts[None, :] <= position[:, None], starts[None, :], 0), axis=1)
    rel = (position - begin).astype(F32)
    visible = (begin[:, None] == begin[None, :]) & (position[None, :] <= position[:, None])
    frequency = 10000.0 ** (-(jnp.arange(HD // 2, dtype=F32) * 2.0 / HD))
    angles = rel[:, None] * frequency[None, :]
    cosine, sine = jnp.cos(angles)[:, None, :], jnp.sin(angles)[:, None, :]

    x = x_all.astype(F32)
    rstd_one = lax.rsqrt(jnp.mean(x * x, axis=-1, keepdims=True) + EPS)
    normed_one = (x * rstd_one * gain_one).astype(BF16)
    query = rotate(dot(normed_one, query_w).reshape(N, heads, HD), cosine, sine).astype(BF16)
    key = rotate(dot(normed_one, key_w).reshape(N, heads, HD), cosine, sine).astype(BF16)
    value = (0.5 * dot(normed_one, value_w) + 0.5 * v_all.astype(F32)).astype(BF16).reshape(N, heads, HD)
    scores = jnp.einsum("ihd,jhd->hij", query, key, preferred_element_type=F32) * SCALE
    scores = jnp.where(visible[None], scores, NEG)
    top = jnp.max(scores, axis=-1, keepdims=True)
    probs = jnp.exp(scores - top)
    denom = jnp.sum(probs, axis=-1, keepdims=True)
    probs = probs / denom
    probs_low = probs.astype(BF16)
    attn = jnp.einsum("hij,jhd->ihd", probs_low, value, preferred_element_type=F32)
    attn_low = attn.reshape(N, HT).astype(BF16)
    attn_parts = []
    for j, part in enumerate(gather_t(attn_low)):
        part = part.reshape(T, M, HT)
        attn_parts.append(jnp.concatenate([part[b ^ j] for b in range(T)], axis=0))
    after = x
    for j in range(T):
        after = after + dot(attn_parts[j], pick(out_w, t ^ j))
    rstd_two = lax.rsqrt(jnp.mean(after * after, axis=-1, keepdims=True) + EPS)
    hat_two = after * rstd_two
    normed_two = (hat_two * gain_two).astype(BF16)
    gate = dot(normed_two, gate_w)
    up = dot(normed_two, up_w)
    sig = jax.nn.sigmoid(gate)
    act = gate * sig
    hidden = (act * up).astype(BF16)

    grad_hidden = dot_cols(c_all, down_w)
    grad_gate = (grad_hidden * up * (sig * (1.0 + gate * (1.0 - sig)))).astype(BF16)
    grad_up = (grad_hidden * act).astype(BF16)
    grad_two_part = dot_cols(grad_gate, gate_w) + dot_cols(grad_up, up_w)
    gain_two_grad = jnp.sum(grad_two_part * hat_two, axis=0)
    grad_two = reduce_t(grad_two_part) * gain_two
    hat_own = hat_two[:M]
    grad_after = c_own.astype(F32) + rstd_two[:M] * (
        grad_two - hat_own * jnp.mean(grad_two * hat_own, axis=-1, keepdims=True))
    grad_branch = jnp.concatenate(gather_t(grad_after.astype(BF16)), axis=0)
    result = reduce_t(dot(hidden, down_w)) + after[:M]
    layer_out = outward(result.astype(BF16))
    grad_down = dot_rows(hidden, c_all)
    grad_gu = dot_rows(normed_two, jnp.concatenate([grad_gate, grad_up], axis=1))

    grad_attn = dot_cols(grad_branch, pick(out_w, t)).astype(BF16).reshape(N, heads, HD)
    delta = jnp.sum(grad_attn.astype(F32) * attn, axis=-1).T
    grad_probs = jnp.einsum("ihd,jhd->hij", grad_attn, value, preferred_element_type=F32)
    grad_scores = (probs * (grad_probs - delta[..., None])).astype(BF16)
    grad_query = jnp.einsum("hij,jhd->ihd", grad_scores, key, preferred_element_type=F32) * SCALE
    grad_key = jnp.einsum("hij,ihd->jhd", grad_scores, query, preferred_element_type=F32) * SCALE
    grad_blend = jnp.einsum("hij,ihd->jhd", probs_low, grad_attn, preferred_element_type=F32).reshape(N, HT)
    grad_query = rotate(grad_query, cosine, -sine).reshape(N, HT).astype(BF16)
    grad_key = rotate(grad_key, cosine, -sine).reshape(N, HT).astype(BF16)
    grad_value = (0.5 * grad_blend).astype(BF16)
    grad_one_part = dot_cols(grad_query, query_w) + dot_cols(grad_key, key_w) + dot_cols(grad_value, value_w)
    hat_one = x * rstd_one
    gain_one_grad = jnp.sum(grad_one_part * hat_one, axis=0)
    grad_one = reduce_t(grad_one_part) * gain_one
    hat_own = hat_one[:M]
    input_grad = grad_after + rstd_one[:M] * (
        grad_one - hat_own * jnp.mean(grad_one * hat_own, axis=-1, keepdims=True))
    input_grad = outward(input_grad.astype(BF16)).astype(F32)
    v_parts = natural(exchange_t([grad_value[j * M:(j + 1) * M] for j in range(T)]))
    v1_out = v1_acc + outward(v_parts.transpose(1, 0, 2).reshape(M, D)).astype(F32)

    attn_full = natural([p.T for p in attn_parts]).reshape(2 * G, T, rows, N)
    grad_out = dot(pick(attn_full, t, 1).reshape(2 * G * rows, N), grad_branch)
    grad_gains = jnp.stack([gain_one_grad, gain_two_grad], axis=1)
    grad_gains = jnp.concatenate([grad_gains, jnp.zeros((D, 126), F32)], axis=1)
    grad_qkv = dot_rows(normed_one, jnp.concatenate([grad_query, grad_key, grad_value], axis=1))
    down_g = reduce_r(grad_down)
    gu_g = scatter_cols(grad_gu)
    out_g = reduce_r(grad_out)
    qkv_g = scatter_cols(jnp.concatenate([grad_qkv, grad_gains], axis=1))

    def col_join(parts):
        return parts.transpose(1, 0, 2).reshape(rows, D)

    def hidden_join(parts):
        return parts.reshape(T, rows, 2 * G, frows).transpose(1, 2, 0, 3).reshape(rows, FF)

    gain_g = jnp.sum(qkv_g[:, :, 3 * HT:3 * HT + 2], axis=0)
    return (layer_out, input_grad, v1_out, gain_g[:, 0], col_join(qkv_g[:, :, :HT]), col_join(qkv_g[:, :, HT:2 * HT]),
            col_join(qkv_g[:, :, 2 * HT:3 * HT]), out_g, gain_g[:, 1], hidden_join(gu_g[:, :, :FT]),
            hidden_join(gu_g[:, :, FT:]), down_g)


FAST_G, FAST_T, FAST_L, D, HT, FT, FROWS, ROWS = 4, 4, 64, 1024, 256, 704, 88, 32
M, N = 2 * FAST_L, 8 * FAST_L
HALF = N // 2
WQ = 3 * HT + 128
ORDER = (0, 2, 1, 3)
HD = 64
ARRIVED = ((0, 0), (1, 0), (2, 0), (3, 0), (0, 1), (2, 1), (1, 1), (3, 1))
LEAVING = {(0, 0): (0, 0), (1, 0): (0, 1), (2, 0): (1, 0), (3, 0): (1, 1), (0, 1): (2, 0), (2, 1): (2, 1), (1, 1): (3, 0), (3, 1): (3, 1)}
VMEM = pl.BlockSpec(memory_space=pltpu.VMEM)
SMEM = pl.BlockSpec(memory_space=pltpu.SMEM)
ANY = pl.BlockSpec(memory_space=pltpu.HBM)


def shape(dims, dtype=BF16):
    return jax.ShapeDtypeStruct(dims, dtype)


def call(kernel, outs, specs, args, scratch=(), mib=40):
    return pl.pallas_call(
        kernel,
        out_shape=outs,
        in_specs=specs,
        out_specs=jax.tree.map(lambda _: VMEM, outs),
        scratch_shapes=list(scratch),
        compiler_params=pltpu.CompilerParams(vmem_limit_bytes=mib << 20),
        cost_estimate=pl.CostEstimate(flops=1, bytes_accessed=1, transcendentals=0),
    )(*args)


def aligned(index, size):
    return pl.ds(pl.multiple_of(index * size, size), size)


def eye(rows, lanes):
    return (lax.broadcasted_iota(jnp.int32, (rows, lanes), 0) == lax.broadcasted_iota(jnp.int32, (rows, lanes), 1)).astype(BF16)


def tiles_in(block):
    lines = [jnp.concatenate([block[j * 8:j * 8 + 8, i * 128:i * 128 + 128] for j in range(11)], axis=1) for i in range(8)]
    return jnp.concatenate(lines, axis=0)


def tiles_out(block):
    lines = [jnp.concatenate([block[i * 8:i * 8 + 8, j * 128:j * 128 + 128] for i in range(8)], axis=1) for j in range(11)]
    return jnp.concatenate(lines, axis=0)


def line_tiles_in(block):
    tiles = [block[j * 8:j * 8 + 8, i * 128:i * 128 + 128] for j in range(4) for i in range(8)]
    tiles += [jnp.zeros_like(tiles[0])] * 3
    return jnp.concatenate([jnp.concatenate(tiles[n * 7:n * 7 + 7], axis=1) for n in range(5)], axis=0)


def line_tiles_out(block):
    tiles = [block[n * 8:n * 8 + 8, i * 128:i * 128 + 128] for n in range(5) for i in range(7)]
    return jnp.concatenate([jnp.concatenate(tiles[j * 8:j * 8 + 8], axis=1) for j in range(4)], axis=0)


def pack_first(ids, gain_one, gain_two, wq, wk, wv, wo, x, v, c, out, keep, lines, xv_out, c_out, rows, whole, sem):
    h, t = ids[1], ids[2]
    copies = []
    for j in (2, 3, 0, 1):
        to = keep if j < 2 else out
        for i, w in enumerate((wq, wk, wv)):
            copies.append((w.at[:, aligned(t ^ j, HT)], to.at[j % 2, :, i * HT:(i + 1) * HT]))
    copies += [(wo, whole), (x.at[1 - h], xv_out.at[:, :D]), (v.at[1 - h], xv_out.at[:, D:]), (c.at[1 - h], c_out)]
    started = fetch(copies, sem)
    rows[...] = jnp.zeros_like(rows)
    rows[0:1] = gain_one[...].astype(F32)
    rows[1:2] = gain_two[...].astype(F32)
    gains = dot_rows(rows[...].astype(BF16), eye(8, 128)).astype(BF16)
    for j in range(4):
        (keep if j < 2 else out)[j % 2, :, 3 * HT:] = gains
    started[12].wait()
    lines[...] = line_tiles_in(whole[...].astype(F32)).astype(BF16)
    for n, copy in enumerate(started):
        if n != 12:
            copy.wait()


def pack_hidden(ids, wg, wu, wd, keep, out, down, nat, gate, up, whole, sem):
    t = ids[2]
    started = fetch([(wg, gate), (wu, up), (wd, whole)], sem)
    for a, w in enumerate((gate, up)):
        started[a].wait()
        for m in range(4):
            for i in range(8):
                at, to = (i * 4 + m) * FROWS, a * FT + i * FROWS
                nat[m, :, to:to + FROWS] = w[:, at:at + FROWS].astype(F32)
    for j in range(4):
        to = keep if j < 2 else out
        to[j % 2] = nat[t ^ j].astype(BF16)
    started[2].wait()
    down[...] = tiles_in(whole[...].astype(F32)).astype(BF16)


def pack_block(kept, first, last, tail, out, sem):
    width = ROWS
    parts = (kept.at[0], first.at[0], last.at[0], last.at[1], tail)
    started = fetch([(part, out.at[i * width:i * width + part.shape[0]]) for i, part in enumerate(parts)], sem)
    for copy in started:
        copy.wait()


def pack_pair(kept, first, out, sem):
    started = fetch([(kept.at[1], out.at[0]), (first.at[1], out.at[1])], sem)
    for copy in started:
        copy.wait()


def pack_out(b0, b1, b2, b3, out, raw, sem):
    started = fetch([((b0, b1, b2, b3)[n // 2].at[n % 2, 4 * ROWS:], raw.at[n]) for n in range(8)], sem)
    for n in range(8):
        started[n].wait()
        out[n * ROWS:(n + 1) * ROWS] = line_tiles_out(raw[n].astype(F32)).astype(BF16)


def pack_second(ids, x, v, moved, xv_out, v_keep, own, sem):
    h, t = ids[1], ids[2]
    started = fetch([(x.at[h], xv_out.at[:FAST_L, :D]), (v.at[h], own.at[:FAST_L]),
                     (moved.at[:, :D], xv_out.at[FAST_L:, :D]), (moved.at[:, D:], own.at[FAST_L:])], sem)
    for copy in started:
        copy.wait()
    for j in range(2):
        v_keep[j] = own[:, aligned(t ^ j, HT)]
        xv_out[:, D + j * HT:D + (j + 1) * HT] = own[:, aligned(t ^ (j + 2), HT)]


def pack_third(mine, moved, v_keep, out, v_two):
    out[:M, :D] = mine[:, :D]
    out[M:, :D] = moved[:, :D]
    out[:M, D:] = v_keep[1]
    out[M:, D:] = moved[:, D + HT:]
    v_two[:M] = v_keep[0]
    v_two[M:] = moved[:, D:D + HT]


def fetch(copies, sem):
    started = []
    for i, (source, target) in enumerate(copies):
        copy = pltpu.make_async_copy(source, target, sem.at[i])
        copy.start()
        started.append(copy)
    return started


def swap_halves(u):
    width = u.shape[-1]
    lane = lax.broadcasted_iota(jnp.int32, u.shape, 1)
    up = pltpu.roll(u, width - HD // 2, 1)
    down = pltpu.roll(u, HD // 2, 1)
    return jnp.where(lane % HD < HD // 2, up, down)


def scale_of(x):
    return lax.rsqrt(jnp.mean(x * x, axis=-1, keepdims=True) + EPS)


def attend_kernel(ids, x2, xc, v2, cs, sn, bias, b0, b1, b2, b3, w, normed, qkv, attn, low, lse, gains, sem):
    g, h, t = ids[0], ids[1], ids[2]
    copies = []
    for n, (k, dh) in enumerate(ARRIVED):
        b = (b0, b1, b2, b3)[n // 2]
        for i, s in enumerate(ORDER):
            row = ((g ^ k) * 2 + (h ^ dh)) * 4 + (t ^ s)
            copies.append((b.at[n % 2, i * ROWS:(i + 1) * ROWS], w.at[aligned(row, ROWS)]))
    for copy in fetch(copies, sem):
        copy.wait()
    gains[...] = dot_cols(eye(8, 128), w[:, 3 * HT:])
    gain = gains[0:1, :]
    for b in range(2):
        rows = slice(b * HALF, (b + 1) * HALF)
        source = x2 if b == 0 else xc
        x = source[:, :D].astype(F32)
        r = (x * scale_of(x) * gain).astype(BF16)
        normed[rows] = r
        out = dot(r, w[:, :3 * HT])
        for i in range(2):
            u = out[:, i * HT:(i + 1) * HT]
            qkv[rows, i * HT:(i + 1) * HT] = (u * cs[rows] + swap_halves(u) * sn[rows]).astype(BF16)
        value = v2[...] if b == 0 else xc[:, D:]
        qkv[rows, 2 * HT:] = (0.5 * out[:, 2 * HT:] + 0.5 * value.astype(F32)).astype(BF16)
    outs, tops = [], []
    mask = bias[...].astype(F32)
    for i in range(4):
        q, k, v = (qkv[:, n * HT + i * HD:n * HT + (i + 1) * HD] for n in range(3))
        s = dot_cols(q, k) * SCALE + mask
        top = jnp.max(s, axis=-1, keepdims=True)
        p = jnp.exp(s - top)
        total = jnp.sum(p, axis=-1, keepdims=True)
        outs.append(dot(p.astype(BF16), v) / total)
        tops.append(top + jnp.log(total))
    o = jnp.concatenate(outs, axis=1)
    attn[...] = o
    low[...] = o.astype(BF16)
    lse[...] = jnp.concatenate(tops, axis=1)


def after_kernel(ids, x2, xc, o2, oc, gains, co2, coc, full, after, normed, own_w, w, sem):
    g, h, t = ids[0], ids[1], ids[2]
    copies = []
    for i, s in enumerate(ORDER):
        source = co2 if i < 2 else coc
        for n, (k, dh) in enumerate(ARRIVED):
            row = ((g ^ k) * 2 + (h ^ dh)) * 4 + (t ^ s)
            at = (i % 2) * HT + n * ROWS
            copies.append((source.at[at:at + ROWS], w.at[aligned(row, ROWS)]))
    started = fetch(copies, sem)
    for i, s in enumerate(ORDER):
        source = o2 if i < 2 else oc
        for p in range(4):
            q = ORDER.index(ORDER[p] ^ s)
            full[p * M:(p + 1) * M, aligned(t ^ s, HT)] = source[(i % 2) * N + q * M:(i % 2) * N + (q + 1) * M]
    for copy in started:
        copy.wait()
    own_w[...] = w[aligned(t, HT)]
    gain = gains[1:2, :]
    for b in range(2):
        rows = slice(b * HALF, (b + 1) * HALF)
        source = x2 if b == 0 else xc
        a = source[:, :D].astype(F32) + dot(full[rows], w[...])
        if b == 0:
            after[...] = a[:M]
        normed[rows] = (a * scale_of(a) * gain).astype(BF16)


def feed_kernel(ids, normed, gains, c2, cc, u0, u1, u2, u3, out_keep, out_send, r_keep, r_send, gain_g, a_keep, a_send, b_keep, b_send,
                w, wd, wide, raw, hidden, dgu, gu_g, sem, sem_d):
    g, h, t = ids[0], ids[1], ids[2]
    copies, copies_d = [], []
    for n, (k, dh) in enumerate(ARRIVED):
        b = (u0, u1, u2, u3)[n // 2]
        for i, s in enumerate(ORDER):
            row = ((g ^ k) * 2 + (h ^ dh)) * 4 + (t ^ s)
            copies.append((b.at[n % 2, i * ROWS:(i + 1) * ROWS], w.at[aligned(row, ROWS)]))
        copies_d.append((b.at[n % 2, 4 * ROWS:], raw.at[n]))
    started_d, started = fetch(copies_d, sem_d), fetch(copies, sem)
    for n, (k, dh) in enumerate(ARRIVED):
        started_d[n].wait()
        wide[aligned((g ^ k) * 2 + (h ^ dh), FROWS)] = tiles_out(raw[n].astype(F32))
    wd[...] = wide[...].astype(BF16)
    for copy in started:
        copy.wait()
    gain_sum = jnp.zeros((1, D), F32)
    for b in range(2):
        rows = slice(b * HALF, (b + 1) * HALF)
        c = (c2 if b == 0 else cc)[...]
        gu = dot(normed[rows], w[...])
        gate, up = gu[:, :FT], gu[:, FT:]
        sig = 1.0 / (1.0 + jnp.exp(-gate))
        act = gate * sig
        hid = (act * up).astype(BF16)
        hidden[rows] = hid
        dh = dot_cols(c, wd[...])
        dgu[rows, :FT] = (dh * up * (sig * (1.0 + gate * (1.0 - sig)))).astype(BF16)
        dgu[rows, FT:] = (dh * act).astype(BF16)
        dr = dot_cols(dgu[rows], w[...])
        out = dot(hid, wd[...])
        gain_sum = gain_sum + jnp.sum(dr * normed[rows].astype(F32), axis=0, keepdims=True)
        (r_keep if b == 0 else r_send)[...] = dr.astype(BF16)
        (out_keep if b == 0 else out_send)[...] = out.astype(BF16)
    gain_g[...] = gain_sum / gains[1:2, :]
    wide[...] = dot_rows(hidden[:HALF], c2[...]) + dot_rows(hidden[HALF:], cc[...])
    for k in range(4):
        gu_g[...] = dot_rows(normed[:, aligned(g ^ k, HT)], dgu[...])
        for e in range(2):
            target, at = LEAVING[(k, e)]
            target = (a_keep, a_send, b_keep, b_send)[target]
            target[at, :4 * ROWS] = gu_g[aligned(h ^ e, 4 * ROWS)].astype(BF16)
            target[at, 4 * ROWS:] = tiles_in(wide[aligned((g ^ k) * 2 + (h ^ e), FROWS)]).astype(BF16)


def fold_kernel(keep, moved, kept, send):
    kept[...] = keep[:M].astype(F32) + moved[:M].astype(F32)
    send[...] = (keep[M:].astype(F32) + moved[M:].astype(F32)).astype(BF16)


def fold_both_kernel(keep, dv, moved, kept, send):
    kept[...] = keep[:M].astype(F32) + moved[:M, :D].astype(F32)
    send[:, :D] = (keep[M:].astype(F32) + moved[M:, :D].astype(F32)).astype(BF16)
    send[:, D:D + HT] = dv[M:]
    send[:, D + HT:] = moved[M:, D:]


def branch_kernel(keep, moved, after, gains, c2, grad_after, low):
    a = after[...]
    scale = scale_of(a)
    hat = a * scale
    dy = (keep[...] + moved[...].astype(F32)) * gains[1:2, :]
    d = c2[:M].astype(F32) + scale * (dy - hat * jnp.mean(dy * hat, axis=-1, keepdims=True))
    grad_after[...] = d
    low[...] = d.astype(BF16)


def attend_back_kernel(ids, da2, dac, wo, qkv, attn, lse, bias, cs, sn, w, normed, gains, gain_two, full,
                       r_keep, r_send, dv_keep, a_keep, a_send, b_keep, b_send, do, dk, dv, dqkv, scratch, rows_g, qkv_g):
    g, h, t = ids[0], ids[1], ids[2]
    for b in range(2):
        rows = slice(b * HALF, (b + 1) * HALF)
        do[rows] = dot_cols((da2 if b == 0 else dac)[...], wo[...]).astype(BF16)
    dqs = []
    mask = bias[...].astype(F32)
    for i in range(4):
        lanes = slice(i * HD, (i + 1) * HD)
        q, k, v = (qkv[:, n * HT + i * HD:n * HT + (i + 1) * HD] for n in range(3))
        d = do[:, lanes]
        delta = jnp.sum(d.astype(F32) * attn[:, lanes], axis=-1, keepdims=True)
        p = jnp.exp(dot_cols(q, k) * SCALE + mask - lse[:, i:i + 1])
        ds = (p * (dot_cols(d, v) - delta)).astype(BF16)
        dqs.append(dot(ds, k))
        dk[:, lanes], dv[:, lanes] = dot_rows(ds, q), dot_rows(p.astype(BF16), d)
    u = jnp.concatenate(dqs, axis=1) * SCALE
    dqkv[:, :HT] = (u * cs[...] - swap_halves(u) * sn[...]).astype(BF16)
    gain_sum = jnp.zeros((1, D), F32)
    for b in range(2):
        rows = slice(b * HALF, (b + 1) * HALF)
        u = dk[rows] * SCALE
        dqkv[rows, HT:2 * HT] = (u * cs[rows] - swap_halves(u) * sn[rows]).astype(BF16)
        dqkv[rows, 2 * HT:] = (0.5 * dv[rows]).astype(BF16)
        dr = dot_cols(dqkv[rows], w[:, :3 * HT])
        gain_sum = gain_sum + jnp.sum(dr * normed[rows].astype(F32), axis=0, keepdims=True)
        if b == 0:
            r_keep[...] = dr.astype(BF16)
            dv_keep[...] = dqkv[rows, 2 * HT:]
        else:
            r_send[:, :D] = dr.astype(BF16)
            r_send[:, D:] = dqkv[rows, 2 * HT:]
    rows_g[...] = jnp.zeros_like(rows_g)
    rows_g[0:1] = gain_sum / gains[0:1, :]
    rows_g[1:2] = gain_two[...]
    for k in range(4):
        lanes = aligned(g ^ k, HT)
        qkv_g[:, :3 * HT] = dot_rows(normed[:, lanes], dqkv[...])
        qkv_g[:, 3 * HT:] = dot_rows(rows_g[:, lanes].astype(BF16), eye(8, 128))
        scratch[...] = dot_rows(full[:HALF, lanes], da2[...]) + dot_rows(full[HALF:, lanes], dac[...])
        for e in range(2):
            target, at = LEAVING[(k, e)]
            target = (a_keep, a_send, b_keep, b_send)[target]
            target[at, :4 * ROWS] = qkv_g[aligned(h ^ e, 4 * ROWS)].astype(BF16)
            target[at, 4 * ROWS:] = line_tiles_in(scratch[aligned((h ^ e) * 4 + t, ROWS)]).astype(BF16)


def sum_first_kernel(a_keep, a_moved, b_keep, b_moved, a_own, a_send, b_own, b_send):
    for keep, moved, own, out in ((a_keep, a_moved, a_own, a_send), (b_keep, b_moved, b_own, b_send)):
        own[...] = (keep[0].astype(F32) + moved[0].astype(F32)).astype(BF16)
        out[...] = (keep[1].astype(F32) + moved[1].astype(F32)).astype(BF16)


def sum_second_kernel(b_own, b_moved, b_send):
    b_send[...] = (b_own[...].astype(F32) + b_moved[...].astype(F32)).astype(BF16)


def sum_third(a_own, a_moved, moved, total):
    total[...] = (a_own[...].astype(F32) + a_moved[...].astype(F32)) + moved[...].astype(F32)


def sum_hidden_kernel(ids, a_own, a_moved, moved, kept, send, down, total):
    t = ids[2]
    sum_third(a_own, a_moved, moved, total)
    for j in range(4):
        (kept if j < 2 else send)[j % 2] = total[aligned(t ^ j, ROWS)].astype(BF16)
    down[...] = tiles_out(total[4 * ROWS:])


def sum_qkv_kernel(ids, a_own, a_moved, moved, kept, send, out, total):
    t = ids[2]
    sum_third(a_own, a_moved, moved, total)
    for j in range(4):
        (kept if j < 2 else send)[j % 2] = total[aligned(t ^ j, ROWS)].astype(BF16)
    out[...] = line_tiles_out(total[4 * ROWS:])


def join_qkv_kernel(ids, kept, first, last, q, k, v, gain_one, gain_two):
    t = ids[2]
    parts = (kept[0], first[0], last[0], last[1])
    for s, part in zip(ORDER, parts):
        for i, ref in enumerate((q, k, v)):
            ref[:, aligned(t ^ s, HT)] = part[:, i * HT:(i + 1) * HT].astype(F32)
    low = [part[:, 3 * HT:].astype(F32) for part in parts]
    total = jnp.transpose((low[0] + low[1]) + (low[2] + low[3]))
    gain_one[...] = total[0:1]
    gain_two[...] = total[1:2]


def join_hidden_kernel(ids, kept, first, last, gate, up, nat):
    t = ids[2]
    for s, part in zip(ORDER, (kept[0], first[0], last[0], last[1])):
        nat[t ^ s] = part.astype(F32)
    for m in range(4):
        for a, ref in enumerate((gate, up)):
            for i in range(8):
                to, at = (i * 4 + m) * FROWS, a * FT + i * FROWS
                ref[:, to:to + FROWS] = nat[m, :, at:at + FROWS]


def input_kernel(ids, keep, moved, x2, gains, grad_after, dv, dv_core, own, send, both):
    t = ids[2]
    x = x2[:M, :D].astype(F32)
    scale = scale_of(x)
    hat = x * scale
    dy = (keep[...] + moved[:, :D].astype(F32)) * gains[0:1, :]
    both[:, :D] = (grad_after[...] + scale * (dy - hat * jnp.mean(dy * hat, axis=-1, keepdims=True))).astype(BF16)
    parts = (dv[:M], moved[:, D:D + HT], dv_core[:M, D:], moved[:, D + HT:])
    for s, part in zip(ORDER, parts):
        both[:, aligned(4 + (t ^ s), HT)] = part
    own[...] = both[:FAST_L]
    send[...] = both[FAST_L:]


def home_kernel(ids, own, moved, v1, grad, v_out):
    h = ids[1]
    grad[h] = own[:, :D].astype(F32)
    grad[1 - h] = moved[:, :D].astype(F32)
    v_out[h] = v1[h] + own[:, D:].astype(F32)
    v_out[1 - h] = v1[1 - h] + moved[:, D:].astype(F32)


def result_kernel(keep, moved, after, own, send):
    out = after[...] + (keep[...] + moved[...].astype(F32))
    own[...] = out[:FAST_L].astype(BF16)
    send[...] = out[FAST_L:].astype(BF16)


def result_home_kernel(ids, own, moved, out):
    h = ids[1]
    out[h] = own[...]
    out[1 - h] = moved[...]


def fast(plan, layer_in, first_layer_value, v1_acc, cotangent, seq_starts, norm1_gain, w_query, w_key, w_value,
         w_out, norm2_gain, w_gate, w_up, w_down):
    L = FAST_L
    g, gy = lax.axis_index("gx"), lax.axis_index("gy")
    h, t = gy // 4, gy % 4
    ids = jnp.stack([g, h, t]).astype(jnp.int32)

    def to_z(array):
        return send(array, plan.t_swap[2])

    def to_core(array):
        return send(array, plan.t_swap[1])

    def to_h(array):
        return send(array, plan.h_swap)

    def to_x(array):
        return send(array, plan.g_swap[1])

    def to_y(array):
        return send(array, plan.g_swap[2])

    def after_these(array, *others):
        return lax.optimization_barrier((array,) + others)[0]

    def fenced(part, *inputs):
        results = jax.eval_shape(part, *inputs)
        nothing = lambda *_: jax.tree.map(lambda a: jnp.zeros(a.shape, a.dtype), results)
        return lax.cond(ids[0] >= 0, part, nothing, *inputs)

    def spread(own, other, *first):
        a_pair = jnp.stack([own, to_x(own)])
        b_pair = jnp.stack([other, to_y(other)])
        a_pair, b_pair = lax.optimization_barrier((a_pair, b_pair) + first)[:2]
        return a_pair, to_y(a_pair), b_pair, to_x(b_pair)

    def pair_of(kept, first):
        return call(pack_pair, shape(kept.shape), [ANY] * 2, (kept, first), [pltpu.SemaphoreType.DMA((2,))])

    def block_of(kept, first, last, tail):
        return call(pack_block, shape((4 * ROWS + tail.shape[0], tail.shape[1])), [ANY] * 4, (kept, first, last, tail),
                    [pltpu.SemaphoreType.DMA((5,))])

    q_send, q_keep, o_block, xv_send, c_send = call(
        pack_first, (shape((2, ROWS, WQ)), shape((2, ROWS, WQ)), shape((40, WQ)), shape((L, 2 * D)), shape((L, D))),
        [SMEM] + [VMEM] * 2 + [ANY] * 7,
        (ids, norm1_gain[None], norm2_gain[None], w_query, w_key, w_value, w_out, layer_in, first_layer_value, cotangent),
        [pltpu.VMEM((8, ROWS), F32), pltpu.VMEM((ROWS, D), BF16), pltpu.SemaphoreType.DMA((16,))], mib=63)
    q_first = to_z(q_send)
    xv_moved = to_h(xv_send)
    q_last = to_core(pair_of(q_keep, q_first))
    q_block = block_of(q_keep, q_first, q_last, o_block)
    q_other = to_h(q_block)

    starts = pick(after_these(seq_starts, q_block), h)
    member = t ^ jnp.array(ORDER, jnp.int32)
    half = h ^ jnp.arange(2, dtype=jnp.int32)
    position = ((half[None, :] * 4 + member[:, None]) * L)[:, :, None] + jnp.arange(L, dtype=jnp.int32)
    position = position.reshape(N) + g * N
    begin = jnp.max(jnp.where(starts[None, :] <= position[:, None], starts[None, :], 0), axis=1)
    visible = (begin[:, None] == begin[None, :]) & (position[None, :] <= position[:, None])
    bias = jnp.where(visible, 0.0, NEG).astype(BF16)
    lane = jnp.arange(HT, dtype=jnp.int32)
    frequency = 10000.0 ** (-((lane % (HD // 2)).astype(F32) * 2.0 / HD))
    angles = (position - begin).astype(F32)[:, None] * frequency[None, :]
    cs = jnp.cos(angles)
    sn = jnp.sin(angles) * jnp.where(lane % HD < HD // 2, -1.0, 1.0)[None, :]

    u_keep, u_send, d_block = call(
        pack_hidden, (shape((2, ROWS, 2 * FT)), shape((2, ROWS, 2 * FT)), shape((2 * ROWS, 2 * FT))), [SMEM] + [ANY] * 3,
        (after_these(ids, q_send), w_gate, w_up, w_down),
        [pltpu.VMEM((4, ROWS, 2 * FT), F32), pltpu.VMEM((ROWS, 4 * FT), BF16), pltpu.VMEM((ROWS, 4 * FT), BF16), pltpu.VMEM((FROWS, D), BF16),
         pltpu.SemaphoreType.DMA((3,))], mib=63)
    u_first = to_z(u_send)
    u_last = to_core(pair_of(u_keep, after_these(u_first, q_block)))
    u_block = block_of(u_keep, u_first, u_last, d_block)

    xv_out, v_keep = call(pack_second, (shape((M, D + 2 * HT)), shape((2, M, HT))), [SMEM] + [ANY] * 3,
                          (after_these(ids, u_block), layer_in, first_layer_value, xv_moved), [pltpu.VMEM((M, D), BF16), pltpu.SemaphoreType.DMA((4,))], mib=63)
    x_two, v_two = call(pack_third, (shape((HALF, D + HT)), shape((HALF, HT))), [VMEM] * 3, (xv_out, to_z(xv_out), v_keep))
    x_core = to_core(x_two)
    q_other, cs, sn, bias, _ = lax.optimization_barrier((q_other, cs, sn, bias, xv_out))
    q_parts = spread(q_block, q_other, x_two)

    u_other = to_h(after_these(u_block, q_block))
    c_moved = to_h(after_these(c_send, u_other))
    u_a = jnp.stack([u_block, to_x(after_these(u_block, q_parts[2]))])
    u_b = jnp.stack([u_other, to_y(u_other)])
    o_own = call(pack_out, shape((HT, D)), [ANY] * 4, q_parts, [pltpu.VMEM((8, 40, WQ), BF16), pltpu.SemaphoreType.DMA((8,))])
    o_first = to_z(o_own)
    c_own = jnp.concatenate([pick(cotangent, h), after_these(c_moved, o_own)], axis=0)
    q_parts = lax.optimization_barrier(q_parts + (u_a, u_b, c_own))[:4]
    c_two = jnp.concatenate([c_own, to_z(c_own)], axis=0)
    c_core = to_core(c_two)
    qkv_w, normed_one, qkv, attn, attn_low, lse, gains = call(
        attend_kernel,
        (shape((D, WQ)), shape((N, D)), shape((N, 3 * HT)), shape((N, HT), F32), shape((N, HT)), shape((N, 4), F32), shape((8, D), F32)),
        [SMEM] + [VMEM] * 6 + [ANY] * 4, (ids, x_two, x_core, v_two, cs, sn, bias, *q_parts),
        [pltpu.SemaphoreType.DMA((32,))])
    a_two = jnp.concatenate([attn_low, to_z(after_these(attn_low, c_two))], axis=0)
    o_two = jnp.concatenate([o_own, o_first], axis=0)
    o_core = to_core(after_these(o_two, attn_low))
    u_parts = (u_a, to_y(u_a), u_b, to_x(u_b))
    a_core = to_core(a_two)
    attn_full, after, normed_two, out_w = call(
        after_kernel, (shape((N, D)), shape((M, D), F32), shape((N, D)), shape((HT, D))),
        [SMEM] + [VMEM] * 5 + [ANY] * 2, (ids, x_two, x_core, a_two, a_core, gains, o_two, o_core),
        [pltpu.VMEM((D, D), BF16), pltpu.SemaphoreType.DMA((32,))])
    block = (2, 6 * ROWS, 2 * FT)
    out_keep, out_send, r_keep, r_send, gain_two_g, a_keep, a_send, b_keep, b_send = call(
        feed_kernel, (shape((HALF, D)),) * 4 + (shape((1, D), F32),) + (shape(block),) * 4,
        [SMEM] + [VMEM] * 4 + [ANY] * 4, (ids, normed_two, gains, c_two, c_core, *u_parts),
        [pltpu.VMEM((D, 2 * FT), BF16), pltpu.VMEM((8 * FROWS, D), BF16), pltpu.VMEM((8 * FROWS, D), F32), pltpu.VMEM((8, 2 * ROWS, 2 * FT), BF16),
         pltpu.VMEM((N, FT), BF16), pltpu.VMEM((N, 2 * FT), BF16), pltpu.VMEM((HT, 2 * FT), F32),
         pltpu.SemaphoreType.DMA((32,)), pltpu.SemaphoreType.DMA((8,))], mib=48)

    r_core = to_core(r_send)
    u_sums = (a_keep, to_y(a_send), b_keep, to_x(b_send))

    def middle(r_keep, r_core, after, gains, c_two, out_keep, o_core):
        kept, sent = call(fold_kernel, (shape((M, D), F32), shape((M, D))), [VMEM] * 2, (r_keep, r_core))
        grad_after, branch = call(branch_kernel, (shape((M, D), F32), shape((M, D))), [VMEM] * 5, (kept, to_z(sent), after, gains, c_two))
        b_two = jnp.concatenate([branch, to_z(branch)], axis=0)
        o_kept, o_sent = call(fold_kernel, (shape((M, D), F32), shape((M, D))), [VMEM] * 2, (out_keep, after_these(o_core, branch)))
        return grad_after, b_two, to_core(b_two), o_kept, o_sent

    grad_after, b_two, b_core, o_kept, o_sent = fenced(
        middle, r_keep, after_these(r_core, a_send), after, gains, c_two, out_keep, to_core(out_send))

    def second_sum(a_own, a_send, b_own, b_send):
        return a_own, a_send, call(sum_second_kernel, shape(b_own.shape), [VMEM] * 2, (b_own, to_y(b_send)))

    def first_sum(sums):
        return call(sum_first_kernel, (shape(sums[0].shape[1:]),) * 4, [VMEM] * 4, sums)

    u_sums = first_sum(lax.optimization_barrier(u_sums + (b_core,))[:4])
    b_core = after_these(b_core, u_sums[3])
    def attend_back(o_sent, *inputs):
        o_moved = to_z(o_sent)
        block = (2, 4 * ROWS + 40, WQ)
        return (o_moved,) + tuple(call(
            attend_back_kernel, (shape((HALF, D)), shape((HALF, D + HT)), shape((HALF, HT))) + (shape(block),) * 4,
            [SMEM] + [VMEM] * 14, (ids,) + inputs,
            [pltpu.VMEM((N, HT), BF16), pltpu.VMEM((N, HT), F32), pltpu.VMEM((N, HT), F32), pltpu.VMEM((N, 3 * HT), BF16),
             pltpu.VMEM((HT, D), F32), pltpu.VMEM((8, D), F32), pltpu.VMEM((HT, WQ), F32)], mib=60))

    o_moved, r_keep, r_send, dv_keep, a_keep, a_send, b_keep, b_send = fenced(
        attend_back, o_sent, b_two, b_core, out_w, qkv, attn, lse, bias, cs, sn, qkv_w, normed_one, gains, gain_two_g, attn_full)
    u_sums = second_sum(*u_sums)
    r_send = after_these(r_send, u_sums[2])
    y_own, y_send = call(result_kernel, (shape((L, D)), shape((L, D))), [VMEM] * 3, (o_kept, o_moved, after))
    layer_out = call(result_home_kernel, shape((2, L, D)), [SMEM] + [VMEM] * 2, (ids, y_own, to_h(y_send)))
    r_core = to_core(r_send)
    kept, sent = call(fold_both_kernel, (shape((M, D), F32), shape((M, D + 2 * HT))), [VMEM] * 3, (r_keep, dv_keep, r_core))
    a_send, b_send, _ = lax.optimization_barrier((a_send, b_send, sent))
    q_sums = (a_keep, to_y(a_send), b_keep, to_x(b_send))
    own, sent = call(input_kernel, (shape((L, 2 * D)), shape((L, 2 * D))), [SMEM] + [VMEM] * 7,
                     (ids, kept, to_z(sent), x_two, gains, grad_after, dv_keep, r_core), [pltpu.VMEM((M, 2 * D), BF16)])
    home = to_h(sent)
    input_grad, v1_out = call(home_kernel, (shape((2, L, D), F32),) * 2, [SMEM] + [VMEM] * 3, (ids, own, home, v1_acc))

    def finish(kernel, sums, rest, first=(), last=()):
        a_own, a_send, b_send = sums
        dims = a_own.shape
        kept, sent, rows = call(kernel, (shape((2, ROWS, dims[1])), shape((2, ROWS, dims[1])), shape(rest, F32)), [SMEM] + [VMEM] * 3,
                                (ids, a_own, to_x(a_send), after_these(to_h(b_send), *first)), [pltpu.VMEM(dims, F32)])
        first = to_z(sent)
        return (ids, kept, first, to_core(pair_of(kept, after_these(first, *last)))), rows

    a_own, a_send, b_own, b_send = first_sum(q_sums)
    q_sums = second_sum(a_own, a_send, after_these(b_own, home), b_send)
    parts, down_g = finish(sum_hidden_kernel, u_sums, (FROWS, D))
    gate_g, up_g = call(join_hidden_kernel, (shape((ROWS, 4 * FT), F32),) * 2, [SMEM] + [VMEM] * 3, parts,
                        [pltpu.VMEM((4, ROWS, 2 * FT), F32)])
    parts, out_g = finish(sum_qkv_kernel, q_sums, (ROWS, D), (gate_g,), (input_grad,))
    query_g, key_g, value_g, gain_one_g, gain_two_g = call(
        join_qkv_kernel, (shape((ROWS, D), F32),) * 3 + (shape((1, ROWS), F32),) * 2, [SMEM] + [VMEM] * 3, parts)
    return (layer_out, input_grad, v1_out, gain_one_g.reshape(ROWS), query_g, key_g, value_g, out_g, gain_two_g.reshape(ROWS), gate_g, up_g, down_g)


def local(plan, layer_in, *rest):
    kept = plan.G == FAST_G and plan.T == FAST_T and layer_in.shape == (2, FAST_L, D) and rest[12].shape == (FROWS, D)
    return (fast if kept else general)(plan, layer_in, *rest)


def solution(mesh):
    plan = Plan(mesh.shape["gx"], mesh.shape["gy"])
    tokens, rows, vector = P(None, ALL, None), P(ALL, None), P(ALL)
    return jax.shard_map(
        functools.partial(local, plan),
        mesh=mesh,
        in_specs=(tokens, tokens, tokens, tokens, P(), vector, rows, rows, rows, rows, vector, rows, rows, rows),
        out_specs=(tokens, tokens, tokens, vector, rows, rows, rows, rows, vector, rows, rows, rows),
        check_vma=False,
    )
```
